32 devices in a mesh: fsdp: 2 (over x), ctx: 4 (over z), tp: 4 (over y, core).
Axes of the slice: x: 2, y: 2, z: 4, core: 2. Of those that a mesh axis runs over, the one named last changes fastest.
Arguments:
- tokens: bfloat16 [8, 1024, 1536], P('fsdp', 'ctx'), may hold values from -6 to 6
- segment_ids: int32 [8, 1024], P('fsdp', 'ctx'), may hold values from 0 to 1023, as said below
- in_gain: bfloat16 [1536], replicated, may hold values from 0.3984375 to 1.59375
- w_zx: bfloat16 [1536, 2, 3072], P(('fsdp', 'ctx'), None, 'tp'), may hold values from -0.15625 to 0.15625
- w_bc: bfloat16 [1536, 256], P(('fsdp', 'ctx')), may hold values from -0.15625 to 0.15625
- w_dt: bfloat16 [1536, 48], P(('fsdp', 'ctx'), 'tp'), may hold values from -0.15625 to 0.15625
- dt_bias: float32 [48], P('tp'), may hold values from -6 to -3
- a_log: float32 [48], P('tp'), may hold values from -0.5 to 2.5
- skip_gain: float32 [48], P('tp'), may hold values from 0.5 to 2
- conv_x: bfloat16 [4, 3072], P(None, 'tp'), may hold values from -3 to 3
- conv_x_bias: bfloat16 [3072], P('tp'), may hold values from -0.5 to 0.5
- conv_bc: bfloat16 [4, 256], replicated, may hold values from -3 to 3
- conv_bc_bias: bfloat16 [256], replicated, may hold values from -0.5 to 0.5
- gate_gain: bfloat16 [3072], P('tp'), may hold values from 0.3984375 to 1.59375
- w_out: bfloat16 [3072, 1536], P('tp', ('fsdp', 'ctx')), may hold values from -0.109375 to 0.109375
- cotangent: bfloat16 [8, 1024, 1536], P('fsdp', 'ctx'), may hold values from -6 to 6
Outputs:
- mixed: bfloat16 [8, 1024, 1536], P('fsdp', 'ctx', 'tp')
- grad_tokens: float32 [8, 1024, 1536], P('fsdp', 'ctx', 'tp')
- grad_in_gain: float32 [1536], P('tp')
- grad_w_zx: float32 [1536, 2, 3072], P(('fsdp', 'ctx'), None, 'tp')
- grad_w_bc: float32 [1536, 256], P(('fsdp', 'ctx'))
- grad_w_dt: float32 [1536, 48], P(('fsdp', 'ctx'), 'tp')
- grad_dt_bias: float32 [48], P('tp')
- grad_a_log: float32 [48], P('tp')
- grad_skip_gain: float32 [48], P('tp')
- grad_conv_x: float32 [4, 3072], P(None, 'tp')
- grad_conv_x_bias: float32 [3072], P('tp')
- grad_conv_bc: float32 [4, 256], replicated
- grad_conv_bc_bias: float32 [256], replicated
- grad_gate_gain: float32 [3072], P('tp')
- grad_w_out: float32 [3072, 1536], P('tp', ('fsdp', 'ctx'))
The draws below stay inside these ranges and needn't reach their ends.
Inputs may be any that keep to these rules, and one draw needn't show every extreme that they name: segment_ids[s, t] is the position within sequence s at which the document holding token t begins: it never exceeds t, never falls along t, equals 0 at t = 0, and equals t exactly where a document begins. In each aligned group of 4 sequences, one sequence holds a document that begins within its first 256 positions and ends within its last 256.
All inputs are finite; a program needn't handle non-finite values.
Results may differ from the reference program's by a relative error of at most 0.01.
Values may be sent and summed in bfloat16 or wider, within the bound.
No kernel may reach another device: no remote copies, remote signals or barrier semaphores. Data moves between devices by JAX's collectives and lax.ppermute only.
A program may use at most 192 MiB of HBM per device.

```python
import math
import jax
import jax.numpy as jnp
from jax import lax

D = 1536
HEADS = 48
HEADDIM = 64
STATE = 128
CONV = 4
LENGTH = 1024
SEQS = 4
INNER = 3072
CTX_TOK = 256
NSEQ = 8


def draw_segment_ids(key, part):
    key = jax.random.fold_in(key, 17)
    shortest = max(LENGTH * 60 // 1024, 2)
    longest = max(LENGTH * 800 // 1024, shortest + 1)
    doc_count = LENGTH // shortest + 2
    key_spans, key_first, key_last, key_pick = jax.random.split(key, 4)
    doc_spans = jax.random.randint(key_spans, (NSEQ, doc_count), shortest, longest + 1)
    starts = jnp.cumsum(doc_spans, axis=1) - doc_spans
    first_cut = jax.random.randint(key_first, (NSEQ, 1), 1, CTX_TOK)
    last_cut = jax.random.randint(key_last, (NSEQ, 1), LENGTH - CTX_TOK + 1, LENGTH + 1)
    filler = jnp.full((NSEQ, doc_count - 3), LENGTH + 1, jnp.int32)
    spanning = jnp.concatenate([jnp.zeros((NSEQ, 1), jnp.int32), first_cut.astype(jnp.int32), last_cut.astype(jnp.int32), filler], axis=1)
    groups = NSEQ // SEQS
    chosen = jax.random.randint(key_pick, (groups, 1), 0, SEQS)
    member = (jnp.arange(SEQS, dtype=jnp.int32)[None, :] == chosen).reshape(NSEQ)
    starts = jnp.where(member[:, None], spanning, starts.astype(jnp.int32))
    positions = jnp.arange(LENGTH, dtype=jnp.int32)
    has_begun = starts[:, :, None] <= positions[None, None, :]
    return jnp.max(jnp.where(has_begun, starts[:, :, None], 0), axis=1).astype(jnp.int32)


def levels(rng, extent, cuts, smallest, high):
    def one(dim, blocks):
        draws = jax.random.uniform(jax.random.fold_in(jax.random.fold_in(rng, 6), dim), (blocks,), jnp.float32, smallest / len(cuts), high / len(cuts))
        return jnp.repeat(jnp.exp(draws), extent[dim] // blocks).reshape((-1,) + (1,) * (len(extent) - dim - 1))

    gain = one(*cuts[0])
    for cut in cuts[1:]:
        gain = gain * one(*cut)
    return gain


def noise(rng, shape, scale, bound, cuts=(), held_as=jnp.bfloat16):
    result = jax.random.normal(rng, shape, jnp.float32) * scale
    if len(cuts) > 0:
        result = levels(rng, shape, cuts, -0.22, 0.18) * result
    return jnp.clip(result, min=-bound, max=bound).astype(held_as)


def setup_inputs(seed: int = 0) -> dict:
    arg_keys = jax.random.split(jax.random.key(seed), 17)
    return {
        "tokens": noise(arg_keys[0], (NSEQ, LENGTH, D), 1.0, 6.0, ((0, 2), (1, 4))),
        "segment_ids": draw_segment_ids(jax.random.fold_in(arg_keys[16], 71), 0),
        "in_gain": jnp.clip(1.0 + 0.12 * jax.random.normal(arg_keys[2], (D,), jnp.float32), 0.3984375, 1.59375).astype(jnp.bfloat16),
        "w_zx": noise(arg_keys[3], (D, 2, INNER), D ** -0.5, 0.15625, ((0, 8), (2, 4))),
        "w_bc": noise(arg_keys[4], (D, 2 * STATE), D ** -0.5, 0.15625, ((0, 8),)),
        "w_dt": noise(arg_keys[5], (D, HEADS), D ** -0.5, 0.15625, ((0, 8), (1, 4))),
        "dt_bias": jnp.clip(-6.0 + 3.0 * jax.random.uniform(arg_keys[6], (HEADS,), jnp.float32) ** levels(arg_keys[6], (HEADS,), ((0, 4),), -0.2, 0.2), -6.0, -3.0),
        "a_log": jnp.clip(-0.5 + 3.0 * jax.random.uniform(arg_keys[7], (HEADS,), jnp.float32) ** levels(arg_keys[7], (HEADS,), ((0, 4),), -0.2, 0.2), -0.5, 2.5),
        "skip_gain": jnp.clip(0.5 + 1.5 * jax.random.uniform(arg_keys[8], (HEADS,), jnp.float32) ** levels(arg_keys[8], (HEADS,), ((0, 4),), -0.2, 0.2), 0.5, 2.0),
        "conv_x": noise(arg_keys[9], (CONV, INNER), CONV ** -0.5, 3.0, ((1, 4),)),
        "conv_x_bias": jnp.clip(jax.random.uniform(arg_keys[10], (INNER,), jnp.float32, -0.5, 0.5) * levels(arg_keys[10], (INNER,), ((0, 4),), -0.4, 0.0), -0.5, 0.5).astype(jnp.bfloat16),
        "conv_bc": noise(arg_keys[11], (CONV, 2 * STATE), CONV ** -0.5, 3.0),
        "conv_bc_bias": jnp.clip(jax.random.uniform(arg_keys[12], (2 * STATE,), jnp.float32, -0.5, 0.5), -0.5, 0.5).astype(jnp.bfloat16),
        "gate_gain": jnp.clip(1.0 + 0.12 * jax.random.normal(arg_keys[13], (INNER,), jnp.float32), 0.3984375, 1.59375).astype(jnp.bfloat16),
        "w_out": noise(arg_keys[14], (INNER, D), INNER ** -0.5, 0.109375, ((0, 4), (1, 8))),
        "cotangent": noise(arg_keys[15], (NSEQ, LENGTH, D), 1.0, 6.0, ((0, 2), (1, 4))),
    }


norm_eps = 1e-05

@jax.custom_vjp
def low(v):
    return lax.optimization_barrier(v.astype(jnp.bfloat16)).astype(jnp.float32)

@jax.custom_vjp
def low_back(v):
    return v

def low_keep(v):
    return (low(v), None)

def low_pass(kept, grad):
    return (grad,)

def back_keep(v):
    return (v, None)

def back_low(kept, grad):
    return (low(grad),)
low.defvjp(low_keep, low_pass)
low_back.defvjp(back_keep, back_low)

def conv_apply(u_val, rim_val, weight, bias_val, seg_ids, positions):
    extended = jnp.concatenate([rim_val, u_val], axis=1)
    tap_count = weight.shape[0]
    length = u_val.shape[1]
    conv_sum = jnp.zeros_like(u_val) + bias_val[None, None, :]
    for tap_index in range(tap_count):
        lag_size = tap_count - 1 - tap_index
        window = extended[:, tap_index:tap_index + length, :]
        usable = (seg_ids <= positions[None, :] - lag_size).astype(u_val.dtype)
        conv_sum = conv_sum + weight[tap_index][None, None, :] * window * usable[:, :, None]
    return conv_sum

def ssd_parts(x_heads, b_mat, c_mat, dt_val, log_decay, seg_ids, positions):
    highest = lax.Precision.HIGHEST
    cum_decay = jnp.cumsum(log_decay, axis=1)
    lower_tri = positions[:, None] >= positions[None, :]
    same_doc = (seg_ids[:, :, None] == seg_ids[:, None, :]) & lower_tri[None, :, :]
    same_float = same_doc.astype(log_decay.dtype)[..., None]
    log_gap = cum_decay[:, :, None, :] - cum_decay[:, None, :, :]
    decay_mat = jnp.exp(jnp.where(same_doc[..., None], log_gap, 0.0)) * same_float
    scores = jnp.einsum('btn,bsn->bts', c_mat, b_mat, precision=highest)
    weights = decay_mat * scores[..., None] * dt_val[:, None, :, :]
    y_local = jnp.einsum('btsh,bshp->bthp', weights, x_heads, precision=highest)
    block_start = positions[0]
    carried = (seg_ids < block_start).astype(log_decay.dtype)
    into_scale = jnp.exp(cum_decay) * carried[..., None]
    last_doc = (seg_ids == seg_ids[:, -1:]).astype(log_decay.dtype)
    tail_scale = jnp.exp(cum_decay[:, -1:, :] - cum_decay) * last_doc[..., None]
    state_local = jnp.einsum('bsh,bshp,bsn->bhpn', tail_scale * dt_val, x_heads, b_mat, precision=highest)
    decay_total = jnp.exp(cum_decay[:, -1, :]) * carried[:, -1:]
    return (y_local, into_scale, decay_total, state_local)

def layer(x_val, seg_ids, in_gain, w_zx, w_bc, w_dt, dt_bias, a_log, skip_gain, conv_x, conv_x_bias, conv_bc, conv_bc_bias, gate_gain, w_out):
    highest = lax.Precision.HIGHEST
    batch_size = x_val.shape[0]
    positions = jnp.arange(LENGTH, dtype=jnp.int32)
    inv_rms = lax.rsqrt(lax.optimization_barrier(jnp.mean(x_val * x_val, axis=-1, keepdims=True)) + norm_eps)
    normed = low(x_val * inv_rms * in_gain)
    zx_both = low_back(jnp.einsum('bld,dkf->blkf', normed, w_zx, precision=highest))
    z_part = zx_both[:, :, 0]
    x_part = zx_both[:, :, 1]
    bc_part = low_back(jnp.dot(normed, w_bc, precision=highest))
    dt_raw = low_back(jnp.dot(normed, w_dt, precision=highest))
    u_in = jnp.concatenate([x_part, bc_part], axis=-1)
    rim_rows = jnp.zeros((batch_size, CONV - 1, u_in.shape[2]), x_val.dtype)
    conv_weight = jnp.concatenate([conv_x, conv_bc], axis=1)
    conv_bias = jnp.concatenate([conv_x_bias, conv_bc_bias])
    activated = jax.nn.silu(conv_apply(u_in, rim_rows, conv_weight, conv_bias, seg_ids, positions))
    x_heads = activated[..., :INNER].reshape(batch_size, LENGTH, HEADS, HEADDIM)
    b_mat = activated[..., INNER:INNER + STATE]
    c_mat = activated[..., INNER + STATE:]
    dt_val = jax.nn.softplus(dt_raw + dt_bias)
    log_decay = -dt_val * jnp.exp(a_log)
    block_len = math.gcd(LENGTH, 256)
    blocks = LENGTH // block_len

    def split_blocks(array_in):
        shaped = array_in.reshape((batch_size, blocks, block_len) + array_in.shape[2:])
        return jnp.moveaxis(shaped, 1, 0)
    block_items = tuple((split_blocks(array_in) for array_in in (x_heads, b_mat, c_mat, dt_val, log_decay, seg_ids)))
    block_items = block_items + (positions.reshape(blocks, block_len),)

    def block_step(state_val, pieces):
        heads_in, b_in, c_in, dt_in, decay_in, seg_in, pos_in = pieces
        y_local, into_scale, decay_total, state_local = ssd_parts(heads_in, b_in, c_in, dt_in, decay_in, seg_in, pos_in)
        carried_read = jnp.einsum('btn,bhpn->bthp', c_in, state_val, precision=highest)
        y_block = y_local + into_scale[..., None] * carried_read
        new_state = decay_total[:, :, None, None] * state_val + state_local
        return (new_state, y_block)
    state_zero = jnp.zeros((batch_size, HEADS, HEADDIM, STATE), x_val.dtype)
    _, y_blocks = lax.scan(jax.checkpoint(block_step), state_zero, block_items)
    y_heads = jnp.moveaxis(y_blocks, 0, 1).reshape(batch_size, LENGTH, HEADS, HEADDIM)
    y_heads = y_heads + skip_gain[:, None] * x_heads
    y_flat = y_heads.reshape(batch_size, LENGTH, INNER)
    gated_val = y_flat * jax.nn.silu(z_part)
    inv_gate = lax.rsqrt(lax.optimization_barrier(jnp.mean(gated_val * gated_val, axis=-1, keepdims=True)) + norm_eps)
    hidden = low(gated_val * inv_gate * gate_gain)
    return x_val + jnp.dot(hidden, w_out, precision=highest)

def reference(tokens, segment_ids, in_gain, w_zx, w_bc, w_dt, dt_bias, a_log, skip_gain, conv_x, conv_x_bias, conv_bc, conv_bc_bias, gate_gain, w_out, cotangent):
    params = tuple((param.astype(jnp.float32) for param in (in_gain, w_zx, w_bc, w_dt, dt_bias, a_log, skip_gain, conv_x, conv_x_bias, conv_bc, conv_bc_bias, gate_gain, w_out)))
    group_size = math.gcd(NSEQ, 4)

    def reshape_group(array_in):
        return array_in.reshape((NSEQ // group_size, group_size) + array_in.shape[1:])

    def group_step(totals, pieces):
        tok_in, seg_in, cot_in = pieces

        def forward(x_val, *weights):
            return layer(x_val, seg_in, *weights)
        out_val, pull_back = jax.vjp(forward, tok_in.astype(jnp.float32), *params)
        grad_list = pull_back(cot_in.astype(jnp.float32))
        totals = tuple((total_val + grad_item for total_val, grad_item in zip(totals, grad_list[1:])))
        return (totals, (out_val.astype(jnp.bfloat16), grad_list[0]))
    zero_grads = tuple((jnp.zeros_like(param) for param in params))
    totals, outputs = lax.scan(group_step, zero_grads, (reshape_group(tokens), reshape_group(segment_ids), reshape_group(cotangent)))
    mixed = outputs[0].reshape(NSEQ, LENGTH, D)
    grad_tokens = outputs[1].reshape(NSEQ, LENGTH, D)
    return (mixed, grad_tokens, totals[0], totals[1], totals[2], totals[3], totals[4], totals[5], totals[6], totals[7], totals[8], totals[9], totals[10], totals[11], totals[12])
```

```python
import functools

import jax
import jax.numpy as jnp
from jax import lax
from jax.experimental import pallas as pl
from jax.experimental.pallas import tpu as pltpu
from jax.sharding import PartitionSpec as P

D = 1536
HEADDIM = 64
STATE = 128
CONV = 4
INNER = 3072
NORM_EPS = 1e-05
LANES = 128
HALO = 16

bf16 = jnp.bfloat16
f32 = jnp.float32
NN = (((1,), (0,)), ((), ()))
NT = (((1,), (1,)), ((), ()))
TN = (((0,), (0,)), ((), ()))


def rotate(v, axis, steps):
    n = lax.axis_size(axis)
    return lax.ppermute(v, axis, [(i, (i + steps) % n) for i in range(n)])


def shift(v, axis, steps):
    n = lax.axis_size(axis)
    return lax.ppermute(v, axis, [(i, i + steps) for i in range(n) if 0 <= i + steps < n])


def flip(v, axis, mask):
    n = lax.axis_size(axis)
    return lax.ppermute(v, axis, [(i, i ^ mask) for i in range(n)])


def cube_sum(v, axis):
    mask = 1
    while mask < lax.axis_size(axis):
        v = v + flip(v, axis, mask)
        mask *= 2
    return v


def ring_gather(v):
    nc, nf = lax.axis_size("ctx"), lax.axis_size("fsdp")
    c, f = lax.axis_index("ctx"), lax.axis_index("fsdp")
    rows = v.shape[0]
    whole = jnp.zeros((rows * nc * nf, v.shape[1]), v.dtype)
    current = v
    for step in range(nc):
        if step:
            current = rotate(current, "ctx", 1)
        owner = lax.rem(c - step + nc, nc)
        piece = current
        for j in range(nf):
            if j:
                piece = rotate(piece, "fsdp", 1)
            place = lax.rem(f - j + nf, nf) * nc + owner
            whole = lax.dynamic_update_slice_in_dim(whole, piece, place * rows, 0)
    return whole


def ring_scatter(g):
    nc, nf = lax.axis_size("ctx"), lax.axis_size("fsdp")
    c, f = lax.axis_index("ctx"), lax.axis_index("fsdp")
    rows = g.shape[0] // (nc * nf)

    def piece(ff, cc):
        return lax.dynamic_slice_in_dim(g, (lax.rem(ff, nf) * nc + cc) * rows, rows, 0)

    total = None
    for step in range(1, nc + 1):
        cc = lax.rem(c - step + nc, nc)
        mine = piece(f, cc).astype(f32)
        for k in range(1, nf):
            mine = mine + rotate(piece(f + k, cc).astype(bf16), "fsdp", k).astype(f32)
        total = mine if total is None else total + mine
        if step < nc:
            total = rotate(total.astype(bf16), "ctx", 1).astype(f32)
    return total


def cube_scatter(v, axis):
    n, r = lax.axis_size(axis), lax.axis_index(axis)
    width = v.shape[1] // n
    held = [lax.dynamic_slice_in_dim(v, (r ^ k) * width, width, 1) for k in range(n)]
    mask = 1
    while mask < n:
        away = jnp.concatenate([held[i] for i in range(1, len(held), 2)], 1).astype(bf16)
        near = flip(away, axis, mask).astype(f32)
        kept = [held[i] for i in range(0, len(held), 2)]
        held = [k.astype(f32) + near[:, i * width : (i + 1) * width] for i, k in enumerate(kept)]
        mask *= 2
    return held[0]


def chain(parts, decay, reverse):
    n = lax.axis_size("ctx")
    entering, last = None, None
    for hop in range(1, n):
        out = parts
        if last is not None:
            out = (parts.astype(f32) + decay * last.astype(f32)).astype(bf16)
        pair = (n - hop, n - hop - 1) if reverse else (hop - 1, hop)
        last = lax.ppermute(out, "ctx", [pair])
        entering = last if entering is None else entering + last
    return entering


def dot(a, b, dims=NN):
    return lax.dot_general(a, b, dims, preferred_element_type=f32)


def split(v, terms):
    out = []
    for i in range(terms):
        t = v.astype(bf16)
        out.append(t)
        if i + 1 < terms:
            v = v - t.astype(f32)
    return out


def head_map(inner, transposed):
    shape = (inner, LANES) if transposed else (LANES, inner)
    ch = lax.broadcasted_iota(jnp.int32, shape, 0 if transposed else 1)
    hd = lax.broadcasted_iota(jnp.int32, shape, 1 if transposed else 0)
    return jnp.where(ch // HEADDIM == hd, 1.0, 0.0).astype(bf16)


def widen(v, inner):
    e = head_map(inner, False)
    return dot(jnp.concatenate(split(v, 2), 1), jnp.concatenate([e, e], 0))


def narrow(v, terms):
    e = head_map(v.shape[1], True)
    out = None
    for t in split(v, terms):
        s = dot(t, e)
        out = s if out is None else out + s
    return out


def tri_sum(tri, v, dims=NN):
    out = None
    for t in split(v, 3):
        s = dot(tri, t, dims)
        out = s if out is None else out + s
    return out


def triangle(q, strict=False):
    r = lax.broadcasted_iota(jnp.int32, (q, q), 0)
    c = lax.broadcasted_iota(jnp.int32, (q, q), 1)
    return jnp.where(c < r if strict else c <= r, 1.0, 0.0).astype(bf16)


def halves(v):
    lane = lax.broadcasted_iota(jnp.int32, v.shape, 1)
    zero = jnp.zeros_like(v)
    return jnp.where(lane < HEADDIM, v, zero), jnp.where(lane >= HEADDIM, v, zero)


def sigmoid(v):
    return 1.0 / (1.0 + jnp.exp(-v))


def project_kernel(nx, start, w, taps, bias, head_par, *refs, inner, conv):
    u_ref, pre_ref, act_ref, xdt_ref, dtl_ref, state_ref, dec_ref = refs[-7:]
    q = start.shape[0]
    u = dot(nx[...], w[...])
    u_ref[...] = u[:, :conv].astype(bf16)
    at = lax.broadcasted_iota(jnp.int32, (q, 1), 0)
    begin = start[...]
    since = at - begin
    for lo in range(0, conv, LANES):
        cols = slice(lo, lo + LANES)
        ut = u[:, cols]
        acc = bias[0:1, cols] + taps[CONV - 1 : CONV, cols] * ut[HALO:]
        for j in range(1, CONV):
            window = ut[HALO - j : HALO - j + q]
            acc = acc + taps[CONV - 1 - j : CONV - j, cols] * jnp.where(since >= j, window, 0.0)
        pre_ref[:, cols] = acc.astype(bf16)
        act_ref[:, cols] = (acc * sigmoid(acc)).astype(bf16)
    v = u[HALO:, conv:] + head_par[0:1, :]
    dt = jnp.maximum(v, 0.0) + jnp.log1p(jnp.exp(-jnp.abs(v)))
    cum = tri_sum(triangle(q), -dt * jnp.exp(head_par[1:2, :]))
    dtl_ref[:, :LANES] = dt
    dtl_ref[:, LANES:] = cum
    end = cum[q - 1 : q, :]
    begin_last = begin[q - 1 : q, :]
    tail = jnp.where(begin == begin_last, jnp.exp(end - cum), 0.0)
    xh = act_ref[:, :inner].astype(f32)
    xdt = (xh * widen(dt, inner)).astype(bf16)
    xdt_ref[...] = xdt
    weighted = (xdt.astype(f32) * widen(tail, inner)).astype(bf16)
    b = act_ref[:, inner : inner + STATE]
    state_ref[...] = dot(b, weighted, TN).astype(bf16)
    total = jnp.where(begin_last < 0, jnp.exp(end), 0.0)
    dec_ref[...] = widen(jnp.broadcast_to(total, (8, LANES)), inner)[0:1]


def score_mask(begin_col, q):
    r = lax.broadcasted_iota(jnp.int32, (q, q), 0)
    c = lax.broadcasted_iota(jnp.int32, (q, q), 1)
    return (c <= r) & (c >= begin_col)


def score_mask_t(begin_row, q):
    r = lax.broadcasted_iota(jnp.int32, (q, q), 0)
    c = lax.broadcasted_iota(jnp.int32, (q, q), 1)
    return (r <= c) & (r >= begin_row)


def local_kernel(act, xdt, dtl, start, y_ref, *, inner):
    q = start.shape[0]
    b = act[:, inner : inner + STATE]
    c = act[:, inner + STATE : inner + 2 * STATE]
    scores = jnp.where(score_mask(start[...], q), dot(c, b, NT), 0.0)
    cum = dtl[:, LANES:]
    cum_t = cum.T
    for pair in range(inner // LANES):
        cols = slice(pair * LANES, (pair + 1) * LANES)
        weights = []
        for h in (2 * pair, 2 * pair + 1):
            gap = jnp.minimum(cum[:, h : h + 1] - cum_t[h : h + 1, :], 0.0)
            weights.append((jnp.exp(gap) * scores).astype(bf16))
        even, odd = halves(xdt[:, cols])
        y_ref[:, cols] = dot(weights[0], even) + dot(weights[1], odd)


def gate_sums_kernel(y_in, act, dtl, start, state, z, dh, rows, y_ref, sums_ref, *, inner):
    q = start.shape[0]
    c = act[:, inner + STATE : inner + 2 * STATE]
    into = widen(jnp.where(start[...] < 0, jnp.exp(dtl[:, LANES:]), 0.0), inner)
    y = y_in[...] + into * dot(c, state[...])
    y_ref[...] = y
    zz = z[...]
    gated = (y + rows[0:1, :] * act[:, :inner].astype(f32)) * (zz * sigmoid(zz))
    e = dh[...] * rows[1:2, :]
    ones = jnp.ones((8, inner), bf16)
    sq = dot(ones, (gated * gated).astype(bf16), NT)
    eg = dot(ones, (e * gated).astype(bf16), NT)
    row = lax.broadcasted_iota(jnp.int32, (8, q), 0)
    sums_ref[...] = jnp.where(row == 0, sq, eg)


def gate_kernel(y_in, act, dtl, start, z, dh, sums, rows, *refs, inner):
    hidden_ref, dy_ref, dz_ref, dstate_ref, grads_ref = refs[-5:]
    xh = act[:, :inner].astype(f32)
    y = y_in[...] + rows[0:1, :] * xh
    zz = z[...]
    sig = sigmoid(zz)
    silu = zz * sig
    gated = y * silu
    gain = rows[1:2, :]
    d_hidden = dh[...]
    sums_t = sums[...].T
    inv = lax.rsqrt(sums_t[:, 0:1] / INNER + NORM_EPS)
    back = sums_t[:, 1:2] * (inv * inv * inv) / INNER
    scaled = gated * inv
    hidden_ref[...] = (scaled * gain).astype(bf16)
    dg = inv * (d_hidden * gain) - gated * back
    dy = (dg * silu).astype(bf16)
    dy_ref[...] = dy
    dz_ref[...] = (dg * y * sig * (1.0 + zz * (1.0 - sig))).astype(bf16)
    gate_row = jnp.sum(d_hidden * scaled, axis=0, keepdims=True)
    dy_wide = dy.astype(f32)
    skip_row = jnp.sum(dy_wide * xh, axis=0, keepdims=True)
    row = lax.broadcasted_iota(jnp.int32, (8, inner), 0)
    grads_ref[...] = jnp.where(row == 0, gate_row, jnp.where(row == 1, skip_row, 0.0))
    into = widen(jnp.where(start[...] < 0, jnp.exp(dtl[:, LANES:]), 0.0), inner)
    c = act[:, inner + STATE : inner + 2 * STATE]
    dstate_ref[...] = dot(c, (into * dy_wide).astype(bf16), TN).astype(bf16)


def local_back_kernel(act, xdt, dtl, start, start_row, dy, state, dx_ref, dbc_ref, *, inner):
    q = start.shape[0]
    b = act[:, inner : inner + STATE]
    c = act[:, inner + STATE : inner + 2 * STATE]
    mask = score_mask_t(start_row[...], q)
    scores = jnp.where(mask, dot(b, c, NT), 0.0)
    cum = dtl[:, LANES:]
    cum_t = cum.T
    total = jnp.zeros((q, q), f32)
    for pair in range(inner // LANES):
        cols = slice(pair * LANES, (pair + 1) * LANES)
        dy_pair = dy[:, cols]
        x_even, x_odd = halves(xdt[:, cols])
        dy_even, dy_odd = halves(dy_pair)
        out = None
        for h, x_one, dy_one in ((2 * pair, x_even, dy_even), (2 * pair + 1, x_odd, dy_odd)):
            decay = jnp.exp(jnp.minimum(cum_t[h : h + 1, :] - cum[:, h : h + 1], 0.0))
            total = total + dot(x_one, dy_pair, NT) * decay
            term = dot((decay * scores).astype(bf16), dy_one)
            out = term if out is None else out + term
        dx_ref[:, cols] = out
    d_scores = jnp.where(mask, total, 0.0).astype(bf16)
    into = widen(jnp.where(start[...] < 0, jnp.exp(cum), 0.0), inner)
    weighted = (into * dy[...].astype(f32)).astype(bf16)
    dbc_ref[:, :STATE] = dot(d_scores, c)
    dbc_ref[:, STATE:] = dot(d_scores, b, TN) + dot(weighted, state[...], NT)


def conv_back_kernel(
    act, xdt, dtl, start, dy, y_in, dx, dbc, state, later, pre, u, dec, taps, rows, head_par, *refs, inner, conv
):
    du_ref, rim_ref, tap_ref, head_ref, dact = refs[-5:]
    q = start.shape[0]
    begin = start[...]
    b = act[:, inner : inner + STATE]
    dt, cum = dtl[:, :LANES], dtl[:, LANES:]
    end = cum[q - 1 : q, :]
    begin_last = begin[q - 1 : q, :]
    tail = widen(jnp.where(begin == begin_last, jnp.exp(end - cum), 0.0), inner)
    x_dt = xdt[...].astype(f32)
    d_y = dy[...].astype(f32)
    g = later[...]
    dx_tail = tail * dot(b, g)
    dact[:, inner : inner + STATE] = dbc[:, :STATE] + dot((x_dt * tail).astype(bf16), g, NT)
    dact[:, inner + STATE :] = dbc[:, STATE:]
    dx_local = dx[...]
    dx_all = dx_local + dx_tail
    dact[:, :inner] = dx_all * widen(dt, inner) + rows[0:1, :] * d_y
    flux_near = narrow(d_y * y_in[...] - x_dt * dx_local, 3)
    flux_tail = narrow(x_dt * dx_tail, 2)
    d_dt = narrow(dx_all * act[:, :inner].astype(f32), 2)
    through = jnp.sum(dec[...] * (g.astype(f32) * state[...].astype(f32)), axis=0, keepdims=True)
    through = narrow(jnp.broadcast_to(through, (8, inner)), 2)[0:1]
    d_log = tri_sum(triangle(q), flux_near, TN) + tri_sum(triangle(q, True), flux_tail) + through
    rate = jnp.exp(head_par[1:2, :])
    d_raw = (d_dt - rate * d_log) * (1.0 - jnp.exp(-dt))
    du_ref[:, conv:] = d_raw.astype(bf16)
    bias_row = jnp.sum(d_raw, axis=0, keepdims=True)
    log_row = -jnp.sum(d_log * dt * rate, axis=0, keepdims=True)
    row = lax.broadcasted_iota(jnp.int32, (8, LANES), 0)
    head_ref[...] = jnp.where(row == 0, bias_row, jnp.where(row == 1, log_row, 0.0))
    since = lax.broadcasted_iota(jnp.int32, (q, 1), 0) - begin
    for lo in range(0, conv, LANES):
        cols = slice(lo, lo + LANES)
        p = pre[:, cols].astype(f32)
        sig = sigmoid(p)
        dp = dact[:, cols] * (sig * (1.0 + p * (1.0 - sig)))
        ut = u[:, cols].astype(f32)
        zeros = jnp.zeros((HALO, LANES), f32)
        total = jnp.concatenate([zeros, taps[CONV - 1 : CONV, cols] * dp], 0)
        tap_rows = [jnp.sum(dp * ut[HALO:], axis=0, keepdims=True)]
        for j in range(1, CONV):
            masked = jnp.where(since >= j, dp, 0.0)
            tap_rows.append(jnp.sum(masked * ut[HALO - j : HALO - j + q], axis=0, keepdims=True))
            moved = jnp.concatenate([zeros, taps[CONV - 1 - j : CONV - j, cols] * masked, zeros], 0)
            total = total + moved[j : j + q + HALO]
        du_ref[:, cols] = total[HALO:].astype(bf16)
        rim_ref[:, cols] = total[:HALO].astype(bf16)
        out = jnp.sum(dp, axis=0, keepdims=True)
        for j in range(CONV):
            out = jnp.where(row == CONV - 1 - j, tap_rows[j], jnp.where(row == CONV, out, 0.0) if j == 0 else out)
        tap_ref[:, cols] = out


def call(kernel, first, count, ins, outs, shared=(), scratch=(), flops=0, moved=0, into=None):
    def spec(shape, base):
        block = (None,) + tuple(shape[1:])
        rest = (0,) * (len(shape) - 1)
        return pl.BlockSpec(block, lambda s: (s + base,) + rest)

    in_specs = [spec(a.shape, o) for a, o in ins]
    in_specs += [pl.BlockSpec(a.shape, lambda s, n=a.ndim: (0,) * n) for a in shared]
    operands = [a for a, _ in ins] + list(shared)
    aliases = {}
    if into is not None:
        for i, buf in enumerate(into):
            if buf is not None:
                aliases[len(operands)] = i
                operands.append(buf)
                in_specs.append(pl.BlockSpec(memory_space=pl.ANY))
    return pl.pallas_call(
        kernel,
        grid=(count,),
        in_specs=in_specs,
        out_specs=[spec(s, first if whole else 0) for s, _, whole in outs],
        out_shape=[jax.ShapeDtypeStruct(s, d) for s, d, _ in outs],
        scratch_shapes=list(scratch),
        input_output_aliases=aliases,
        compiler_params=pltpu.CompilerParams(vmem_limit_bytes=48 * 2**20),
        cost_estimate=pl.CostEstimate(flops=flops, bytes_accessed=moved, transcendentals=0),
    )(*operands)


def drop(kernel, n_in, n_alias):
    def run(*refs):
        kernel(*refs[:n_in], *refs[n_in + n_alias :])

    return run


def per_device(
    tokens,
    segment_ids,
    in_gain,
    w_zx,
    w_bc,
    w_dt,
    dt_bias,
    a_log,
    skip_gain,
    conv_x,
    conv_x_bias,
    conv_bc,
    conv_bc_bias,
    gate_gain,
    w_out,
    cotangent,
):
    tp_count, tp_rank = lax.axis_size("tp"), lax.axis_index("tp")
    ctx_rank = lax.axis_index("ctx")
    seqs, q, width = tokens.shape
    inner = w_zx.shape[2]
    heads = w_dt.shape[1]
    conv = inner + 2 * STATE
    cols = width // tp_count
    n_tok = seqs * q
    chunks = 2 if seqs % 2 == 0 else 1
    per = seqs // chunks

    first_w = jnp.concatenate(
        [w_zx[:, 1, :], w_bc, jnp.pad(w_dt, ((0, 0), (0, LANES - heads)))], axis=1
    )
    halo = shift(tokens[:, q - 8 :, :], "ctx", 1)
    w_in = ring_gather(first_w)
    second_w = jnp.concatenate([w_zx[:, 0, :], w_out.T], axis=1)
    second_w, w_in = lax.optimization_barrier((second_w, w_in))
    w_rest = ring_gather(second_w)
    w_z, w_o = w_rest[:, :inner], w_rest[:, inner:]

    x_ext = jnp.concatenate([jnp.zeros_like(halo), halo, tokens], axis=1).astype(f32)
    inv_rms = lax.rsqrt(jnp.mean(x_ext * x_ext, axis=-1, keepdims=True) + NORM_EPS)
    nx = (x_ext * inv_rms * in_gain.astype(f32)).astype(bf16)
    inv_rms = inv_rms[:, HALO:]
    normed = nx[:, HALO:].reshape(n_tok, width)

    begin = segment_ids - ctx_rank * q
    start = begin[:, :, None]
    start_row = begin[:, None, :]
    taps = jnp.concatenate([conv_x, conv_bc], axis=1).astype(f32)
    bias = jnp.concatenate([conv_x_bias, conv_bc_bias]).astype(f32)[None]
    head_par = jnp.pad(jnp.stack([dt_bias, a_log]), ((0, 6), (0, LANES - heads)))
    rows = jnp.pad(jnp.stack([jnp.repeat(skip_gain, HEADDIM), gate_gain.astype(f32)]), ((0, 6), (0, 0)))

    shape = lambda *s: (seqs,) + s
    part = lambda *s: (per,) + s

    bulk = [None] * 5
    states, decs = [], []
    for g in range(chunks):
        have = 0 if g == 0 else 5
        o = g * per
        out = call(
            drop(functools.partial(project_kernel, inner=inner, conv=conv), 6, have),
            o,
            per,
            [(nx, o), (start, o)],
            [
                (shape(q + HALO, conv), bf16, True),
                (shape(q, conv), bf16, True),
                (shape(q, conv), bf16, True),
                (shape(q, inner), bf16, True),
                (shape(q, 2 * LANES), f32, True),
                (part(STATE, inner), bf16, False),
                (part(1, inner), f32, False),
            ],
            shared=(w_in, taps, bias, head_par),
            into=None if g == 0 else bulk,
            flops=2 * per * q * width * conv,
            moved=10 * per * q * conv,
        )
        bulk = list(out[:5])
        states.append(out[5])
        decs.append(out[6])
    u, pre, act, xdt, dtl = bulk
    entering = [chain(states[g], decs[g], False) for g in range(chunks)]

    y_local = call(
        functools.partial(local_kernel, inner=inner),
        0,
        seqs,
        [(act, 0), (xdt, 0), (dtl, 0), (start, 0)],
        [(shape(q, inner), f32, True)],
        flops=8 * seqs * q * q * inner,
        moved=8 * n_tok * inner,
    )[0]
    cot = cotangent.reshape(n_tok, width)
    z = dot(normed, w_z).reshape(seqs, q, inner)
    d_hidden = dot(cot, w_o).reshape(seqs, q, inner)

    state_in = jnp.concatenate(entering, axis=0)
    y_scan, sums = call(
        functools.partial(gate_sums_kernel, inner=inner),
        0,
        seqs,
        [(y_local, 0), (act, 0), (dtl, 0), (start, 0), (state_in, 0), (z, 0), (d_hidden, 0)],
        [(shape(q, inner), f32, True), (shape(8, q), f32, True)],
        shared=(rows,),
        flops=2 * n_tok * inner * 200,
        moved=16 * n_tok * inner,
    )
    sums = cube_sum(sums, "tp")

    bulk = [None] * 3
    d_states, gate_rows = [], []
    for g in range(chunks):
        have = 0 if g == 0 else 3
        out = call(
            drop(functools.partial(gate_kernel, inner=inner), 8, have),
            g * per,
            per,
            [(y_scan, g * per), (act, g * per), (dtl, g * per), (start, g * per), (z, g * per), (d_hidden, g * per), (sums, g * per)],
            [
                (shape(q, inner), bf16, True),
                (shape(q, inner), bf16, True),
                (shape(q, inner), bf16, True),
                (part(STATE, inner), bf16, False),
                (part(8, inner), f32, False),
            ],
            shared=(rows,),
            into=None if g == 0 else bulk,
            flops=2 * per * q * inner * 200,
            moved=20 * per * q * inner,
        )
        bulk = list(out[:3])
        d_states.append(out[3])
        gate_rows.append(jnp.sum(out[4], axis=0))
    hidden, d_y, d_z = bulk
    later = [chain(d_states[g], decs[g], True) for g in range(chunks)]

    hidden2 = hidden.reshape(n_tok, inner)
    dz2 = d_z.reshape(n_tok, inner)
    mixed_part = cube_scatter(dot(hidden2, w_o, NT), "tp")
    own = lax.dynamic_slice_in_dim(tokens.reshape(n_tok, width), tp_rank * cols, cols, 1).astype(f32)
    mixed = (own + mixed_part).astype(bf16).reshape(seqs, q, cols)
    grad_wo = ring_scatter(dot(cot, hidden2, TN))
    grad_wz = ring_scatter(dot(normed, dz2, TN))
    d_norm_z = dot(dz2, w_z, NT)

    dx_local, dbc_local = call(
        functools.partial(local_back_kernel, inner=inner),
        0,
        seqs,
        [(act, 0), (xdt, 0), (dtl, 0), (start, 0), (start_row, 0), (d_y, 0), (state_in, 0)],
        [(shape(q, inner), f32, True), (shape(q, 2 * STATE), f32, True)],
        flops=16 * seqs * q * q * inner,
        moved=12 * n_tok * inner,
    )

    bulk = [None] * 2
    tap_rows, head_rows = [], []
    for g in range(chunks):
        have = 0 if g == 0 else 2
        o = g * per
        out = call(
            drop(functools.partial(conv_back_kernel, inner=inner, conv=conv), 16, have),
            o,
            per,
            [(act, o), (xdt, o), (dtl, o), (start, o), (d_y, o), (y_scan, o), (dx_local, o), (dbc_local, o), (state_in, o), (later[g], 0), (pre, o), (u, o), (decs[g], 0)],
            [
                (shape(q, conv + LANES), bf16, True),
                (shape(HALO, conv), bf16, True),
                (part(8, conv), f32, False),
                (part(8, LANES), f32, False),
            ],
            shared=(taps, rows, head_par),
            scratch=[pltpu.VMEM((q, conv), f32)],
            into=None if g == 0 else bulk,
            flops=2 * per * q * inner * 800,
            moved=30 * per * q * inner,
        )
        bulk = list(out[:2])
        tap_rows.append(jnp.sum(out[2], axis=0))
        head_rows.append(jnp.sum(out[3], axis=0))
    du, rim = bulk
    rim = shift(rim[:, 8:, :], "ctx", -1)
    edge = du[:, q - 8 :, :conv].astype(f32) + rim.astype(f32)
    du = lax.dynamic_update_slice(du, edge.astype(bf16), (0, q - 8, 0))
    du2 = du.reshape(n_tok, conv + LANES)

    d_normed = cube_scatter(d_norm_z + dot(du2, w_in, NT), "tp")
    grad_in = ring_scatter(dot(normed, du2, TN))

    own_inv = inv_rms.reshape(n_tok, 1)
    hat = own * own_inv
    gain = lax.dynamic_slice_in_dim(in_gain, tp_rank * cols, cols, 0).astype(f32)
    gain_row = jnp.sum(d_normed * hat, axis=0)
    d_hat = d_normed * gain
    full_dot = cube_sum(jnp.sum(d_hat * hat, axis=-1).reshape(seqs, q), "tp").reshape(n_tok, 1)
    own_cot = lax.dynamic_slice_in_dim(cot, tp_rank * cols, cols, 1).astype(f32)
    grad_tokens = (own_cot + own_inv * (d_hat - hat * (full_dot / D))).reshape(seqs, q, cols)

    tap_sum, head_sum, gate_sum = sum(tap_rows), sum(head_rows), sum(gate_rows)
    shared_part = cube_sum(tap_sum[: CONV + 1, inner:], "tp").reshape(-1, LANES)
    pieces = [
        tap_sum[: CONV + 1, :inner].reshape(-1, LANES),
        shared_part,
        gate_sum[0].reshape(-1, LANES),
        jnp.pad(gate_sum[1].reshape(heads, HEADDIM).sum(1), (0, LANES - heads))[None],
        head_sum[:2],
        gain_row.reshape(-1, LANES),
    ]
    small = cube_sum(cube_sum(jnp.concatenate(pieces, 0), "fsdp"), "ctx")
    offsets = [0]
    for piece in pieces:
        offsets.append(offsets[-1] + piece.shape[0])
    got = [small[a:b] for a, b in zip(offsets[:-1], offsets[1:])]
    conv_own = got[0].reshape(CONV + 1, inner)
    conv_all = got[1].reshape(CONV + 1, 2 * STATE)

    grad_bc = cube_sum(grad_in[:, inner:conv], "tp")
    return (
        mixed,
        grad_tokens,
        got[5].reshape(cols),
        jnp.stack([grad_wz, grad_in[:, :inner]], axis=1),
        grad_bc,
        grad_in[:, conv : conv + heads],
        got[4][0, :heads],
        got[4][1, :heads],
        got[3][0, :heads],
        conv_own[:CONV],
        conv_own[CONV],
        conv_all[:CONV],
        conv_all[CONV],
        got[2].reshape(inner),
        grad_wo.T,
    )


def solution(mesh):
    return jax.shard_map(
        per_device,
        mesh=mesh,
        in_specs=(
            P("fsdp", "ctx", None),
            P("fsdp", "ctx"),
            P(),
            P(("fsdp", "ctx"), None, "tp"),
            P(("fsdp", "ctx"), None),
            P(("fsdp", "ctx"), "tp"),
            P("tp"),
            P("tp"),
            P("tp"),
            P(None, "tp"),
            P("tp"),
            P(),
            P(),
            P("tp"),
            P("tp", ("fsdp", "ctx")),
            P("fsdp", "ctx", None),
        ),
        out_specs=(
            P("fsdp", "ctx", "tp"),
            P("fsdp", "ctx", "tp"),
            P("tp"),
            P(("fsdp", "ctx"), None, "tp"),
            P(("fsdp", "ctx"), None),
            P(("fsdp", "ctx"), "tp"),
            P("tp"),
            P("tp"),
            P("tp"),
            P(None, "tp"),
            P("tp"),
            P(),
            P(),
            P("tp"),
            P("tp", ("fsdp", "ctx")),
        ),
        check_vma=False,
    )
```

```python
import functools

import jax
import jax.numpy as jnp
from jax import lax
from jax.experimental import pallas as pl
from jax.experimental.pallas import tpu as pltpu
from jax.sharding import PartitionSpec as P

D = 1536
HEADDIM = 64
STATE = 128
CONV = 4
INNER = 3072
NORM_EPS = 1e-05
LANES = 128
HALO = 16
COST = pl.CostEstimate(flops=2 * 10**12, bytes_accessed=8 * 10**9, transcendentals=0)

bf16 = jnp.bfloat16
f32 = jnp.float32
NN = (((1,), (0,)), ((), ()))
NT = (((1,), (1,)), ((), ()))
TN = (((0,), (0,)), ((), ()))


def rotate(v, axis, steps):
    n = lax.axis_size(axis)
    return lax.ppermute(v, axis, [(i, (i + steps) % n) for i in range(n)])


def shift(v, axis, steps):
    n = lax.axis_size(axis)
    return lax.ppermute(v, axis, [(i, i + steps) for i in range(n) if 0 <= i + steps < n])


def flip(v, axis, mask):
    n = lax.axis_size(axis)
    return lax.ppermute(v, axis, [(i, i ^ mask) for i in range(n)])


def cube_sum(v, axis):
    mask = 1
    while mask < lax.axis_size(axis):
        v = v + flip(v, axis, mask)
        mask *= 2
    return v


def after(v, *deps):
    return lax.optimization_barrier((v,) + deps)[0]


def ring_pieces(v):
    out = [v]
    for _ in range(1, lax.axis_size("ctx")):
        out.append(rotate(out[-1], "ctx", 1))
    return out


def all_pieces(ring, *start):
    nc, nf = lax.axis_size("ctx"), lax.axis_size("fsdp")
    c, f = lax.axis_index("ctx"), lax.axis_index("fsdp")
    pieces, places = [], []
    for step, piece in enumerate(ring):
        owner = lax.rem(c - step + nc, nc)
        if start:
            piece = after(piece, *start)
        for j in range(nf):
            if j:
                piece = rotate(piece, "fsdp", 1)
            pieces.append(piece)
            places.append(lax.rem(f - j + nf, nf) * nc + owner)
    return pieces, jnp.stack(places).astype(jnp.int32)


def assemble(pieces, places):
    rows = pieces[0].shape[0]
    whole = jnp.zeros((rows * len(pieces), pieces[0].shape[1]), pieces[0].dtype)
    for i, piece in enumerate(pieces):
        whole = lax.dynamic_update_slice_in_dim(whole, piece, places[i] * rows, 0)
    return whole


class Spread:
    def __init__(self, g, runs):
        nc, nf = lax.axis_size("ctx"), lax.axis_size("fsdp")
        c, f = lax.axis_index("ctx"), lax.axis_index("fsdp")
        self.g, self.rows, self.runs = g, g.shape[0] // (nc * nf), runs
        self.place = lambda k, step: lax.rem(f + k, nf) * nc + lax.rem(c - step + nc, nc)
        self.come = []
        for run in runs:
            for k in range(1, nf):
                take = lambda at, count: lax.dynamic_slice_in_dim(g, at * self.rows, count * self.rows, 0)
                if len(run) == nc:
                    sent = take(lax.rem(f + k, nf) * nc, nc)
                else:
                    sent = jnp.concatenate([take(self.place(k, step), 1) for step in run])
                self.come.append((run, rotate(sent, "fsdp", k)))

    def landed(self, step):
        return [v for run, v in self.come if step in run]

    def terms(self, step):
        nc, c = lax.axis_size("ctx"), lax.axis_index("ctx")
        out = [(self.g, self.place(0, step))]
        for run, v in self.come:
            if step in run:
                out.append((v, lax.rem(c - step + nc, nc) if len(run) == nc else run.index(step)))
        return out


def block_sum(groups, last, rows, dtype, order):
    arrays = [a for group in groups for a, _ in group]
    places = jnp.stack([jnp.asarray(at, jnp.int32) for group in groups for _, at in group])
    widths = [group[0][0].shape[1] for group in groups]
    specs = [pl.BlockSpec((rows, a.shape[1]), lambda i, p, j=j: (p[j], 0)) for j, a in enumerate(arrays)]
    if last is not None:
        arrays.append(last)
        specs.append(pl.BlockSpec(last.shape, lambda i, p: (0, 0)))
        order.land(last)
    deps = order.deps()

    def kernel(places_ref, *refs):
        out, at, lo = refs[-1], 0, 0
        for group, width in zip(groups, widths):
            total = sum(r[...].astype(f32) for r in refs[at : at + len(group)])
            if last is not None:
                total = total + refs[len(arrays) - 1][:, lo : lo + width].astype(f32)
            out[:, lo : lo + width] = total.astype(dtype)
            at, lo = at + len(group), lo + width

    out = pl.pallas_call(
        kernel,
        grid_spec=pltpu.PrefetchScalarGridSpec(
            num_scalar_prefetch=1,
            grid=(1,),
            in_specs=specs + [pl.BlockSpec(memory_space=pl.ANY)] * len(deps),
            out_specs=pl.BlockSpec((rows, sum(widths)), lambda i, p: (0, 0)),
        ),
        out_shape=jax.ShapeDtypeStruct((rows, sum(widths)), dtype),
        compiler_params=pltpu.CompilerParams(vmem_limit_bytes=32 * 2**20),
        cost_estimate=COST,
    )(places, *arrays, *deps)
    return order.leave(out)


class Ring:
    def __init__(self, spreads, order):
        self.spreads, self.at = spreads, 0
        self.total, self.come = None, None
        self.step(order)

    def done(self):
        return self.at == lax.axis_size("ctx")

    def step(self, order):
        if self.done():
            return
        self.at += 1
        groups = [one.terms(self.at) for one in self.spreads]
        last = lax.axis_size("ctx") == self.at
        self.total = block_sum(groups, self.come, self.spreads[0].rows, f32 if last else bf16, order)
        if not last:
            self.come = rotate(self.total, "ctx", 1)


def halve_kernel(near, come, near_ref, away_ref):
    total = near[...] + come[...].astype(f32)
    near_ref[...] = total[:, : near_ref.shape[1]]
    away_ref[...] = total[:, near_ref.shape[1] :].astype(bf16)


def add_kernel(a, b, out_ref):
    out_ref[...] = a[...] + b[...]


class Cube:
    def __init__(self, near, away):
        self.near, self.away, self.mask = near, away, 1
        self.come = flip(away, "tp", 1)

    def halve(self, order):
        seqs, rows, wide = self.near.shape
        while self.mask * 2 < lax.axis_size("tp"):
            wide //= 2
            order.land(self.come)
            out = (seqs, rows, wide)
            self.near, self.away = call(
                halve_kernel,
                0,
                seqs,
                [(self.near, 0), (self.come, 0)],
                [(out, f32, True), (out, bf16, True)],
                deps=order.deps(),
            )
            order.leave(self.away)
            self.mask *= 2
            self.come = flip(self.away, "tp", self.mask)

    def total(self):
        return self.near + self.come.astype(f32)


class Hops:
    def __init__(self, v, axes):
        self.v = v
        self.todo = [(axis, 1 << i) for axis in axes for i in range(lax.axis_size(axis).bit_length() - 1)]
        self.come = None

    def go(self, order):
        if self.come is not None:
            order.land(self.come)
            self.v = small_call(add_kernel, [self.v, self.come], [(self.v.shape, f32)], order)[0]
            order.leave(self.v)
            self.come = None
        if self.todo:
            self.come = flip(self.v, *self.todo.pop(0))

    def end(self, order):
        while self.come is not None:
            self.go(order)
        return self.v


def small_call(kernel, operands, outs, order, scalar=None, scratch=()):
    deps = order.deps()
    n_in = len(operands) + (scalar is not None)

    def run(*refs):
        kernel(*refs[:n_in], *refs[n_in + len(deps) :])

    vmem = pl.BlockSpec(memory_space=pltpu.VMEM)
    return pl.pallas_call(
        run,
        in_specs=([] if scalar is None else [pl.BlockSpec(memory_space=pltpu.SMEM)])
        + [vmem] * len(operands)
        + [pl.BlockSpec(memory_space=pl.ANY)] * len(deps),
        out_specs=[vmem] * len(outs),
        out_shape=[jax.ShapeDtypeStruct(*o) for o in outs],
        scratch_shapes=list(scratch),
        compiler_params=pltpu.CompilerParams(vmem_limit_bytes=32 * 2**20),
        cost_estimate=COST,
    )(*([] if scalar is None else [scalar]), *operands, *deps)


class Chain:
    def __init__(self, parts, decay, reverse):
        self.parts, self.decay, self.reverse = parts, decay, reverse
        self.hop, self.last, self.entering = 0, None, []

    def send(self, order):
        n = lax.axis_size("ctx")
        self.hop += 1
        if self.hop >= n:
            return
        out = self.parts
        if self.last is not None:
            order.land(self.last)
            out = small_call(
                combine_kernel, [self.parts, self.decay, self.last], [(out.shape, bf16)], order
            )[0]
            order.leave(out)
        hop = self.hop
        pair = (n - hop, n - hop - 1) if self.reverse else (hop - 1, hop)
        self.last = lax.ppermute(out, "ctx", [pair])
        self.entering.append(self.last)

    def land(self, order):
        order.land(self.last)


class Order:
    def __init__(self):
        self.waits = []

    def land(self, *arrays):
        self.waits += arrays

    def enter(self, v):
        v = after(v, *self.waits)
        self.waits = []
        return v

    def deps(self):
        waits, self.waits = self.waits, []
        return waits

    def leave(self, v):
        self.waits = self.waits + [v]
        return v


def dot(a, b, dims=NN):
    return lax.dot_general(a, b, dims, preferred_element_type=f32)


def split(v, terms):
    out = []
    for i in range(terms):
        t = v.astype(bf16)
        out.append(t)
        if i + 1 < terms:
            v = v - t.astype(f32)
    return out


def constants(inner, q):
    heads = jnp.arange(LANES, dtype=jnp.int32)[:, None] == jnp.arange(inner, dtype=jnp.int32)[None] // HEADDIM
    spread = heads.astype(bf16)
    tri = jnp.arange(q, dtype=jnp.int32)[None] <= jnp.arange(q, dtype=jnp.int32)[:, None]
    return jnp.concatenate([spread, spread]), spread.T, tri.astype(bf16)


def widen(v, spread):
    return dot(jnp.concatenate(split(v, 2), 1), spread[...])


def narrow(v, gather, terms):
    out = None
    for t in split(v, terms):
        s = dot(t, gather[...])
        out = s if out is None else out + s
    return out


def tri_sum(tri, v, dims=NN):
    out = None
    for t in split(v, 3):
        s = dot(tri[...], t, dims)
        out = s if out is None else out + s
    return out


def one_of(refs):
    total = refs[0][...]
    for r in refs[1:]:
        total = total + r[...]
    return total


def halves(v):
    lane = lax.broadcasted_iota(jnp.int32, v.shape, 1)
    zero = jnp.zeros_like(v)
    return jnp.where(lane < HEADDIM, v, zero), jnp.where(lane >= HEADDIM, v, zero)


def sigmoid(v):
    return lax.logistic(v)


def gather_rows(places, pieces, whole):
    rows = pieces[0].shape[0]
    for i, piece in enumerate(pieces):
        whole[pl.ds(pl.multiple_of(places[i] * rows, 16), rows), :] = piece[...]


def project_kernel(nx, start, w, taps, bias, head_par, spread, tri, *refs, inner, conv):
    u_ref, pre_ref, act_ref, xdt_ref, dtl_ref, state_ref, dec_ref = refs[-7:]
    q = start.shape[0]
    u = dot(nx[...], w[...])
    u_ref[...] = u[:, :conv].astype(bf16)
    at = lax.broadcasted_iota(jnp.int32, (q, 1), 0)
    begin = start[...]
    since = at - begin
    for lo in range(0, conv, LANES):
        cols = slice(lo, lo + LANES)
        ut = u[:, cols]
        acc = bias[0:1, cols] + taps[CONV - 1 : CONV, cols] * ut[HALO:]
        for j in range(1, CONV):
            window = ut[HALO - j : HALO - j + q]
            acc = acc + taps[CONV - 1 - j : CONV - j, cols] * jnp.where(since >= j, window, 0.0)
        pre_ref[:, cols] = acc.astype(bf16)
        act_ref[:, cols] = (acc * sigmoid(acc)).astype(bf16)
    v = u[HALO:, conv:] + head_par[0:1, :]
    dt = jnp.maximum(v, 0.0) + jnp.log1p(jnp.exp(-jnp.abs(v)))
    cum = tri_sum(tri, -dt * jnp.exp(head_par[1:2, :]))
    dtl_ref[:, :LANES] = dt
    dtl_ref[:, LANES:] = cum
    end = cum[q - 1 : q, :]
    begin_last = begin[q - 1 : q, :]
    tail = jnp.where(begin == begin_last, jnp.exp(end - cum), 0.0)
    xh = act_ref[:, :inner].astype(f32)
    xdt = (xh * widen(dt, spread)).astype(bf16)
    xdt_ref[...] = xdt
    weighted = (xdt.astype(f32) * widen(tail, spread)).astype(bf16)
    b = act_ref[:, inner : inner + STATE]
    state_ref[...] = dot(b, weighted, TN).astype(bf16)
    total = jnp.where(begin_last < 0, jnp.exp(end), 0.0)
    dec_ref[...] = widen(jnp.broadcast_to(total, (8, LANES)), spread)[0:1]


def project_first_kernel(places, nx, start, taps, bias, head_par, spread, tri, *refs, pieces, inner, conv):
    w = refs[-1]

    @pl.when(pl.program_id(0) == 0)
    def _():
        gather_rows(places, refs[:pieces], w)

    project_kernel(nx, start, w, taps, bias, head_par, spread, tri, *refs[pieces:-1], inner=inner, conv=conv)


def combine_kernel(parts, decay, last, out_ref):
    out_ref[...] = (parts[...].astype(f32) + decay[...] * last[...].astype(f32)).astype(bf16)


def score_mask(begin_col, q):
    r = lax.broadcasted_iota(jnp.int32, (q, q), 0)
    c = lax.broadcasted_iota(jnp.int32, (q, q), 1)
    return (c <= r) & (c >= begin_col)


def score_mask_t(begin_row, q):
    r = lax.broadcasted_iota(jnp.int32, (q, q), 0)
    c = lax.broadcasted_iota(jnp.int32, (q, q), 1)
    return (r <= c) & (r >= begin_row)


def local_kernel(act, xdt, dtl, start, y_ref, *, inner):
    q = start.shape[0]
    b = act[:, inner : inner + STATE]
    c = act[:, inner + STATE : inner + 2 * STATE]
    scores = jnp.where(score_mask(start[...], q), dot(c, b, NT), 0.0)
    cum = dtl[:, LANES:]
    cum_t = cum.T
    for pair in range(inner // LANES):
        cols = slice(pair * LANES, (pair + 1) * LANES)
        weights = []
        for h in (2 * pair, 2 * pair + 1):
            gap = jnp.minimum(cum[:, h : h + 1] - cum_t[h : h + 1, :], 0.0)
            weights.append((jnp.exp(gap) * scores).astype(bf16))
        even, odd = halves(xdt[:, cols])
        y_ref[:, cols] = dot(weights[0], even) + dot(weights[1], odd)


def gate_sums_kernel(nx, cot, y_in, act, dtl, start, state, w, rows, spread, y_ref, z_ref, dh_ref, sums_ref, *, inner):
    q = start.shape[0]
    c = act[:, inner + STATE : inner + 2 * STATE]
    zz = dot(nx[HALO:], w[:, :inner])
    z_ref[...] = zz.astype(bf16)
    d_hidden = dot(cot[...], w[:, inner:])
    dh_ref[...] = d_hidden.astype(bf16)
    into = widen(jnp.where(start[...] < 0, jnp.exp(dtl[:, LANES:]), 0.0), spread)
    y = y_in[...] + into * dot(c, one_of(state))
    y_ref[...] = y
    gated = (y + rows[0:1, :] * act[:, :inner].astype(f32)) * (zz * sigmoid(zz))
    e = d_hidden * rows[1:2, :]
    ones = jnp.ones((8, inner), bf16)
    sq = dot(ones, (gated * gated).astype(bf16), NT)
    eg = dot(ones, (e * gated).astype(bf16), NT)
    row = lax.broadcasted_iota(jnp.int32, (8, q), 0)
    sums_ref[...] = jnp.where(row == 0, sq, eg)


def gate_sums_first_kernel(places, nx, cot, y_in, act, dtl, start, *refs, pieces, hops, inner):
    state, (rows, spread), refs = refs[:hops], refs[hops : hops + 2], refs[hops + 2 :]
    y_ref, z_ref, dh_ref, sums_ref, w = refs[pieces], refs[pieces + 1], refs[pieces + 2], refs[pieces + 3], refs[-1]

    @pl.when(pl.program_id(0) == 0)
    def _():
        gather_rows(places, refs[:pieces], w)

    gate_sums_kernel(
        nx, cot, y_in, act, dtl, start, state, w, rows, spread, y_ref, z_ref, dh_ref, sums_ref, inner=inner
    )


def gate_sums_next_kernel(nx, cot, y_in, act, dtl, start, *refs, hops, inner):
    gate_sums_kernel(nx, cot, y_in, act, dtl, start, refs[:hops], *refs[hops:], inner=inner)


def mix_kernel(rank, hidden, w, near_ref, away_ref):
    seqs, q, cols = near_ref.shape
    k = pl.program_id(0)
    out = dot(hidden[...].reshape(seqs * q, hidden.shape[2]), w[...], NT).reshape(seqs, q, cols)

    @pl.when(lax.rem(k, 2) == 0)
    def _():
        near_ref[...] = out

    @pl.when(lax.rem(k, 2) == 1)
    def _():
        away_ref[...] = out.astype(bf16)


def norm_back_kernel(rank, du, rim, nx, z_part, w_in, near_ref, away_ref, gain_ref, own, part):
    seqs, q = du.shape[0], du.shape[1] - HALO
    cols = w_in.shape[0]
    tp = near_ref.shape[2] * 2 // cols
    k = pl.program_id(0)

    @pl.when(k == 0)
    def _():
        for s in range(seqs):
            own[s * q : (s + 1) * q - 16, :] = du[s, HALO:q, :]
            edge = du[s, q : q + HALO, :].astype(f32)
            own[(s + 1) * q - 16 : (s + 1) * q, :] = (edge + rim[s].astype(f32)).astype(bf16)
        part[...] = jnp.zeros_like(part)

    out = dot(own[...], w_in[...], NT)
    gains = jnp.zeros((1, cols), f32)
    for s in range(seqs):
        mine = out[s * q : (s + 1) * q] + z_part[s, HALO:, :].astype(f32)
        prod = mine * nx[s, HALO:, :].astype(f32)
        folded = prod[:, :LANES]
        for lo in range(LANES, cols, LANES):
            folded = folded + prod[:, lo : lo + LANES]
        part[s * q : (s + 1) * q, :] += folded
        gains = gains + jnp.sum(prod, axis=0, keepdims=True)
        for j in range(tp):
            to = slice(j // 2 * cols, (j // 2 + 1) * cols)

            @pl.when(k == j)
            def _():
                ref = away_ref if j % 2 else near_ref
                ref[s, :q, to] = mine.astype(ref.dtype)

    gain_ref[...] = jnp.broadcast_to(gains, gain_ref.shape)

    @pl.when(k == tp - 1)
    def _():
        ones = jnp.ones((16, LANES), bf16)
        for s in range(seqs):
            total = None
            for t in split(part[s * q : (s + 1) * q, :], 2):
                one = dot(ones, t, NT)
                total = one if total is None else total + one
            total = jnp.concatenate([total, jnp.zeros((16, cols - q), f32)], 1)
            for j in range(tp):
                to = slice(j // 2 * cols, (j // 2 + 1) * cols)
                ref = away_ref if j % 2 else near_ref
                ref[s, q:, to] = total.astype(ref.dtype)


def pack_kernel(gain, *refs, chunks, inner, conv):
    taps, heads, gates = refs[:chunks], refs[chunks : 2 * chunks], refs[2 * chunks : 3 * chunks]
    tp_ref, own_ref = refs[-2:]
    total = lambda refs: sum(jnp.sum(r[...], axis=0) for r in refs)
    tap = total(taps)
    row = lax.broadcasted_iota(jnp.int32, gain.shape, 0)
    tp_ref[:, : 2 * STATE] = tap[:, inner:]
    tp_ref[:, 2 * STATE :] = jnp.where(row == 0, gain[...], 0.0)
    own_ref[:, :inner] = tap[:, :inner]
    own_ref[:, inner : inner + LANES] = total(heads)
    own_ref[:, inner + LANES :] = total(gates)


def norm_kernel(x, halo, gain, nx_ref, inv_ref):
    wide = x[...].astype(f32)
    width = wide.shape[1]
    inv = lax.rsqrt(jnp.mean(wide * wide, axis=-1, keepdims=True) + NORM_EPS)
    inv_ref[...] = inv
    nx_ref[HALO:, :] = (wide * inv * gain[0:1, :]).astype(bf16)
    edge = halo[...].astype(f32)
    inv = lax.rsqrt(jnp.mean(edge * edge, axis=-1, keepdims=True) + NORM_EPS)
    nx_ref[:HALO, :] = (edge * inv * gain[0:1, :]).astype(bf16)


def gate_kernel(y_in, act, dtl, start, z, dh, sums, rows, spread, *refs, inner):
    hidden_ref, dy_ref, dz_ref, dstate_ref, grads_ref = refs[-5:]
    xh = act[:, :inner].astype(f32)
    y = y_in[...] + rows[0:1, :] * xh
    zz = z[...].astype(f32)
    sig = sigmoid(zz)
    silu = zz * sig
    gated = y * silu
    gain = rows[1:2, :]
    d_hidden = dh[...].astype(f32)
    sums_t = sums[...].T
    inv = lax.rsqrt(sums_t[:, 0:1] / INNER + NORM_EPS)
    back = sums_t[:, 1:2] * (inv * inv * inv) / INNER
    scaled = gated * inv
    hidden_ref[...] = (scaled * gain).astype(bf16)
    dg = inv * (d_hidden * gain) - gated * back
    dy = (dg * silu).astype(bf16)
    dy_ref[...] = dy
    dz_ref[:HALO, :] = jnp.zeros((HALO, inner), bf16)
    dz_ref[HALO:, :] = (dg * y * sig * (1.0 + zz * (1.0 - sig))).astype(bf16)
    gate_row = jnp.sum(d_hidden * scaled, axis=0, keepdims=True)
    dy_wide = dy.astype(f32)
    skip_row = jnp.sum(dy_wide * xh, axis=0, keepdims=True)
    row = lax.broadcasted_iota(jnp.int32, (8, inner), 0)
    grads_ref[...] = jnp.where(row == 0, gate_row, jnp.where(row == 1, skip_row, 0.0))
    into = widen(jnp.where(start[...] < 0, jnp.exp(dtl[:, LANES:]), 0.0), spread)
    c = act[:, inner + STATE : inner + 2 * STATE]
    dstate_ref[...] = dot(c, (into * dy_wide).astype(bf16), TN).astype(bf16)


def local_back_kernel(act, xdt, dtl, start, start_row, dy, *refs, hops, inner):
    state, (spread, dx_ref, dbc_ref) = refs[:hops], refs[hops:]
    q = start.shape[0]
    b = act[:, inner : inner + STATE]
    c = act[:, inner + STATE : inner + 2 * STATE]
    mask = score_mask_t(start_row[...], q)
    scores = jnp.where(mask, dot(b, c, NT), 0.0)
    cum = dtl[:, LANES:]
    cum_t = cum.T
    total = jnp.zeros((q, q), f32)
    for pair in range(inner // LANES):
        cols = slice(pair * LANES, (pair + 1) * LANES)
        dy_pair = dy[:, cols]
        x_even, x_odd = halves(xdt[:, cols])
        dy_even, dy_odd = halves(dy_pair)
        out = None
        for h, x_one, dy_one in ((2 * pair, x_even, dy_even), (2 * pair + 1, x_odd, dy_odd)):
            decay = jnp.exp(jnp.minimum(cum_t[h : h + 1, :] - cum[:, h : h + 1], 0.0))
            total = total + dot(x_one, dy_pair, NT) * decay
            term = dot((decay * scores).astype(bf16), dy_one)
            out = term if out is None else out + term
        dx_ref[:, cols] = out
    d_scores = jnp.where(mask, total, 0.0).astype(bf16)
    into = widen(jnp.where(start[...] < 0, jnp.exp(cum), 0.0), spread)
    weighted = (into * dy[...].astype(f32)).astype(bf16)
    dbc_ref[:, :STATE] = dot(d_scores, c)
    dbc_ref[:, STATE:] = dot(d_scores, b, TN) + dot(weighted, one_of(state), NT)


def conv_back_kernel(act, xdt, dtl, start, dy, y_in, dx, dbc, pre, u, dec, *refs, hops, inner, conv):
    state, later, refs = refs[:hops], refs[hops : 2 * hops], refs[2 * hops :]
    taps, rows, head_par, spread, gather, tri = refs[:6]
    du_ref, tap_ref, head_ref, dact = refs[-4:]
    q = start.shape[0]
    begin = start[...]
    b = act[:, inner : inner + STATE]
    dt, cum = dtl[:, :LANES], dtl[:, LANES:]
    end = cum[q - 1 : q, :]
    begin_last = begin[q - 1 : q, :]
    tail = widen(jnp.where(begin == begin_last, jnp.exp(end - cum), 0.0), spread)
    x_dt = xdt[...].astype(f32)
    d_y = dy[...].astype(f32)
    g = one_of(later)
    dx_tail = tail * dot(b, g)
    dact[:, inner : inner + STATE] = dbc[:, :STATE] + dot((x_dt * tail).astype(bf16), g, NT)
    dact[:, inner + STATE :] = dbc[:, STATE:]
    dx_local = dx[...]
    dx_all = dx_local + dx_tail
    dact[:, :inner] = dx_all * widen(dt, spread) + rows[0:1, :] * d_y
    flux_near = narrow(d_y * y_in[...] - x_dt * dx_local, gather, 3)
    flux_tail = narrow(x_dt * dx_tail, gather, 2)
    d_dt = narrow(dx_all * act[:, :inner].astype(f32), gather, 2)
    through = jnp.sum(dec[...] * (g.astype(f32) * one_of(state).astype(f32)), axis=0, keepdims=True)
    through = narrow(jnp.broadcast_to(through, (8, inner)), gather, 2)[0:1]
    d_log = tri_sum(tri, flux_near, TN) + (tri_sum(tri, flux_tail) - flux_tail) + through
    rate = jnp.exp(head_par[1:2, :])
    d_raw = (d_dt - rate * d_log) * (1.0 - jnp.exp(-dt))
    du_ref[:HALO, conv:] = jnp.zeros((HALO, LANES), bf16)
    du_ref[HALO:, conv:] = d_raw.astype(bf16)
    bias_row = jnp.sum(d_raw, axis=0, keepdims=True)
    log_row = -jnp.sum(d_log * dt * rate, axis=0, keepdims=True)
    row = lax.broadcasted_iota(jnp.int32, (8, LANES), 0)
    head_ref[...] = jnp.where(row == 0, bias_row, jnp.where(row == 1, log_row, 0.0))
    since = lax.broadcasted_iota(jnp.int32, (q, 1), 0) - begin
    for lo in range(0, conv, LANES):
        cols = slice(lo, lo + LANES)
        p = pre[:, cols].astype(f32)
        sig = sigmoid(p)
        dp = dact[:, cols] * (sig * (1.0 + p * (1.0 - sig)))
        ut = u[:, cols].astype(f32)
        zeros = jnp.zeros((HALO, LANES), f32)
        total = jnp.concatenate([zeros, taps[CONV - 1 : CONV, cols] * dp], 0)
        tap_rows = [jnp.sum(dp * ut[HALO:], axis=0, keepdims=True)]
        for j in range(1, CONV):
            masked = jnp.where(since >= j, dp, 0.0)
            tap_rows.append(jnp.sum(masked * ut[HALO - j : HALO - j + q], axis=0, keepdims=True))
            moved = jnp.concatenate([zeros, taps[CONV - 1 - j : CONV - j, cols] * masked, zeros], 0)
            total = total + moved[j : j + q + HALO]
        du_ref[:, cols] = total.astype(bf16)
        out = jnp.sum(dp, axis=0, keepdims=True)
        for j in range(CONV):
            out = jnp.where(row == CONV - 1 - j, tap_rows[j], jnp.where(row == CONV, out, 0.0) if j == 0 else out)
        tap_ref[:, cols] = out


def call(kernel, first, count, ins, outs, shared=(), scalar=None, scratch=(), into=None, deps=()):
    def spec(shape, base):
        block = (None,) + tuple(shape[1:])
        rest = (0,) * (len(shape) - 1)
        return pl.BlockSpec(block, lambda s: (s + base,) + rest)

    in_specs = [spec(a.shape, o) for a, o in ins]
    in_specs += [pl.BlockSpec(a.shape, lambda s, n=a.ndim: (0,) * n) for a in shared]
    operands = [a for a, _ in ins] + list(shared)
    if scalar is not None:
        in_specs.insert(0, pl.BlockSpec(memory_space=pltpu.SMEM))
        operands.insert(0, scalar)
    n_args = len(operands)
    operands += list(deps)
    in_specs += [pl.BlockSpec(memory_space=pl.ANY)] * len(deps)
    aliases = {}
    if into is not None:
        for i, buf in enumerate(into):
            if buf is not None:
                aliases[len(operands)] = i
                operands.append(buf)
                in_specs.append(pl.BlockSpec(memory_space=pl.ANY))
    n_in = len(operands)

    def run(*refs):
        kernel(*refs[:n_args], *refs[n_in:])

    return pl.pallas_call(
        run,
        grid=(count,),
        in_specs=in_specs,
        out_specs=[spec(s, first if whole else 0) if whole is not None else pl.BlockSpec(s, lambda i, n=len(s): (0,) * n) for s, _, whole in outs],
        out_shape=[jax.ShapeDtypeStruct(s, d) for s, d, _ in outs],
        scratch_shapes=list(scratch),
        input_output_aliases=aliases,
        compiler_params=pltpu.CompilerParams(vmem_limit_bytes=48 * 2**20),
        cost_estimate=COST,
    )(*operands)


def call_slices(kernel, rank, tp, wholes, weights, outs, scratch=(), deps=()):
    specs, operands = [], []
    for a, cut in wholes:
        if cut:
            block = a.shape[:-1] + (a.shape[-1] // tp,)
            specs.append(pl.BlockSpec(block, lambda k, r, n=a.ndim: (0,) * (n - 1) + (r[0] ^ k,)))
        else:
            specs.append(pl.BlockSpec(a.shape, lambda k, r, n=a.ndim: (0,) * n))
        operands.append(a)
    for a, at, cols in weights:
        specs.append(pl.BlockSpec((a.shape[0] // tp, cols), lambda k, r, j=at // cols: (r[0] ^ k, j)))
        operands.append(a)
    n_args = len(operands) + 1
    operands += list(deps)
    specs += [pl.BlockSpec(memory_space=pl.ANY)] * len(deps)
    n_in = len(operands) + 1

    def run(*refs):
        kernel(*refs[:n_args], *refs[n_in:])

    out_specs = []
    for shape, _, cut in outs:
        n = len(shape)
        if cut is None:
            out_specs.append(pl.BlockSpec((shape[0], shape[1] // tp), lambda k, r: (0, r[0] ^ k)))
        elif cut:
            out_specs.append(
                pl.BlockSpec(shape[:-1] + (shape[-1] * 2 // tp,), lambda k, r, n=n: (0,) * (n - 1) + (k // 2,))
            )
        else:
            out_specs.append(pl.BlockSpec(shape, lambda k, r, n=n: (0,) * n))
    return pl.pallas_call(
        run,
        grid_spec=pltpu.PrefetchScalarGridSpec(
            num_scalar_prefetch=1,
            grid=(tp,),
            in_specs=specs,
            out_specs=out_specs,
            scratch_shapes=list(scratch),
        ),
        out_shape=[jax.ShapeDtypeStruct(s, d) for s, d, _ in outs],
        compiler_params=pltpu.CompilerParams(vmem_limit_bytes=48 * 2**20),
        cost_estimate=COST,
    )(rank, *operands)


def pack(taps, heads, gates, gain, order, inner, conv):
    out = small_call(
        functools.partial(pack_kernel, chunks=len(taps), inner=inner, conv=conv),
        [gain, *taps, *heads, *gates],
        [((8, 2 * STATE + gain.shape[1]), f32), ((8, 2 * inner + LANES), f32)],
        order,
    )
    order.leave(out[0])
    return out


def per_device(
    tokens,
    segment_ids,
    in_gain,
    w_zx,
    w_bc,
    w_dt,
    dt_bias,
    a_log,
    skip_gain,
    conv_x,
    conv_x_bias,
    conv_bc,
    conv_bc_bias,
    gate_gain,
    w_out,
    cotangent,
):
    tp_count, tp_rank = lax.axis_size("tp"), lax.axis_index("tp")
    ctx_rank = lax.axis_index("ctx")
    seqs, q, width = tokens.shape
    inner = w_zx.shape[2]
    heads = w_dt.shape[1]
    conv = inner + 2 * STATE
    cols = width // tp_count
    n_tok = seqs * q
    chunks = 2 if seqs % 2 == 0 else 1
    per = seqs // chunks

    n_ctx = lax.axis_size("ctx")
    rank = tp_rank.astype(jnp.int32)[None]
    shape = lambda *s: (seqs,) + s
    part = lambda *s: (per,) + s
    order = Order()

    first_w = jnp.concatenate(
        [w_zx[:, 1, :], w_bc, jnp.pad(w_dt, ((0, 0), (0, LANES - heads)))], axis=1
    )
    ring_in = ring_pieces(first_w)
    halo = shift(jnp.pad(tokens[:, q - 8 :, :], ((0, 0), (8, 0), (0, 0))), "ctx", 1)
    pieces_in, places = all_pieces(ring_in)
    in_kernel = first_w.shape[0] % 16 == 0
    second_w = jnp.concatenate([w_zx[:, 0, :], w_out.T], axis=1)
    ring_rest = ring_pieces(after(second_w, ring_in[-1]))
    pieces_rest, _ = all_pieces(ring_rest, pieces_in[-1])
    spread, gather, tri = constants(inner, q)
    if not in_kernel:
        w_in, w_rest = assemble(pieces_in, places), assemble(pieces_rest, places)

    gain = jnp.broadcast_to(in_gain.astype(f32)[None], (8, width))
    bulk = None
    order.land(halo)
    for g in range(chunks):
        order.land(*ring_in[g + 1 : g + 2], *pieces_in[2 * g + 1 : 2 * g + 2])
        bulk = call(
            norm_kernel,
            g * per,
            per,
            [(tokens, g * per), (halo, g * per)],
            deps=order.deps(),
            outs=[(shape(q + HALO, width), bf16, True), (shape(q, 1), f32, True)],
            shared=(gain,),
            into=bulk,
        )
        order.leave(bulk[1])
    nx, inv_rms = bulk

    begin = segment_ids - ctx_rank * q
    start = begin[:, :, None]
    start_row = begin[:, None, :]
    taps = jnp.concatenate([conv_x, conv_bc], axis=1).astype(f32)
    bias = jnp.concatenate([conv_x_bias, conv_bc_bias]).astype(f32)[None]
    head_par = jnp.pad(jnp.stack([dt_bias, a_log]), ((0, 6), (0, LANES - heads)))
    rows = jnp.pad(jnp.stack([jnp.repeat(skip_gain, HEADDIM), gate_gain.astype(f32)]), ((0, 6), (0, 0)))

    bulk = [None] * 5
    chains, decs = [], []
    for g in range(chunks):
        have = 0 if g == 0 else 5
        o = g * per
        order.land(ring_rest[min(g + 1, n_ctx - 1)])
        if g:
            order.land(pieces_rest[min(2 * g - 1, len(pieces_rest) - 1)])
        first = g == 0 and in_kernel
        given = [taps, bias, head_par, spread, tri]
        outs = [
            (shape(q + HALO, conv), bf16, True),
            (shape(q, conv), bf16, True),
            (shape(q, conv), bf16, True),
            (shape(q, inner), bf16, True),
            (shape(q, 2 * LANES), f32, True),
            (part(STATE, inner), bf16, False),
            (part(1, inner), f32, False),
        ]
        if first:
            kernel = functools.partial(project_first_kernel, pieces=len(pieces_in), inner=inner, conv=conv)
        else:
            kernel = functools.partial(project_kernel, inner=inner, conv=conv)
        out = call(
            kernel,
            o,
            per,
            [(nx, o), (start, o)],
            outs + [((width, conv + LANES), bf16, None)] if first else outs,
            shared=given + pieces_in if first else [w_in] + given,
            scalar=places if first else None,
            into=None if g == 0 else bulk,
            deps=order.deps(),
        )
        if first:
            w_in = out[7]
        bulk = list(out[:5])
        decs.append(order.leave(out[6]))
        chains.append(Chain(out[5], out[6], False))
        chains[-1].send(order)
    u, pre, act, xdt, dtl = bulk

    states = chains
    landing = lambda i: pieces_rest[min(i, len(pieces_rest) - 1)]
    if n_ctx > 2:
        states[0].send(order)
    order.land(ring_rest[min(chunks + 1, n_ctx - 1)], landing(2 * chunks - 1))
    y_local = order.leave(
        call(
            functools.partial(local_kernel, inner=inner),
            0,
            seqs,
            [(act, 0), (xdt, 0), (dtl, 0), (start, 0)],
            deps=order.deps(),
            outs=[(shape(q, inner), f32, True)],
        )[0]
    )
    for one in states[1:]:
        one.send(order)
    for hop in range(3, n_ctx):
        for i, one in enumerate(states):
            if hop == 3:
                order.land(landing(2 * chunks + 1 + 2 * i))
            one.send(order)

    bulk = None
    for g in range(chunks):
        o = g * per
        first = g == 0 and in_kernel
        hops = len(states[g].entering)
        outs = [
            (shape(q, inner), f32, True),
            (shape(q, inner), bf16, True),
            (shape(q, inner), bf16, True),
            (shape(8, q), f32, True),
        ]
        if first:
            kernel = functools.partial(gate_sums_first_kernel, pieces=len(pieces_rest), hops=hops, inner=inner)
            given = [rows, spread] + pieces_rest
            outs = outs + [((width, width), bf16, None)]
        else:
            kernel = functools.partial(gate_sums_next_kernel, hops=hops, inner=inner)
            given = [w_rest, rows, spread]
        out = call(
            kernel,
            o,
            per,
            [(nx, o), (cotangent, o), (y_local, o), (act, o), (dtl, o), (start, o)]
            + [(v, 0) for v in states[g].entering],
            outs,
            shared=given,
            scalar=places if first else None,
            deps=order.deps(),
            into=bulk,
        )
        if first:
            w_rest = out[4]
        bulk = list(out[:4])
        order.leave(out[3])
    y_scan, z, d_hidden, sums = bulk
    sums = cube_sum(sums, "tp")

    bulk = [None] * 3
    chains, gate_rows = [], []
    for g in range(chunks):
        have = 0 if g == 0 else 3
        o = g * per
        out = call(
            functools.partial(gate_kernel, inner=inner),
            o,
            per,
            [(y_scan, o), (act, o), (dtl, o), (start, o), (z, o), (d_hidden, o), (sums, o)],
            deps=order.deps(),
            outs=[
                (shape(q, inner), bf16, True),
                (shape(q, inner), bf16, True),
                (shape(q + HALO, inner), bf16, True),
                (part(STATE, inner), bf16, False),
                (part(8, inner), f32, False),
            ],
            shared=(rows, spread),
            into=None if g == 0 else bulk,
        )
        bulk = list(out[:3])
        order.leave(out[3])
        chains.append(Chain(out[3], decs[g], True))
        chains[-1].send(order)
        gate_rows.append(out[4])
    hidden, d_y, d_z = bulk

    def hop(i):
        if i < len(chains):
            chains[i].send(order)

    def back_local(g):
        o = g * per
        out = call(
            functools.partial(local_back_kernel, hops=n_ctx - 1, inner=inner),
            0,
            per,
            [(act, o), (xdt, o), (dtl, o), (start, o), (start_row, o), (d_y, o)]
            + [(v, 0) for v in states[g].entering],
            deps=order.deps(),
            outs=[(part(q, inner), f32, False), (part(q, 2 * STATE), f32, False)],
            shared=(spread,),
        )
        order.leave(out[1])
        return out

    nx2 = nx.reshape(seqs * (q + HALO), width)
    steps = tuple(range(1, n_ctx + 1))
    grad = order.leave(dot(nx2, order.enter(d_z).reshape(seqs * (q + HALO), inner), TN).astype(bf16))
    rest_z = Spread(grad, [steps])
    hop(0)
    hop(1)
    grad = order.leave(
        dot(cotangent.reshape(n_tok, width), order.enter(hidden).reshape(n_tok, inner), TN).astype(bf16)
    )
    rest_o = Spread(grad, [steps])
    back = [back_local(0)]
    hop(0)
    hop(1)
    back += [back_local(g) for g in range(1, chunks)]
    for _ in range(3, n_ctx):
        hop(0)
        hop(1)
    z_part = order.leave(dot(order.enter(d_z).reshape(seqs * (q + HALO), inner), w_rest[:, :inner], NT).astype(bf16))
    z_part = z_part.reshape(seqs, q + HALO, width)
    own = lax.dynamic_slice_in_dim(tokens, tp_rank * cols, cols, 2).astype(f32)

    bulk = [None]
    tap_rows, head_rows = [], []
    for g in range(chunks):
        have = 0 if g == 0 else 1
        o = g * per
        chains[g].land(order)
        out = call(
            functools.partial(conv_back_kernel, hops=n_ctx - 1, inner=inner, conv=conv),
            o,
            per,
            [(act, o), (xdt, o), (dtl, o), (start, o), (d_y, o), (y_scan, o), (back[g][0], 0), (back[g][1], 0), (pre, o), (u, o), (decs[g], 0)]
            + [(v, 0) for v in states[g].entering + chains[g].entering],
            deps=order.deps(),
            outs=[
                (shape(q + HALO, conv + LANES), bf16, True),
                (part(8, conv), f32, False),
                (part(8, LANES), f32, False),
            ],
            shared=(taps, rows, head_par, spread, gather, tri),
            scratch=[pltpu.VMEM((q, conv), f32)],
            into=None if g == 0 else bulk,
        )
        bulk = list(out[:1])
        tap_rows.append(out[1])
        head_rows.append(out[2])
        order.leave(out[2])
        if g == 0:
            ring = Ring([rest_z, rest_o], order)
    du = bulk[0]
    rim = shift(du[:, :HALO, :], "ctx", -1)

    grad = order.leave(dot(nx2, du.reshape(seqs * (q + HALO), conv + LANES), TN).astype(bf16))
    spread_in = Spread(grad, [steps[:1], steps[1:]])
    ring.step(order)

    in_gain_own = lax.dynamic_slice_in_dim(in_gain, tp_rank * cols, cols, 0).astype(f32)
    order.land(rim)
    near, away, gain_part = call_slices(
        norm_back_kernel,
        rank,
        tp_count,
        [(du, False), (rim, False), (nx, True), (z_part, True)],
        [(w_in, 0, conv + LANES)],
        deps=order.deps(),
        outs=[
            (shape(q + HALO, width // 2), f32, False),
            (shape(q + HALO, width // 2), bf16, False),
            ((8, width), f32, None),
        ],
        scratch=[pltpu.VMEM((n_tok, conv + LANES), bf16), pltpu.VMEM((n_tok, LANES), f32)],
    )
    order.leave(gain_part)
    cube = Cube(near, away)
    tp_part, own_part = pack(tap_rows, head_rows, gate_rows, gain_part, order, inner, conv)
    tp_hops = Hops(tp_part, ["tp"])
    tp_hops.go(order)

    ring_in = Ring([spread_in], order)
    ring.step(order)
    tp_hops.go(order)
    near, away = call_slices(
        mix_kernel,
        rank,
        tp_count,
        [(hidden, False)],
        deps=order.deps(),
        weights=[(w_rest, inner, inner)],
        outs=[(shape(q, width // 2), f32, True), (shape(q, width // 2), bf16, True)],
    )
    order.leave(near)
    cube_mix = Cube(near, away)
    cube.halve(order)
    small = Hops(jnp.concatenate([tp_hops.end(order), own_part], 1), ["fsdp", "ctx"])
    small.go(order)
    ring_in.step(order)
    cube_mix.halve(order)
    small.go(order)
    while not ring_in.done():
        ring_in.step(order)
        ring.step(order)
        small.go(order)
    grad_rest, grad_in = ring.total, ring_in.total
    grad_wz, grad_wo = grad_rest[:, :inner], grad_rest[:, inner:]
    grad_x = grad_in[:, :inner]
    bc_hops = Hops(grad_in[:, inner:conv], ["tp"])
    bc_hops.go(order)
    small = small.end(order)
    grad_bc = bc_hops.end(order)
    grad_dt = grad_in[:, conv : conv + heads]
    d_normed = cube.total()
    mixed = (own + cube_mix.total()).astype(bf16)

    conv_all = small[: CONV + 1, : 2 * STATE]
    gain_row = lax.dynamic_slice_in_dim(small[0, 2 * STATE :], tp_rank * cols, cols, 0) / in_gain_own
    small = small[:, 2 * STATE + width :]
    conv_own = small[: CONV + 1, :inner]
    head_own = small[:, inner : inner + LANES]
    gate_own = small[:, inner + LANES :]

    hat = own * inv_rms
    full_dot = d_normed[:, q, :q][:, :, None]
    own_cot = lax.dynamic_slice_in_dim(cotangent, tp_rank * cols, cols, 2).astype(f32)
    grad_tokens = own_cot + inv_rms * (d_normed[:, :q] * in_gain_own - hat * (full_dot / D))

    return (
        mixed,
        grad_tokens,
        gain_row,
        jnp.stack([grad_wz, grad_x], axis=1),
        grad_bc,
        grad_dt,
        head_own[0, :heads],
        head_own[1, :heads],
        gate_own[1].reshape(heads, HEADDIM).sum(1),
        conv_own[:CONV],
        conv_own[CONV],
        conv_all[:CONV],
        conv_all[CONV],
        gate_own[0],
        grad_wo.T,
    )


def solution(mesh):
    return jax.shard_map(
        per_device,
        mesh=mesh,
        in_specs=(
            P("fsdp", "ctx", None),
            P("fsdp", "ctx"),
            P(),
            P(("fsdp", "ctx"), None, "tp"),
            P(("fsdp", "ctx"), None),
            P(("fsdp", "ctx"), "tp"),
            P("tp"),
            P("tp"),
            P("tp"),
            P(None, "tp"),
            P("tp"),
            P(),
            P(),
            P("tp"),
            P("tp", ("fsdp", "ctx")),
            P("fsdp", "ctx", None),
        ),
        out_specs=(
            P("fsdp", "ctx", "tp"),
            P("fsdp", "ctx", "tp"),
            P("tp"),
            P(("fsdp", "ctx"), None, "tp"),
            P(("fsdp", "ctx"), None),
            P(("fsdp", "ctx"), "tp"),
            P("tp"),
            P("tp"),
            P("tp"),
            P(None, "tp"),
            P("tp"),
            P(),
            P(),
            P("tp"),
            P("tp", ("fsdp", "ctx")),
        ),
        check_vma=False,
    )
```

```python
import functools

import jax
import jax.numpy as jnp
from jax import lax
from jax.experimental import pallas as pl
from jax.experimental.pallas import tpu as pltpu
from jax.sharding import PartitionSpec as P

D = 1536
HEADDIM = 64
STATE = 128
CONV = 4
INNER = 3072
NORM_EPS = 1e-05
LANES = 128
HALO = 16
COST = pl.CostEstimate(flops=2 * 10**12, bytes_accessed=8 * 10**9, transcendentals=0)

bf16 = jnp.bfloat16
f32 = jnp.float32
NN = (((1,), (0,)), ((), ()))
NT = (((1,), (1,)), ((), ()))
TN = (((0,), (0,)), ((), ()))


def rotate(v, axis, steps):
    n = lax.axis_size(axis)
    return lax.ppermute(v, axis, [(i, (i + steps) % n) for i in range(n)])


def shift(v, axis, steps):
    n = lax.axis_size(axis)
    return lax.ppermute(v, axis, [(i, i + steps) for i in range(n) if 0 <= i + steps < n])


def flip(v, axis, mask):
    n = lax.axis_size(axis)
    return lax.ppermute(v, axis, [(i, i ^ mask) for i in range(n)])


def cube_sum(v, axis):
    mask = 1
    while mask < lax.axis_size(axis):
        v = v + flip(v, axis, mask)
        mask *= 2
    return v


def after(v, *deps):
    return lax.optimization_barrier((v,) + deps)[0]


def ring_pieces(v):
    out = [v]
    for _ in range(1, lax.axis_size("ctx")):
        out.append(rotate(out[-1], "ctx", 1))
    return out


def all_pieces(ring, *start):
    nc, nf = lax.axis_size("ctx"), lax.axis_size("fsdp")
    c, f = lax.axis_index("ctx"), lax.axis_index("fsdp")
    pieces, places = [], []
    for step, piece in enumerate(ring):
        owner = lax.rem(c - step + nc, nc)
        if start:
            piece = after(piece, *start)
        for j in range(nf):
            if j:
                piece = rotate(piece, "fsdp", 1)
            pieces.append(piece)
            places.append(lax.rem(f - j + nf, nf) * nc + owner)
    return pieces, jnp.stack(places).astype(jnp.int32)


def assemble(pieces, places):
    rows = pieces[0].shape[0]
    whole = jnp.zeros((rows * len(pieces), pieces[0].shape[1]), pieces[0].dtype)
    for i, piece in enumerate(pieces):
        whole = lax.dynamic_update_slice_in_dim(whole, piece, places[i] * rows, 0)
    return whole


class Spread:
    def __init__(self, g, runs):
        nc, nf = lax.axis_size("ctx"), lax.axis_size("fsdp")
        c, f = lax.axis_index("ctx"), lax.axis_index("fsdp")
        self.g, self.rows, self.runs = g, g.shape[0] // (nc * nf), runs
        self.place = lambda k, step: lax.rem(f + k, nf) * nc + lax.rem(c - step + nc, nc)
        self.come = []
        for run in runs:
            self.send(g, run)

    def more(self, run, order):
        waits = list(order.waits)
        self.send(order.enter(self.g), run)
        order.waits = waits

    def send(self, g, run):
        nc, nf, f = lax.axis_size("ctx"), lax.axis_size("fsdp"), lax.axis_index("fsdp")
        take = lambda at, count: lax.dynamic_slice_in_dim(g, at * self.rows, count * self.rows, 0)
        for k in range(1, nf):
            if len(run) == nc:
                sent = take(lax.rem(f + k, nf) * nc, nc)
            else:
                sent = jnp.concatenate([take(self.place(k, step), 1) for step in run])
            self.sent = sent
            self.come.append((run, rotate(sent, "fsdp", k)))

    def landed(self, step):
        return [v for run, v in self.come if step in run]

    def terms(self, step):
        nc, c = lax.axis_size("ctx"), lax.axis_index("ctx")
        out = [(self.g, self.place(0, step))]
        for run, v in self.come:
            if step in run:
                out.append((v, lax.rem(c - step + nc, nc) if len(run) == nc else run.index(step)))
        return out


def block_sum(groups, last, rows, dtype, order, apart=False):
    arrays = [a for group in groups for a, _ in group]
    places = jnp.stack([jnp.asarray(at, jnp.int32) for group in groups for _, at in group])
    widths = [group[0][0].shape[1] for group in groups]
    specs = [pl.BlockSpec((rows, a.shape[1]), lambda i, p, j=j: (p[j], 0)) for j, a in enumerate(arrays)]
    if last is not None:
        arrays.append(last)
        specs.append(pl.BlockSpec(last.shape, lambda i, p: (0, 0)))
        order.land(last)
    deps = order.deps()
    outs = widths if apart else [sum(widths)]

    def kernel(places_ref, *refs):
        at, lo = 0, 0
        for i, (group, width) in enumerate(zip(groups, widths)):
            total = sum(r[...].astype(f32) for r in refs[at : at + len(group)])
            if last is not None:
                total = total + refs[len(arrays) - 1][:, lo : lo + width].astype(f32)
            if apart:
                refs[i - len(groups)][...] = total.astype(dtype)
            else:
                refs[-1][:, lo : lo + width] = total.astype(dtype)
            at, lo = at + len(group), lo + width

    out = pl.pallas_call(
        kernel,
        grid_spec=pltpu.PrefetchScalarGridSpec(
            num_scalar_prefetch=1,
            grid=(1,),
            in_specs=specs + [pl.BlockSpec(memory_space=pl.ANY)] * len(deps),
            out_specs=[pl.BlockSpec((rows, w), lambda i, p: (0, 0)) for w in outs],
        ),
        out_shape=[jax.ShapeDtypeStruct((rows, w), dtype) for w in outs],
        compiler_params=pltpu.CompilerParams(vmem_limit_bytes=16 * 2**20),
        cost_estimate=COST,
    )(places, *arrays, *deps)
    order.leave(out[0])
    return out if apart else out[0]


def finish(ring, rest, shapes, order):
    ring.at += 1
    terms = [t for one in ring.spreads for t in one.terms(ring.at)]
    rows = ring.spreads[0].rows
    order.land(ring.come)
    deps = order.deps()
    places = jnp.stack([jnp.asarray(at, jnp.int32) for _, at in terms])
    specs = [pl.BlockSpec((rows, a.shape[1]), lambda i, p, j=j: (p[j], 0)) for j, (a, _) in enumerate(terms)]
    whole = lambda shape: pl.BlockSpec(shape, lambda i, p, n=len(shape): (0,) * n)

    def kernel(*refs):
        n = 3 + len(terms)
        finish_kernel(*refs[:n], *refs[n + len(deps) :], terms=len(terms))

    return pl.pallas_call(
        kernel,
        grid_spec=pltpu.PrefetchScalarGridSpec(
            num_scalar_prefetch=1,
            grid=(1,),
            in_specs=specs
            + [whole(ring.come.shape), whole(rest.shape)]
            + [pl.BlockSpec(memory_space=pl.ANY)] * len(deps),
            out_specs=[whole(s) for s in shapes],
        ),
        out_shape=[jax.ShapeDtypeStruct(s, f32) for s in shapes],
        compiler_params=pltpu.CompilerParams(vmem_limit_bytes=16 * 2**20),
        cost_estimate=COST,
    )(places, *[a for a, _ in terms], ring.come, rest, *deps)


class Ring:
    def __init__(self, spreads, order):
        self.spreads, self.at = spreads, 0
        self.total, self.come = None, None
        self.step(order)

    def done(self):
        return self.at == lax.axis_size("ctx")

    def step(self, order):
        if self.done():
            return
        self.at += 1
        groups = [one.terms(self.at) for one in self.spreads]
        last = lax.axis_size("ctx") == self.at
        self.total = block_sum(groups, self.come, self.spreads[0].rows, f32 if last else bf16, order, last)
        if not last:
            self.come = rotate(self.total, "ctx", 1)


def halve_kernel(near, come, near_ref, away_ref):
    total = near[...].astype(f32) + come[...].astype(f32)
    near_ref[...] = total[:, : near_ref.shape[1]]
    away_ref[...] = total[:, near_ref.shape[1] :].astype(bf16)


def add_kernel(a, b, out_ref):
    out_ref[...] = a[...] + b[...]


def add_both_kernel(a, b, come, a_ref, b_ref):
    wide = a_ref.shape[1]
    a_ref[...] = a[...] + come[:, :wide]
    b_ref[...] = b[...] + come[:, wide:]


class Cube:
    def __init__(self, near, away):
        self.near, self.away, self.mask = near, away, 1
        self.come = flip(away, "tp", 1)

    def halve(self, order):
        seqs, rows, wide = self.near.shape
        while self.mask * 2 < lax.axis_size("tp"):
            wide //= 2
            order.land(self.come)
            out = (seqs, rows, wide)
            self.near, self.away = call(
                halve_kernel,
                0,
                seqs,
                [(self.near, 0), (self.come, 0)],
                [(out, f32, True), (out, bf16, True)],
                deps=order.deps(),
            vmem=16,
            )
            order.leave(self.away)
            self.mask *= 2
            self.come = flip(self.away, "tp", self.mask)

    def total(self):
        return self.near + self.come.astype(f32)


class Hops:
    def __init__(self, v, own, axes=("tp", "fsdp", "ctx")):
        self.v, self.own = v, own
        hops = {axis: [(axis, 1 << i) for i in range(lax.axis_size(axis).bit_length() - 1)] for axis in axes}
        self.todo = hops["tp"][:1] + hops.get("fsdp", []) + hops.get("ctx", []) + hops["tp"][1:]
        self.come, self.both = None, False

    def go(self, order):
        if self.come is not None:
            order.land(self.come)
            if self.both:
                self.v, self.own = small_call(
                    add_both_kernel, [self.v, self.own, self.come], [(self.v.shape, f32), (self.own.shape, f32)], order
                )
            else:
                self.v = small_call(add_kernel, [self.v, self.come], [(self.v.shape, f32)], order)[0]
            order.leave(self.v)
            self.come = None
        if self.todo:
            axis, mask = self.todo.pop(0)
            self.both = axis != "tp" and self.own is not None
            self.come = flip(jnp.concatenate([self.v, self.own], 1) if self.both else self.v, axis, mask)

    def end(self, order):
        while self.come is not None:
            self.go(order)
        return self.v


def small_call(kernel, operands, outs, order, scalar=None, scratch=()):
    deps = order.deps()
    n_in = len(operands) + (scalar is not None)

    def run(*refs):
        kernel(*refs[:n_in], *refs[n_in + len(deps) :])

    vmem = pl.BlockSpec(memory_space=pltpu.VMEM)
    return pl.pallas_call(
        run,
        in_specs=([] if scalar is None else [pl.BlockSpec(memory_space=pltpu.SMEM)])
        + [vmem] * len(operands)
        + [pl.BlockSpec(memory_space=pl.ANY)] * len(deps),
        out_specs=[vmem] * len(outs),
        out_shape=[jax.ShapeDtypeStruct(*o) for o in outs],
        scratch_shapes=list(scratch),
        compiler_params=pltpu.CompilerParams(vmem_limit_bytes=16 * 2**20),
        cost_estimate=COST,
    )(*([] if scalar is None else [scalar]), *operands, *deps)


class Chain:
    def __init__(self, parts, decay, reverse):
        self.parts, self.decay, self.reverse = parts, decay, reverse
        self.hop, self.last, self.entering = 0, None, []

    def send(self, order):
        n = lax.axis_size("ctx")
        self.hop += 1
        if self.hop >= n:
            return
        out = self.parts
        if self.last is not None:
            order.land(self.last)
            out = small_call(
                combine_kernel, [self.parts, self.decay, self.last], [(out.shape, bf16)], order
            )[0]
            order.leave(out)
        hop = self.hop
        pair = (n - hop, n - hop - 1) if self.reverse else (hop - 1, hop)
        self.last = lax.ppermute(out, "ctx", [pair])
        self.entering.append(self.last)

    def land(self, order):
        order.land(self.last)


class Order:
    def __init__(self):
        self.waits = []

    def land(self, *arrays):
        self.waits += arrays

    def enter(self, v):
        v = after(v, *self.waits)
        self.waits = []
        return v

    def deps(self):
        waits, self.waits = self.waits, []
        return waits

    def leave(self, v):
        self.waits = self.waits + [v]
        return v


def dot(a, b, dims=NN):
    return lax.dot_general(a, b, dims, preferred_element_type=f32)


def split(v, terms):
    out = []
    for i in range(terms):
        t = v.astype(bf16)
        out.append(t)
        if i + 1 < terms:
            v = v - t.astype(f32)
    return out


def constants(inner, q):
    heads = jnp.arange(LANES, dtype=jnp.int32)[:, None] == jnp.arange(inner, dtype=jnp.int32)[None] // HEADDIM
    spread = heads.astype(bf16)
    tri = jnp.arange(q, dtype=jnp.int32)[None] <= jnp.arange(q, dtype=jnp.int32)[:, None]
    return jnp.concatenate([spread, spread]), spread.T, tri.astype(bf16)


def widen(v, spread):
    return dot(jnp.concatenate(split(v, 2), 1), spread[...])


def narrow(v, gather, terms):
    out = None
    for t in split(v, terms):
        s = dot(t, gather[...])
        out = s if out is None else out + s
    return out


def tri_sum(tri, v, dims=NN):
    out = None
    for t in split(v, 3):
        s = dot(tri[...], t, dims)
        out = s if out is None else out + s
    return out


def one_of(refs):
    total = refs[0][...]
    for r in refs[1:]:
        total = total + r[...]
    return total


def halves(v):
    lane = lax.broadcasted_iota(jnp.int32, v.shape, 1)
    zero = jnp.zeros_like(v)
    return jnp.where(lane < HEADDIM, v, zero), jnp.where(lane >= HEADDIM, v, zero)


def sigmoid(v):
    return lax.logistic(v)


def gather_rows(places, pieces, whole):
    rows = pieces[0].shape[0]
    for i, piece in enumerate(pieces):
        whole[pl.ds(pl.multiple_of(places[i] * rows, 16), rows), :] = piece[...]


def project_kernel(nx, start, w, taps, bias, head_par, spread, tri, *refs, inner, conv):
    u_ref, pre_ref, act_ref, xdt_ref, dtl_ref, state_ref, dec_ref = refs[-7:]
    q = start.shape[0]
    u = dot(nx[...], w[...])
    u_ref[...] = u[:, :conv].astype(bf16)
    at = lax.broadcasted_iota(jnp.int32, (q, 1), 0)
    begin = start[...]
    since = at - begin
    for lo in range(0, conv, LANES):
        cols = slice(lo, lo + LANES)
        ut = u[:, cols]
        acc = bias[0:1, cols] + taps[CONV - 1 : CONV, cols] * ut[HALO:]
        for j in range(1, CONV):
            window = ut[HALO - j : HALO - j + q]
            acc = acc + taps[CONV - 1 - j : CONV - j, cols] * jnp.where(since >= j, window, 0.0)
        pre_ref[:, cols] = acc.astype(bf16)
        act_ref[:, cols] = (acc * sigmoid(acc)).astype(bf16)
    v = u[HALO:, conv:] + head_par[0:1, :]
    dt = jnp.maximum(v, 0.0) + jnp.log1p(jnp.exp(-jnp.abs(v)))
    cum = tri_sum(tri, -dt * jnp.exp(head_par[1:2, :]))
    dtl_ref[:, :LANES] = dt
    dtl_ref[:, LANES:] = cum
    end = cum[q - 1 : q, :]
    begin_last = begin[q - 1 : q, :]
    tail = jnp.where(begin == begin_last, jnp.exp(end - cum), 0.0)
    xh = act_ref[:, :inner].astype(f32)
    xdt = (xh * widen(dt, spread)).astype(bf16)
    xdt_ref[...] = xdt
    weighted = (xdt.astype(f32) * widen(tail, spread)).astype(bf16)
    b = act_ref[:, inner : inner + STATE]
    state_ref[...] = dot(b, weighted, TN).astype(bf16)
    total = jnp.where(begin_last < 0, jnp.exp(end), 0.0)
    dec_ref[...] = widen(jnp.broadcast_to(total, (8, LANES)), spread)[0:1]


def project_first_kernel(places, nx, start, taps, bias, head_par, spread, tri, *refs, pieces, inner, conv):
    w = refs[-1]

    @pl.when(pl.program_id(0) == 0)
    def _():
        gather_rows(places, refs[:pieces], w)

    project_kernel(nx, start, w, taps, bias, head_par, spread, tri, *refs[pieces:-1], inner=inner, conv=conv)


def combine_kernel(parts, decay, last, out_ref):
    out_ref[...] = (parts[...].astype(f32) + decay[...] * last[...].astype(f32)).astype(bf16)


def score_mask(begin_col, q):
    r = lax.broadcasted_iota(jnp.int32, (q, q), 0)
    c = lax.broadcasted_iota(jnp.int32, (q, q), 1)
    return (c <= r) & (c >= begin_col)


def score_mask_t(begin_row, q):
    r = lax.broadcasted_iota(jnp.int32, (q, q), 0)
    c = lax.broadcasted_iota(jnp.int32, (q, q), 1)
    return (r <= c) & (r >= begin_row)


def local_kernel(act, xdt, dtl, start, y_ref, *, inner):
    q = start.shape[0]
    b = act[:, inner : inner + STATE]
    c = act[:, inner + STATE : inner + 2 * STATE]
    scores = jnp.where(score_mask(start[...], q), dot(c, b, NT), 0.0)
    cum = dtl[:, LANES:]
    cum_t = cum.T
    for pair in range(inner // LANES):
        cols = slice(pair * LANES, (pair + 1) * LANES)
        weights = []
        for h in (2 * pair, 2 * pair + 1):
            gap = jnp.minimum(cum[:, h : h + 1] - cum_t[h : h + 1, :], 0.0)
            weights.append((jnp.exp(gap) * scores).astype(bf16))
        even, odd = halves(xdt[:, cols])
        y_ref[:, cols] = dot(weights[0], even) + dot(weights[1], odd)


def gate_sums_kernel(nx, cot, y_in, act, dtl, start, state, w, rows, spread, y_ref, z_ref, dh_ref, sums_ref, *, inner):
    q = start.shape[0]
    c = act[:, inner + STATE : inner + 2 * STATE]
    zz = dot(nx[HALO:], w[:, :inner])
    z_ref[...] = zz
    d_hidden = dot(cot[...], w[:, inner:])
    dh_ref[...] = d_hidden
    into = widen(jnp.where(start[...] < 0, jnp.exp(dtl[:, LANES:]), 0.0), spread)
    y = y_in[...] + into * dot(c, one_of(state))
    y_ref[...] = y
    gated = (y + rows[0:1, :] * act[:, :inner].astype(f32)) * (zz * sigmoid(zz))
    e = d_hidden * rows[1:2, :]
    ones = jnp.ones((8, inner), bf16)
    sq = dot(ones, (gated * gated).astype(bf16), NT)
    eg = dot(ones, (e * gated).astype(bf16), NT)
    row = lax.broadcasted_iota(jnp.int32, (8, q), 0)
    sums_ref[...] = jnp.where(row == 0, sq, eg)


def gate_sums_first_kernel(places, nx, cot, y_in, act, dtl, start, *refs, pieces, hops, inner):
    state, (rows, spread), refs = refs[:hops], refs[hops : hops + 2], refs[hops + 2 :]
    y_ref, z_ref, dh_ref, sums_ref, w = refs[pieces], refs[pieces + 1], refs[pieces + 2], refs[pieces + 3], refs[-1]

    @pl.when(pl.program_id(0) == 0)
    def _():
        gather_rows(places, refs[:pieces], w)

    gate_sums_kernel(
        nx, cot, y_in, act, dtl, start, state, w, rows, spread, y_ref, z_ref, dh_ref, sums_ref, inner=inner
    )


def gate_sums_next_kernel(nx, cot, y_in, act, dtl, start, *refs, hops, inner):
    gate_sums_kernel(nx, cot, y_in, act, dtl, start, refs[:hops], *refs[hops:], inner=inner)


def mix_kernel(rank, hidden, w, near_ref, away_ref):
    seqs, q, cols = near_ref.shape
    k = pl.program_id(0)
    out = dot(hidden[...].reshape(seqs * q, hidden.shape[2]), w[...], NT).astype(bf16).reshape(seqs, q, cols)

    @pl.when(lax.rem(k, 2) == 0)
    def _():
        near_ref[...] = out

    @pl.when(lax.rem(k, 2) == 1)
    def _():
        away_ref[...] = out


def out_back_kernel(rank, du, rim, nx, z_part, w_in, near_ref, away_ref, gain_ref, own, part):
    seqs, q = du.shape[0], du.shape[1] - HALO
    cols = w_in.shape[0]
    tp = near_ref.shape[2] * 2 // cols
    k = pl.program_id(0)

    @pl.when(k == 0)
    def _():
        for s in range(seqs):
            own[s * q : (s + 1) * q - 16, :] = du[s, HALO:q, :]
            edge = du[s, q : q + HALO, :].astype(f32)
            own[(s + 1) * q - 16 : (s + 1) * q, :] = (edge + rim[s].astype(f32)).astype(bf16)
        part[...] = jnp.zeros_like(part)

    out = dot(own[...], w_in[...], NT)
    gains = jnp.zeros((1, cols), f32)
    for s in range(seqs):
        mine = out[s * q : (s + 1) * q] + z_part[s, HALO:, :].astype(f32)
        prod = mine * nx[s, HALO:, :].astype(f32)
        folded = prod[:, :LANES]
        for lo in range(LANES, cols, LANES):
            folded = folded + prod[:, lo : lo + LANES]
        part[s * q : (s + 1) * q, :] += folded
        gains = gains + jnp.sum(prod, axis=0, keepdims=True)
        for j in range(tp):
            to = slice(j // 2 * cols, (j // 2 + 1) * cols)

            @pl.when(k == j)
            def _():
                (away_ref if j % 2 else near_ref)[s, :q, to] = mine.astype(bf16)

    gain_ref[...] = jnp.broadcast_to(gains, gain_ref.shape)

    @pl.when(k == tp - 1)
    def _():
        ones = jnp.ones((16, LANES), bf16)
        for s in range(seqs):
            total = None
            for t in split(part[s * q : (s + 1) * q, :], 2):
                one = dot(ones, t, NT)
                total = one if total is None else total + one
            total = jnp.concatenate([total, jnp.zeros((16, cols - q), f32)], 1)
            for j in range(tp):
                to = slice(j // 2 * cols, (j // 2 + 1) * cols)
                (away_ref if j % 2 else near_ref)[s, q:, to] = total.astype(bf16)


def pack_kernel(gain, *refs, chunks, inner, conv):
    taps, heads, gates = refs[:chunks], refs[chunks : 2 * chunks], refs[2 * chunks : 3 * chunks]
    tp_ref, own_ref = refs[-2:]
    total = lambda refs: sum(jnp.sum(r[...], axis=0) for r in refs)
    tap = total(taps)
    row = lax.broadcasted_iota(jnp.int32, gain.shape, 0)
    tp_ref[:, : 2 * STATE] = tap[:, inner:]
    tp_ref[:, 2 * STATE :] = jnp.where(row == 0, gain[...], 0.0)
    own_ref[:, :inner] = tap[:, :inner]
    own_ref[:, inner : inner + LANES] = total(heads)
    own_ref[:, inner + LANES :] = total(gates)


def unpack_kernel(
    rank, v, own, come, gain, gather, conv_ref, convb_ref, bc_ref, bcb_ref, dtb_ref, alog_ref, skip_ref, gate_ref, gain_ref
):
    inner, cols = gate_ref.shape[1], gain_ref.shape[1]
    heads = skip_ref.shape[1]
    bc = v[:, : 2 * STATE] + come[:, : 2 * STATE]
    bc_ref[...] = bc[:CONV]
    bcb_ref[...] = bc[CONV : CONV + 1]
    at = pl.multiple_of(2 * STATE + rank[0] * cols, LANES)
    gain_ref[...] = (v[0:1, pl.ds(at, cols)] + come[0:1, pl.ds(at, cols)]) / gain[0:1, :]
    taps = own[:, :inner]
    conv_ref[...] = taps[:CONV]
    convb_ref[...] = taps[CONV : CONV + 1]
    head = own[:, inner : inner + LANES]
    dtb_ref[...] = head[0:1, :heads]
    alog_ref[...] = head[1:2, :heads]
    gate = own[:, inner + LANES :]
    gate_ref[...] = gate[0:1]
    skip_ref[...] = narrow(gate, gather, 3)[1:2, :heads]


def tokens_kernel(near, come, own, cot, inv, gain, out_ref):
    q, cols = out_ref.shape
    total = near[...] + come[...].astype(f32)
    both = jnp.broadcast_to(total[q : q + 8, :q][0:1], (8, q)).T[:, 0:1]
    hat = own[...].astype(f32) * inv[...]
    out_ref[...] = cot[...].astype(f32) + inv[...] * (total[:q] * gain[0:1, :] - hat * (both / D))


def finish_kernel(places, *refs, terms):
    come, rest = refs[terms], refs[terms + 1]
    zx_ref, bc_ref, dt_ref = refs[-3:]
    inner, wide, heads = zx_ref.shape[2], bc_ref.shape[1], dt_ref.shape[1]
    total = sum(r[...].astype(f32) for r in refs[:terms]) + come[...].astype(f32)
    zx_ref[:, 0, :] = rest[...]
    zx_ref[:, 1, :] = total[:, :inner]
    bc_ref[...] = total[:, inner : inner + wide]
    dt_ref[...] = total[:, inner + wide : inner + wide + heads]


def norm_kernel(x, halo, gain, nx_ref, inv_ref):
    wide = x[...].astype(f32)
    width = wide.shape[1]
    inv = lax.rsqrt(jnp.mean(wide * wide, axis=-1, keepdims=True) + NORM_EPS)
    inv_ref[...] = inv
    nx_ref[HALO:, :] = (wide * inv * gain[0:1, :]).astype(bf16)
    edge = halo[...].astype(f32)
    inv = lax.rsqrt(jnp.mean(edge * edge, axis=-1, keepdims=True) + NORM_EPS)
    nx_ref[:HALO, :] = (edge * inv * gain[0:1, :]).astype(bf16)


def gate_kernel(y_in, act, dtl, start, z, dh, sums, rows, spread, *refs, inner):
    hidden_ref, dz_ref, dy_ref, dstate_ref, grads_ref = refs[-5:]
    xh = act[:, :inner].astype(f32)
    y = y_in[...] + rows[0:1, :] * xh
    zz = z[...].astype(f32)
    sig = sigmoid(zz)
    silu = zz * sig
    gated = y * silu
    gain = rows[1:2, :]
    d_hidden = dh[...].astype(f32)
    sums_t = sums[...].T
    inv = lax.rsqrt(sums_t[:, 0:1] / INNER + NORM_EPS)
    back = sums_t[:, 1:2] * (inv * inv * inv) / INNER
    scaled = gated * inv
    hidden_ref[...] = (scaled * gain).astype(bf16)
    dg = inv * (d_hidden * gain) - gated * back
    dy = (dg * silu).astype(bf16)
    dy_ref[...] = dy
    dz_ref[:HALO, :] = jnp.zeros((HALO, inner), bf16)
    dz_ref[HALO:, :] = (dg * y * sig * (1.0 + zz * (1.0 - sig))).astype(bf16)
    gate_row = jnp.sum(d_hidden * scaled, axis=0, keepdims=True)
    dy_wide = dy.astype(f32)
    skip_row = jnp.sum(dy_wide * xh, axis=0, keepdims=True)
    row = lax.broadcasted_iota(jnp.int32, (8, inner), 0)
    grads_ref[...] = jnp.where(row == 0, gate_row, jnp.where(row == 1, skip_row, 0.0))
    into = widen(jnp.where(start[...] < 0, jnp.exp(dtl[:, LANES:]), 0.0), spread)
    c = act[:, inner + STATE : inner + 2 * STATE]
    dstate_ref[...] = dot(c, (into * dy_wide).astype(bf16), TN).astype(bf16)


def local_back_kernel(act, xdt, dtl, start, start_row, dy, *refs, hops, inner):
    state, (spread, dx_ref, dbc_ref) = refs[:hops], refs[hops:]
    q = start.shape[0]
    b = act[:, inner : inner + STATE]
    c = act[:, inner + STATE : inner + 2 * STATE]
    mask = score_mask_t(start_row[...], q)
    scores = jnp.where(mask, dot(b, c, NT), 0.0)
    cum = dtl[:, LANES:]
    cum_t = cum.T
    total = jnp.zeros((q, q), f32)
    for pair in range(inner // LANES):
        cols = slice(pair * LANES, (pair + 1) * LANES)
        dy_pair = dy[:, cols]
        x_even, x_odd = halves(xdt[:, cols])
        dy_even, dy_odd = halves(dy_pair)
        out = None
        for h, x_one, dy_one in ((2 * pair, x_even, dy_even), (2 * pair + 1, x_odd, dy_odd)):
            decay = jnp.exp(jnp.minimum(cum_t[h : h + 1, :] - cum[:, h : h + 1], 0.0))
            total = total + dot(x_one, dy_pair, NT) * decay
            term = dot((decay * scores).astype(bf16), dy_one)
            out = term if out is None else out + term
        dx_ref[:, cols] = out
    d_scores = jnp.where(mask, total, 0.0).astype(bf16)
    into = widen(jnp.where(start[...] < 0, jnp.exp(cum), 0.0), spread)
    weighted = (into * dy[...].astype(f32)).astype(bf16)
    dbc_ref[:, :STATE] = dot(d_scores, c)
    dbc_ref[:, STATE:] = dot(d_scores, b, TN) + dot(weighted, one_of(state), NT)


def conv_back_kernel(act, xdt, dtl, start, dy, y_in, dx, dbc, pre, u, dec, *refs, hops, inner, conv):
    state, later, refs = refs[:hops], refs[hops : 2 * hops], refs[2 * hops :]
    taps, rows, head_par, spread, gather, tri = refs[:6]
    du_ref, rim_ref, tap_ref, head_ref, dact = refs[-5:]
    q = start.shape[0]
    begin = start[...]
    b = act[:, inner : inner + STATE]
    dt, cum = dtl[:, :LANES], dtl[:, LANES:]
    end = cum[q - 1 : q, :]
    begin_last = begin[q - 1 : q, :]
    tail = widen(jnp.where(begin == begin_last, jnp.exp(end - cum), 0.0), spread)
    x_dt = xdt[...].astype(f32)
    d_y = dy[...].astype(f32)
    g = one_of(later)
    dx_tail = tail * dot(b, g)
    dact[:, inner : inner + STATE] = dbc[:, :STATE] + dot((x_dt * tail).astype(bf16), g, NT)
    dact[:, inner + STATE :] = dbc[:, STATE:]
    dx_local = dx[...]
    dx_all = dx_local + dx_tail
    dact[:, :inner] = dx_all * widen(dt, spread) + rows[0:1, :] * d_y
    flux_near = narrow(d_y * y_in[...] - x_dt * dx_local, gather, 3)
    flux_tail = narrow(x_dt * dx_tail, gather, 2)
    d_dt = narrow(dx_all * act[:, :inner].astype(f32), gather, 2)
    through = jnp.sum(dec[...] * (g.astype(f32) * one_of(state).astype(f32)), axis=0, keepdims=True)
    through = narrow(jnp.broadcast_to(through, (8, inner)), gather, 2)[0:1]
    d_log = tri_sum(tri, flux_near, TN) + (tri_sum(tri, flux_tail) - flux_tail) + through
    rate = jnp.exp(head_par[1:2, :])
    d_raw = (d_dt - rate * d_log) * (1.0 - jnp.exp(-dt))
    du_ref[:HALO, conv:] = jnp.zeros((HALO, LANES), bf16)
    rim_ref[:, conv:] = jnp.zeros((HALO, LANES), bf16)
    du_ref[HALO:, conv:] = d_raw.astype(bf16)
    bias_row = jnp.sum(d_raw, axis=0, keepdims=True)
    log_row = -jnp.sum(d_log * dt * rate, axis=0, keepdims=True)
    row = lax.broadcasted_iota(jnp.int32, (8, LANES), 0)
    head_ref[...] = jnp.where(row == 0, bias_row, jnp.where(row == 1, log_row, 0.0))
    since = lax.broadcasted_iota(jnp.int32, (q, 1), 0) - begin
    for lo in range(0, conv, LANES):
        cols = slice(lo, lo + LANES)
        p = pre[:, cols].astype(f32)
        sig = sigmoid(p)
        dp = dact[:, cols] * (sig * (1.0 + p * (1.0 - sig)))
        ut = u[:, cols].astype(f32)
        zeros = jnp.zeros((HALO, LANES), f32)
        total = jnp.concatenate([zeros, taps[CONV - 1 : CONV, cols] * dp], 0)
        tap_rows = [jnp.sum(dp * ut[HALO:], axis=0, keepdims=True)]
        for j in range(1, CONV):
            masked = jnp.where(since >= j, dp, 0.0)
            tap_rows.append(jnp.sum(masked * ut[HALO - j : HALO - j + q], axis=0, keepdims=True))
            moved = jnp.concatenate([zeros, taps[CONV - 1 - j : CONV - j, cols] * masked, zeros], 0)
            total = total + moved[j : j + q + HALO]
        du_ref[:, cols] = total.astype(bf16)
        rim_ref[:, cols] = total[:HALO].astype(bf16)
        out = jnp.sum(dp, axis=0, keepdims=True)
        for j in range(CONV):
            out = jnp.where(row == CONV - 1 - j, tap_rows[j], jnp.where(row == CONV, out, 0.0) if j == 0 else out)
        tap_ref[:, cols] = out


def call(kernel, first, count, ins, outs, shared=(), scalar=None, scratch=(), into=None, deps=(), vmem=34):
    def spec(shape, base):
        block = (None,) + tuple(shape[1:])
        rest = (0,) * (len(shape) - 1)
        return pl.BlockSpec(block, lambda s: (s + base,) + rest)

    in_specs = [spec(a.shape, o) for a, o in ins]
    in_specs += [
        pl.BlockSpec(a.shape, lambda s, n=a.ndim: (0,) * n, pipeline_mode=pl.Buffered(1)) for a in shared
    ]
    operands = [a for a, _ in ins] + list(shared)
    if scalar is not None:
        in_specs.insert(0, pl.BlockSpec(memory_space=pltpu.SMEM))
        operands.insert(0, scalar)
    n_args = len(operands)
    operands += list(deps)
    in_specs += [pl.BlockSpec(memory_space=pl.ANY)] * len(deps)
    aliases = {}
    if into is not None:
        for i, buf in enumerate(into):
            if buf is not None:
                aliases[len(operands)] = i
                operands.append(buf)
                in_specs.append(pl.BlockSpec(memory_space=pl.ANY))
    n_in = len(operands)

    def run(*refs):
        kernel(*refs[:n_args], *refs[n_in:])

    return pl.pallas_call(
        run,
        grid=(count,),
        in_specs=in_specs,
        out_specs=[spec(s, first if whole else 0) if whole is not None else pl.BlockSpec(s, lambda i, n=len(s): (0,) * n) for s, _, whole in outs],
        out_shape=[jax.ShapeDtypeStruct(s, d) for s, d, _ in outs],
        scratch_shapes=list(scratch),
        input_output_aliases=aliases,
        compiler_params=pltpu.CompilerParams(vmem_limit_bytes=vmem * 2**20),
        cost_estimate=COST,
    )(*operands)


def call_slices(kernel, rank, tp, wholes, weights, outs, scratch=(), deps=()):
    specs, operands = [], []
    for a, cut in wholes:
        if cut:
            block = a.shape[:-1] + (a.shape[-1] // tp,)
            specs.append(pl.BlockSpec(block, lambda k, r, n=a.ndim: (0,) * (n - 1) + (r[0] ^ k,)))
        else:
            specs.append(pl.BlockSpec(a.shape, lambda k, r, n=a.ndim: (0,) * n))
        operands.append(a)
    for a, at, cols in weights:
        specs.append(pl.BlockSpec((a.shape[0] // tp, cols), lambda k, r, j=at // cols: (r[0] ^ k, j)))
        operands.append(a)
    n_args = len(operands) + 1
    operands += list(deps)
    specs += [pl.BlockSpec(memory_space=pl.ANY)] * len(deps)
    n_in = len(operands) + 1

    def run(*refs):
        kernel(*refs[:n_args], *refs[n_in:])

    out_specs = []
    for shape, _, cut in outs:
        n = len(shape)
        if cut is None:
            out_specs.append(pl.BlockSpec((shape[0], shape[1] // tp), lambda k, r: (0, r[0] ^ k)))
        elif cut:
            out_specs.append(
                pl.BlockSpec(shape[:-1] + (shape[-1] * 2 // tp,), lambda k, r, n=n: (0,) * (n - 1) + (k // 2,))
            )
        else:
            out_specs.append(pl.BlockSpec(shape, lambda k, r, n=n: (0,) * n))
    return pl.pallas_call(
        run,
        grid_spec=pltpu.PrefetchScalarGridSpec(
            num_scalar_prefetch=1,
            grid=(tp,),
            in_specs=specs,
            out_specs=out_specs,
            scratch_shapes=list(scratch),
        ),
        out_shape=[jax.ShapeDtypeStruct(s, d) for s, d, _ in outs],
        compiler_params=pltpu.CompilerParams(vmem_limit_bytes=34 * 2**20),
        cost_estimate=COST,
    )(rank, *operands)


def pack(taps, heads, gates, gain, order, inner, conv):
    out = small_call(
        functools.partial(pack_kernel, chunks=len(taps), inner=inner, conv=conv),
        [gain, *taps, *heads, *gates],
        [((8, 2 * STATE + gain.shape[1]), f32), ((8, 2 * inner + LANES), f32)],
        order,
    )
    order.leave(out[0])
    return out


def per_device(
    tokens,
    segment_ids,
    in_gain,
    w_zx,
    w_bc,
    w_dt,
    dt_bias,
    a_log,
    skip_gain,
    conv_x,
    conv_x_bias,
    conv_bc,
    conv_bc_bias,
    gate_gain,
    w_out,
    cotangent,
):
    tp_count, tp_rank = lax.axis_size("tp"), lax.axis_index("tp")
    ctx_rank = lax.axis_index("ctx")
    seqs, q, width = tokens.shape
    inner = w_zx.shape[2]
    heads = w_dt.shape[1]
    conv = inner + 2 * STATE
    cols = width // tp_count
    n_tok = seqs * q
    chunks = 2 if seqs % 2 == 0 else 1
    per = seqs // chunks

    n_ctx = lax.axis_size("ctx")
    rank = tp_rank.astype(jnp.int32)[None]
    shape = lambda *s: (seqs,) + s
    part = lambda *s: (per,) + s
    order = Order()

    first_w = jnp.concatenate(
        [w_zx[:, 1, :], w_bc, jnp.pad(w_dt, ((0, 0), (0, LANES - heads)))], axis=1
    )
    ring_in = ring_pieces(first_w)
    halo = shift(jnp.pad(tokens[:, q - 8 :, :], ((0, 0), (8, 0), (0, 0))), "ctx", 1)
    pieces_in, places = all_pieces(ring_in)
    in_kernel = first_w.shape[0] % 16 == 0
    second_w = jnp.concatenate([w_zx[:, 0, :], w_out.T], axis=1)
    ring_rest = ring_pieces(after(second_w, ring_in[-1]))
    pieces_rest, _ = all_pieces(ring_rest, pieces_in[-1])
    spread, gather, tri = constants(inner, q)
    if not in_kernel:
        w_in, w_rest = assemble(pieces_in, places), assemble(pieces_rest, places)

    gain = jnp.broadcast_to(in_gain.astype(f32)[None], (8, width))
    bulk = None
    order.land(halo)
    for g in range(chunks):
        order.land(*ring_in[g + 1 : g + 2], *pieces_in[2 * g + 1 : 2 * g + 2])
        bulk = call(
            norm_kernel,
            g * per,
            per,
            [(tokens, g * per), (halo, g * per)],
            deps=order.deps(),
            vmem=16,
            outs=[(shape(q + HALO, width), bf16, True), (shape(q, 1), f32, True)],
            shared=(gain,),
            into=bulk,
        )
        order.leave(bulk[1])
    nx, inv_rms = bulk

    begin = segment_ids - ctx_rank * q
    start = begin[:, :, None]
    start_row = begin[:, None, :]
    taps = jnp.concatenate([conv_x, conv_bc], axis=1).astype(f32)
    bias = jnp.concatenate([conv_x_bias, conv_bc_bias]).astype(f32)[None]
    head_par = jnp.pad(jnp.stack([dt_bias, a_log]), ((0, 6), (0, LANES - heads)))
    rows = jnp.pad(jnp.stack([jnp.repeat(skip_gain, HEADDIM), gate_gain.astype(f32)]), ((0, 6), (0, 0)))

    states, decs, kept, y_local = [], [], [], []
    landing = lambda i: pieces_rest[min(i, len(pieces_rest) - 1)]
    for g in range(chunks):
        o = g * per
        order.land(ring_rest[min(g + 1, n_ctx - 1)])
        if g:
            order.land(landing(2 * g - 1))
        first = g == 0 and in_kernel
        given = [taps, bias, head_par, spread, tri]
        outs = [
            (part(q + HALO, conv), bf16, False),
            (part(q, conv), bf16, False),
            (part(q, conv), bf16, False),
            (part(q, inner), bf16, False),
            (part(q, 2 * LANES), f32, False),
            (part(STATE, inner), bf16, False),
            (part(1, inner), f32, False),
        ]
        if first:
            kernel = functools.partial(project_first_kernel, pieces=len(pieces_in), inner=inner, conv=conv)
        else:
            kernel = functools.partial(project_kernel, inner=inner, conv=conv)
        out = call(
            kernel,
            o,
            per,
            [(nx, o), (start, o)],
            outs + [((width, conv + LANES), bf16, None)] if first else outs,
            shared=given + pieces_in if first else [w_in] + given,
            scalar=places if first else None,
            deps=order.deps(),
            vmem=34,
        )
        if first:
            w_in = out[7]
        kept.append(out[:5])
        decs.append(order.leave(out[6]))
        states.append(Chain(out[5], out[6], False))
        states[-1].send(order)

    if n_ctx > 2:
        states[0].send(order)
    for g in range(chunks):
        u, pre, act, xdt, dtl = kept[g]
        if g == 0:
            order.land(ring_rest[min(chunks + 1, n_ctx - 1)], landing(2 * chunks - 1))
        y_local.append(
            order.leave(
                call(
                    functools.partial(local_kernel, inner=inner),
                    0,
                    per,
                    [(act, 0), (xdt, 0), (dtl, 0), (start, g * per)],
                    deps=order.deps(),
            vmem=16,
                    outs=[(part(q, inner), f32, False)],
                )[0]
            )
        )
    if n_ctx > 2:
        for one in states[1:]:
            one.send(order)
    for hop in range(3, n_ctx):
        for i, one in enumerate(states):
            if hop == 3:
                order.land(landing(2 * chunks + 1 + 2 * i))
            one.send(order)

    scans = []
    for g in range(chunks):
        o = g * per
        u, pre, act, xdt, dtl = kept[g]
        first = g == 0 and in_kernel
        hops = len(states[g].entering)
        outs = [
            (part(q, inner), f32, False),
            (part(q, inner), f32, False),
            (part(q, inner), f32, False),
            (part(8, q), f32, False),
        ]
        if first:
            kernel = functools.partial(gate_sums_first_kernel, pieces=len(pieces_rest), hops=hops, inner=inner)
            given = [rows, spread] + pieces_rest
            outs = outs + [((width, width), bf16, None)]
        else:
            kernel = functools.partial(gate_sums_next_kernel, hops=hops, inner=inner)
            given = [w_rest, rows, spread]
        out = call(
            kernel,
            o,
            per,
            [(nx, o), (cotangent, o), (y_local[g], 0), (act, 0), (dtl, 0), (start, o)]
            + [(v, 0) for v in states[g].entering],
            outs,
            shared=given,
            scalar=places if first else None,
            deps=order.deps(),
            vmem=34,
        )
        if first:
            w_rest = out[4]
        scans.append(out[:4])
        order.leave(out[3])
    sums = cube_sum(jnp.concatenate([one[3] for one in scans]), "tp")

    bulk = [None] * 2
    d_ys = []
    chains, gate_rows = [], []
    for g in range(chunks):
        o = g * per
        u, pre, act, xdt, dtl = kept[g]
        y_scan, z, d_hidden, _ = scans[g]
        out = call(
            functools.partial(gate_kernel, inner=inner),
            o,
            per,
            [(y_scan, 0), (act, 0), (dtl, 0), (start, o), (z, 0), (d_hidden, 0), (sums, o)],
            deps=order.deps(),
            vmem=34,
            outs=[
                (shape(q, inner), bf16, True),
                (shape(q + HALO, inner), bf16, True),
                (part(q, inner), bf16, False),
                (part(STATE, inner), bf16, False),
                (part(8, inner), f32, False),
            ],
            shared=(rows, spread),
            into=None if g == 0 else bulk,
        )
        bulk = list(out[:2])
        d_ys.append(out[2])
        order.leave(out[3])
        chains.append(Chain(out[3], decs[g], True))
        chains[-1].send(order)
        gate_rows.append(out[4])
    hidden, d_z = bulk

    def hop(i):
        if i < len(chains):
            chains[i].send(order)

    def back_local(g):
        o = g * per
        u, pre, act, xdt, dtl = kept[g]
        out = call(
            functools.partial(local_back_kernel, hops=n_ctx - 1, inner=inner),
            0,
            per,
            [(act, 0), (xdt, 0), (dtl, 0), (start, o), (start_row, o), (d_ys[g], 0)]
            + [(v, 0) for v in states[g].entering],
            deps=order.deps(),
            vmem=16,
            outs=[(part(q, inner), f32, False), (part(q, 2 * STATE), f32, False)],
            shared=(spread,),
        )
        order.leave(out[1])
        return out

    nx2 = nx.reshape(seqs * (q + HALO), width)
    steps = tuple(range(1, n_ctx + 1))
    grad = order.leave(dot(nx2, order.enter(d_z).reshape(seqs * (q + HALO), inner), TN).astype(bf16))
    rest_z = Spread(grad, [steps])
    hop(0)
    hop(1)
    grad = order.leave(
        dot(cotangent.reshape(n_tok, width), order.enter(hidden).reshape(n_tok, inner), TN).astype(bf16)
    )
    rest_o = Spread(grad, [steps])
    back = [back_local(0)]
    hop(0)
    hop(1)
    back += [back_local(g) for g in range(1, chunks)]
    for _ in range(3, n_ctx):
        hop(0)
        hop(1)
    z_part = order.leave(dot(order.enter(d_z).reshape(seqs * (q + HALO), inner), w_rest[:, :inner], NT).astype(bf16))
    z_part = z_part.reshape(seqs, q + HALO, width)
    own = lax.dynamic_slice_in_dim(tokens, tp_rank * cols, cols, 2)

    bulk = [None] * 2
    tap_rows, head_rows = [], []
    for g in range(chunks):
        have = 0 if g == 0 else 1
        o = g * per
        u, pre, act, xdt, dtl = kept[g]
        chains[g].land(order)
        out = call(
            functools.partial(conv_back_kernel, hops=n_ctx - 1, inner=inner, conv=conv),
            o,
            per,
            [(act, 0), (xdt, 0), (dtl, 0), (start, o), (d_ys[g], 0), (scans[g][0], 0), (back[g][0], 0), (back[g][1], 0), (pre, 0), (u, 0), (decs[g], 0)]
            + [(v, 0) for v in states[g].entering + chains[g].entering],
            deps=order.deps(),
            outs=[
                (shape(q + HALO, conv + LANES), bf16, True),
                (shape(HALO, conv + LANES), bf16, True),
                (part(8, conv), f32, False),
                (part(8, LANES), f32, False),
            ],
            shared=(taps, rows, head_par, spread, gather, tri),
            scratch=[pltpu.VMEM((q, conv), f32)],
            into=None if g == 0 else bulk,
        )
        bulk = list(out[:2])
        tap_rows.append(out[2])
        head_rows.append(out[3])
        order.leave(out[3])
        if g == 0:
            ring = Ring([rest_z, rest_o], order)
    du = bulk[0]
    rim = shift(bulk[1], "ctx", -1)

    grad = order.leave(dot(nx2, du.reshape(seqs * (q + HALO), conv + LANES), TN).astype(bf16))
    spread_in = Spread(grad, [steps[:1]])
    ring.step(order)
    spread_in.more(steps[1:], order)
    order.land(spread_in.sent)

    in_gain_own = lax.dynamic_slice_in_dim(in_gain, tp_rank * cols, cols, 0).astype(f32)
    order.land(rim)
    near, away, gain_part = call_slices(
        out_back_kernel,
        rank,
        tp_count,
        [(du, False), (rim, False), (nx, True), (z_part, True)],
        [(w_in, 0, conv + LANES)],
        deps=order.deps(),
        outs=[
            (shape(q + HALO, width // 2), bf16, False),
            (shape(q + HALO, width // 2), bf16, False),
            ((8, width), f32, None),
        ],
        scratch=[pltpu.VMEM((n_tok, conv + LANES), bf16), pltpu.VMEM((n_tok, LANES), f32)],
    )
    order.leave(gain_part)
    cube = Cube(near, away)

    ring_in = Ring([spread_in], order)
    ring.step(order)
    cube.halve(order)
    near, away = call_slices(
        mix_kernel,
        rank,
        tp_count,
        [(hidden, False)],
        deps=order.deps(),
        weights=[(w_rest, inner, inner)],
        outs=[(shape(q, width // 2), bf16, True), (shape(q, width // 2), bf16, True)],
    )
    order.leave(near)
    cube_mix = Cube(near, away)
    ring_in.step(order)
    while not ring.done():
        ring.step(order)
    grad_wz, grad_wo = ring.total
    cube_mix.halve(order)
    small = Hops(*pack(tap_rows, head_rows, gate_rows, gain_part, order, inner, conv))
    small.go(order)
    while ring_in.at < n_ctx - 1:
        ring_in.step(order)
    small.go(order)
    gain_row = jnp.broadcast_to(in_gain_own[None], (8, cols))
    own_cot = lax.dynamic_slice_in_dim(cotangent, tp_rank * cols, cols, 2)
    order.land(cube.come)
    (grad_tokens,) = call(
        tokens_kernel,
        0,
        seqs,
        [(cube.near, 0), (cube.come, 0), (own, 0), (own_cot, 0), (inv_rms, 0)],
        [(shape(q, cols), f32, True)],
        shared=(gain_row,),
        deps=order.deps(),
            vmem=16,
    )
    order.leave(grad_tokens)
    small.go(order)
    order.land(cube_mix.come)
    mixed = order.leave((order.enter(own).astype(f32) + cube_mix.total()).astype(bf16))
    small.go(order)
    rows_own = grad_wz.shape[0]
    grad_zx, grad_bc, grad_dt = finish(
        ring_in, grad_wz, [(rows_own, 2, inner), (rows_own, 2 * STATE), (rows_own, heads)], order
    )
    bc_hops = Hops(grad_bc, None, ["tp"])
    bc_hops.go(order)
    while small.todo:
        small.go(order)
    order.land(small.come)
    one = lambda n: ((1, n), f32)
    conv_own, convb_own, conv_all, convb_all, dtb, alog, skip, gate, gain_row = small_call(
        unpack_kernel,
        [small.v, small.own, small.come, gain_row, gather],
        [((CONV, inner), f32), one(inner), ((CONV, 2 * STATE), f32), one(2 * STATE), one(heads), one(heads), one(heads), one(inner), one(cols)],
        order,
        scalar=rank,
    )
    grad_bc = bc_hops.end(order)

    return (
        mixed,
        grad_tokens,
        gain_row[0],
        grad_zx,
        grad_bc,
        grad_dt,
        dtb[0],
        alog[0],
        skip[0],
        conv_own,
        convb_own[0],
        conv_all,
        convb_all[0],
        gate[0],
        grad_wo.T,
    )


def solution(mesh):
    return jax.shard_map(
        per_device,
        mesh=mesh,
        in_specs=(
            P("fsdp", "ctx", None),
            P("fsdp", "ctx"),
            P(),
            P(("fsdp", "ctx"), None, "tp"),
            P(("fsdp", "ctx"), None),
            P(("fsdp", "ctx"), "tp"),
            P("tp"),
            P("tp"),
            P("tp"),
            P(None, "tp"),
            P("tp"),
            P(),
            P(),
            P("tp"),
            P("tp", ("fsdp", "ctx")),
            P("fsdp", "ctx", None),
        ),
        out_specs=(
            P("fsdp", "ctx", "tp"),
            P("fsdp", "ctx", "tp"),
            P("tp"),
            P(("fsdp", "ctx"), None, "tp"),
            P(("fsdp", "ctx"), None),
            P(("fsdp", "ctx"), "tp"),
            P("tp"),
            P("tp"),
            P("tp"),
            P(None, "tp"),
            P("tp"),
            P(),
            P(),
            P("tp"),
            P("tp", ("fsdp", "ctx")),
        ),
        check_vma=False,
    )
```

```python
import functools

import jax
import jax.numpy as jnp
from jax import lax
from jax.experimental import pallas as pl
from jax.experimental.pallas import tpu as pltpu
from jax.sharding import PartitionSpec as P

D = 1536
HEADDIM = 64
STATE = 128
CONV = 4
INNER = 3072
NORM_EPS = 1e-05
LANES = 128
HALO = 16
COST = pl.CostEstimate(flops=2 * 10**12, bytes_accessed=8 * 10**9, transcendentals=0)

bf16 = jnp.bfloat16
f32 = jnp.float32
NN = (((1,), (0,)), ((), ()))
NT = (((1,), (1,)), ((), ()))
TN = (((0,), (0,)), ((), ()))


def rotate(v, axis, steps):
    n = lax.axis_size(axis)
    return lax.ppermute(v, axis, [(i, (i + steps) % n) for i in range(n)])


def shift(v, axis, steps):
    n = lax.axis_size(axis)
    return lax.ppermute(v, axis, [(i, i + steps) for i in range(n) if 0 <= i + steps < n])


def flip(v, axis, mask):
    n = lax.axis_size(axis)
    return lax.ppermute(v, axis, [(i, i ^ mask) for i in range(n)])


def cube_sum(v, axis):
    mask = 1
    while mask < lax.axis_size(axis):
        v = v + flip(v, axis, mask)
        mask *= 2
    return v


def after(v, *deps):
    return lax.optimization_barrier((v,) + deps)[0]


def ring_pieces(v):
    out = [v]
    for _ in range(1, lax.axis_size("ctx")):
        out.append(rotate(out[-1], "ctx", 1))
    return out


def all_pieces(ring, *start):
    nc, nf = lax.axis_size("ctx"), lax.axis_size("fsdp")
    c, f = lax.axis_index("ctx"), lax.axis_index("fsdp")
    pieces, places = [], []
    for step, piece in enumerate(ring):
        owner = lax.rem(c - step + nc, nc)
        if start:
            piece = after(piece, *start)
        for j in range(nf):
            if j:
                piece = rotate(piece, "fsdp", 1)
            pieces.append(piece)
            places.append(lax.rem(f - j + nf, nf) * nc + owner)
    return pieces, jnp.stack(places).astype(jnp.int32)


def assemble(pieces, places):
    rows = pieces[0].shape[0]
    whole = jnp.zeros((rows * len(pieces), pieces[0].shape[1]), pieces[0].dtype)
    for i, piece in enumerate(pieces):
        whole = lax.dynamic_update_slice_in_dim(whole, piece, places[i] * rows, 0)
    return whole


class Spread:
    def __init__(self, g, runs):
        nc, nf = lax.axis_size("ctx"), lax.axis_size("fsdp")
        c, f = lax.axis_index("ctx"), lax.axis_index("fsdp")
        self.g, self.rows, self.runs = g, g.shape[0] // (nc * nf), runs
        self.place = lambda k, step: lax.rem(f + k, nf) * nc + lax.rem(c - step + nc, nc)
        self.come = []
        for run in runs:
            self.send(g, run)

    def more(self, run, order):
        waits = list(order.waits)
        self.send(order.enter(self.g), run)
        order.waits = waits

    def send(self, g, run):
        nc, nf, f = lax.axis_size("ctx"), lax.axis_size("fsdp"), lax.axis_index("fsdp")
        take = lambda at, count: lax.dynamic_slice_in_dim(g, at * self.rows, count * self.rows, 0)
        for k in range(1, nf):
            if len(run) == nc:
                sent = take(lax.rem(f + k, nf) * nc, nc)
            else:
                sent = jnp.concatenate([take(self.place(k, step), 1) for step in run])
            self.sent = sent
            self.come.append((run, rotate(sent, "fsdp", k)))

    def landed(self, step):
        return [v for run, v in self.come if step in run]

    def terms(self, step):
        nc, c = lax.axis_size("ctx"), lax.axis_index("ctx")
        out = [(self.g, self.place(0, step))]
        for run, v in self.come:
            if step in run:
                out.append((v, lax.rem(c - step + nc, nc) if len(run) == nc else run.index(step)))
        return out


def block_sum(groups, last, rows, dtype, order, apart=False):
    arrays = [a for group in groups for a, _ in group]
    places = jnp.stack([jnp.asarray(at, jnp.int32) for group in groups for _, at in group])
    widths = [group[0][0].shape[1] for group in groups]
    specs = [pl.BlockSpec((rows, a.shape[1]), lambda i, p, j=j: (p[j], 0)) for j, a in enumerate(arrays)]
    if last is not None:
        arrays.append(last)
        specs.append(pl.BlockSpec(last.shape, lambda i, p: (0, 0)))
        order.land(last)
    deps = order.deps()
    outs = widths if apart else [sum(widths)]

    def kernel(places_ref, *refs):
        at, lo = 0, 0
        for i, (group, width) in enumerate(zip(groups, widths)):
            total = sum(r[...].astype(f32) for r in refs[at : at + len(group)])
            if last is not None:
                total = total + refs[len(arrays) - 1][:, lo : lo + width].astype(f32)
            if apart:
                refs[i - len(groups)][...] = total.astype(dtype)
            else:
                refs[-1][:, lo : lo + width] = total.astype(dtype)
            at, lo = at + len(group), lo + width

    out = pl.pallas_call(
        kernel,
        grid_spec=pltpu.PrefetchScalarGridSpec(
            num_scalar_prefetch=1,
            grid=(1,),
            in_specs=specs + [pl.BlockSpec(memory_space=pl.ANY)] * len(deps),
            out_specs=[pl.BlockSpec((rows, w), lambda i, p: (0, 0)) for w in outs],
        ),
        out_shape=[jax.ShapeDtypeStruct((rows, w), dtype) for w in outs],
        compiler_params=pltpu.CompilerParams(vmem_limit_bytes=16 * 2**20),
        cost_estimate=COST,
    )(places, *arrays, *deps)
    order.leave(out[0])
    return out if apart else out[0]


def finish(ring, rest, shapes, order):
    ring.at += 1
    terms = [t for one in ring.spreads for t in one.terms(ring.at)]
    rows = ring.spreads[0].rows
    order.land(ring.come)
    deps = order.deps()
    places = jnp.stack([jnp.asarray(at, jnp.int32) for _, at in terms])
    specs = [pl.BlockSpec((rows, a.shape[1]), lambda i, p, j=j: (p[j], 0)) for j, (a, _) in enumerate(terms)]
    whole = lambda shape: pl.BlockSpec(shape, lambda i, p, n=len(shape): (0,) * n)

    def kernel(*refs):
        n = 3 + len(terms)
        finish_kernel(*refs[:n], *refs[n + len(deps) :], terms=len(terms))

    return pl.pallas_call(
        kernel,
        grid_spec=pltpu.PrefetchScalarGridSpec(
            num_scalar_prefetch=1,
            grid=(1,),
            in_specs=specs
            + [whole(ring.come.shape), whole(rest.shape)]
            + [pl.BlockSpec(memory_space=pl.ANY)] * len(deps),
            out_specs=[whole(s) for s in shapes],
        ),
        out_shape=[jax.ShapeDtypeStruct(s, f32) for s in shapes],
        compiler_params=pltpu.CompilerParams(vmem_limit_bytes=16 * 2**20),
        cost_estimate=COST,
    )(places, *[a for a, _ in terms], ring.come, rest, *deps)


class Ring:
    def __init__(self, spreads, order):
        self.spreads, self.at = spreads, 0
        self.total, self.come = None, None
        self.step(order)

    def done(self):
        return self.at == lax.axis_size("ctx")

    def step(self, order):
        if self.done():
            return
        self.at += 1
        groups = [one.terms(self.at) for one in self.spreads]
        last = lax.axis_size("ctx") == self.at
        self.total = block_sum(groups, self.come, self.spreads[0].rows, f32 if last else bf16, order, last)
        if not last:
            self.come = rotate(self.total, "ctx", 1)


def halve_kernel(near, come, near_ref, away_ref):
    total = near[...].astype(f32) + come[...].astype(f32)
    near_ref[...] = total[:, : near_ref.shape[1]]
    away_ref[...] = total[:, near_ref.shape[1] :].astype(bf16)


def add_kernel(a, b, out_ref):
    out_ref[...] = a[...] + b[...]


def add_both_kernel(a, b, come, a_ref, b_ref):
    wide = a_ref.shape[1]
    a_ref[...] = a[...] + come[:, :wide]
    b_ref[...] = b[...] + come[:, wide:]


class Cube:
    def __init__(self, near, away):
        self.near, self.away, self.mask = near, away, 1
        self.come = flip(away, "tp", 1)

    def halve(self, order):
        seqs, rows, wide = self.near.shape
        while self.mask * 2 < lax.axis_size("tp"):
            wide //= 2
            order.land(self.come)
            out = (seqs, rows, wide)
            self.near, self.away = call(
                halve_kernel,
                0,
                seqs,
                [(self.near, 0), (self.come, 0)],
                [(out, f32, True), (out, bf16, True)],
                deps=order.deps(),
            vmem=16,
            )
            order.leave(self.away)
            self.mask *= 2
            self.come = flip(self.away, "tp", self.mask)

    def total(self):
        return self.near + self.come.astype(f32)


class Hops:
    def __init__(self, v, own, axes=("tp", "fsdp", "ctx")):
        self.v, self.own = v, own
        hops = {axis: [(axis, 1 << i) for i in range(lax.axis_size(axis).bit_length() - 1)] for axis in axes}
        self.todo = hops["tp"][:1] + hops.get("fsdp", []) + hops.get("ctx", []) + hops["tp"][1:]
        self.come, self.both = None, False

    def go(self, order):
        if self.come is not None:
            order.land(self.come)
            if self.both:
                self.v, self.own = small_call(
                    add_both_kernel, [self.v, self.own, self.come], [(self.v.shape, f32), (self.own.shape, f32)], order
                )
            else:
                self.v = small_call(add_kernel, [self.v, self.come], [(self.v.shape, f32)], order)[0]
            order.leave(self.v)
            self.come = None
        if self.todo:
            axis, mask = self.todo.pop(0)
            self.both = axis != "tp" and self.own is not None
            self.come = flip(jnp.concatenate([self.v, self.own], 1) if self.both else self.v, axis, mask)

    def end(self, order):
        while self.come is not None:
            self.go(order)
        return self.v


def small_call(kernel, operands, outs, order, scalar=None, scratch=()):
    deps = order.deps()
    n_in = len(operands) + (scalar is not None)

    def run(*refs):
        kernel(*refs[:n_in], *refs[n_in + len(deps) :])

    vmem = pl.BlockSpec(memory_space=pltpu.VMEM)
    return pl.pallas_call(
        run,
        in_specs=([] if scalar is None else [pl.BlockSpec(memory_space=pltpu.SMEM)])
        + [vmem] * len(operands)
        + [pl.BlockSpec(memory_space=pl.ANY)] * len(deps),
        out_specs=[vmem] * len(outs),
        out_shape=[jax.ShapeDtypeStruct(*o) for o in outs],
        scratch_shapes=list(scratch),
        compiler_params=pltpu.CompilerParams(vmem_limit_bytes=16 * 2**20),
        cost_estimate=COST,
    )(*([] if scalar is None else [scalar]), *operands, *deps)


class Chain:
    def __init__(self, parts, decay, reverse):
        self.parts, self.decay, self.reverse = parts, decay, reverse
        self.hop, self.last, self.entering = 0, None, []

    def send(self, order):
        n = lax.axis_size("ctx")
        self.hop += 1
        if self.hop >= n:
            return
        out = self.parts
        if self.last is not None:
            order.land(self.last)
            out = small_call(
                combine_kernel, [self.parts, self.decay, self.last], [(out.shape, bf16)], order
            )[0]
            order.leave(out)
        hop = self.hop
        pair = (n - hop, n - hop - 1) if self.reverse else (hop - 1, hop)
        self.last = lax.ppermute(out, "ctx", [pair])
        self.entering.append(self.last)

    def land(self, order):
        order.land(self.last)


class Order:
    def __init__(self):
        self.waits = []

    def land(self, *arrays):
        self.waits += arrays

    def enter(self, v):
        v = after(v, *self.waits)
        self.waits = []
        return v

    def deps(self):
        waits, self.waits = self.waits, []
        return waits

    def leave(self, v):
        self.waits = self.waits + [v]
        return v


def dot(a, b, dims=NN):
    return lax.dot_general(a, b, dims, preferred_element_type=f32)


def split(v, terms):
    out = []
    for i in range(terms):
        t = v.astype(bf16)
        out.append(t)
        if i + 1 < terms:
            v = v - t.astype(f32)
    return out


def constants(inner, q):
    heads = jnp.arange(LANES, dtype=jnp.int32)[:, None] == jnp.arange(inner, dtype=jnp.int32)[None] // HEADDIM
    spread = heads.astype(bf16)
    tri = jnp.arange(q, dtype=jnp.int32)[None] <= jnp.arange(q, dtype=jnp.int32)[:, None]
    return jnp.concatenate([spread, spread]), spread.T, tri.astype(bf16)


def widen(v, spread):
    return dot(jnp.concatenate(split(v, 2), 1), spread[...])


def narrow(v, gather, terms):
    out = None
    for t in split(v, terms):
        s = dot(t, gather[...])
        out = s if out is None else out + s
    return out


def tri_sum(tri, v, dims=NN):
    out = None
    for t in split(v, 3):
        s = dot(tri[...], t, dims)
        out = s if out is None else out + s
    return out


def one_of(refs):
    total = refs[0][...]
    for r in refs[1:]:
        total = total + r[...]
    return total


def halves(v):
    lane = lax.broadcasted_iota(jnp.int32, v.shape, 1)
    zero = jnp.zeros_like(v)
    return jnp.where(lane < HEADDIM, v, zero), jnp.where(lane >= HEADDIM, v, zero)


def sigmoid(v):
    return lax.logistic(v)


def gather_rows(places, pieces, whole):
    rows = pieces[0].shape[0]
    for i, piece in enumerate(pieces):
        whole[pl.ds(pl.multiple_of(places[i] * rows, 16), rows), :] = piece[...]


def project_kernel(nx, start, w, taps, bias, head_par, spread, tri, *refs, inner, conv):
    u_ref, slope_ref, act_ref, xdt_ref, dtl_ref, state_ref, dec_ref = refs[-7:]
    q = start.shape[0]
    u = dot(nx[...], w[...])
    u_ref[...] = u[:, :conv].astype(bf16)
    at = lax.broadcasted_iota(jnp.int32, (q, 1), 0)
    begin = start[...]
    since = jnp.broadcast_to(at - begin, (q, LANES))
    keep = [jnp.where(since >= j, 1.0, 0.0) for j in range(CONV)]
    for lo in range(0, conv, LANES):
        cols = slice(lo, lo + LANES)
        ut = u[:, cols]
        acc = bias[0:1, cols] + taps[CONV - 1 : CONV, cols] * ut[HALO:]
        for j in range(1, CONV):
            window = ut[HALO - j : HALO - j + q]
            acc = acc + taps[CONV - 1 - j : CONV - j, cols] * (window * keep[j])
        sig = sigmoid(acc)
        silu = acc * sig
        act_ref[:, cols] = silu.astype(bf16)
        slope_ref[:, cols] = (sig + silu * (1.0 - sig)).astype(bf16)
    v = u[HALO:, conv:] + head_par[0:1, :]
    dt = jnp.maximum(v, 0.0) + jnp.log1p(jnp.exp(-jnp.abs(v)))
    cum = tri_sum(tri, -dt * jnp.exp(head_par[1:2, :]))
    dtl_ref[:, :LANES] = dt
    dtl_ref[:, LANES:] = cum
    end = cum[q - 1 : q, :]
    begin_last = begin[q - 1 : q, :]
    tail = jnp.where(begin == begin_last, jnp.exp(end - cum), 0.0)
    xh = act_ref[:, :inner].astype(f32)
    xdt = (xh * widen(dt, spread)).astype(bf16)
    xdt_ref[...] = xdt
    weighted = (xdt.astype(f32) * widen(tail, spread)).astype(bf16)
    b = act_ref[:, inner : inner + STATE]
    state_ref[...] = dot(b, weighted, TN).astype(bf16)
    total = jnp.where(begin_last < 0, jnp.exp(end), 0.0)
    dec_ref[...] = widen(jnp.broadcast_to(total, (8, LANES)), spread)[0:1]


def project_first_kernel(places, nx, start, taps, bias, head_par, spread, tri, *refs, pieces, inner, conv):
    w = refs[-1]

    @pl.when(pl.program_id(0) == 0)
    def _():
        gather_rows(places, refs[:pieces], w)

    project_kernel(nx, start, w, taps, bias, head_par, spread, tri, *refs[pieces:-1], inner=inner, conv=conv)


def combine_kernel(parts, decay, last, out_ref):
    out_ref[...] = (parts[...].astype(f32) + decay[...] * last[...].astype(f32)).astype(bf16)


def score_mask(begin_col, q):
    r = lax.broadcasted_iota(jnp.int32, (q, q), 0)
    c = lax.broadcasted_iota(jnp.int32, (q, q), 1)
    return (c <= r) & (c >= begin_col)


def score_mask_t(begin_row, q):
    r = lax.broadcasted_iota(jnp.int32, (q, q), 0)
    c = lax.broadcasted_iota(jnp.int32, (q, q), 1)
    return (r <= c) & (r >= begin_row)


def local_kernel(act, xdt, dtl, start, y_ref, *, inner):
    q = start.shape[0]
    b = act[:, inner : inner + STATE]
    c = act[:, inner + STATE : inner + 2 * STATE]
    scores = jnp.where(score_mask(start[...], q), dot(c, b, NT), 0.0)
    cum = dtl[:, LANES:]
    cum_t = cum.T
    for pair in range(inner // LANES):
        cols = slice(pair * LANES, (pair + 1) * LANES)
        weights = []
        for h in (2 * pair, 2 * pair + 1):
            gap = jnp.minimum(cum[:, h : h + 1] - cum_t[h : h + 1, :], 0.0)
            weights.append((jnp.exp(gap) * scores).astype(bf16))
        even, odd = halves(xdt[:, cols])
        y_ref[:, cols] = dot(weights[0], even) + dot(weights[1], odd)


def gate_sums_kernel(nx, cot, y_in, act, dtl, start, state, w, rows, spread, y_ref, z_ref, dh_ref, sums_ref, *, inner):
    q = start.shape[0]
    c = act[:, inner + STATE : inner + 2 * STATE]
    zz = dot(nx[HALO:], w[:, :inner])
    z_ref[...] = zz
    d_hidden = dot(cot[...], w[:, inner:])
    dh_ref[...] = d_hidden
    into = widen(jnp.where(start[...] < 0, jnp.exp(dtl[:, LANES:]), 0.0), spread)
    y = y_in[...] + into * dot(c, one_of(state))
    y_ref[...] = y
    gated = (y + rows[0:1, :] * act[:, :inner].astype(f32)) * (zz * sigmoid(zz))
    e = d_hidden * rows[1:2, :]
    ones = jnp.ones((8, inner), bf16)
    sq = dot(ones, (gated * gated).astype(bf16), NT)
    eg = dot(ones, (e * gated).astype(bf16), NT)
    row = lax.broadcasted_iota(jnp.int32, (8, q), 0)
    sums_ref[...] = jnp.where(row == 0, sq, eg)


def gate_sums_first_kernel(places, nx, cot, y_in, act, dtl, start, *refs, pieces, hops, inner):
    state, (rows, spread), refs = refs[:hops], refs[hops : hops + 2], refs[hops + 2 :]
    y_ref, z_ref, dh_ref, sums_ref, w = refs[pieces], refs[pieces + 1], refs[pieces + 2], refs[pieces + 3], refs[-1]

    @pl.when(pl.program_id(0) == 0)
    def _():
        gather_rows(places, refs[:pieces], w)

    gate_sums_kernel(
        nx, cot, y_in, act, dtl, start, state, w, rows, spread, y_ref, z_ref, dh_ref, sums_ref, inner=inner
    )


def gate_sums_next_kernel(nx, cot, y_in, act, dtl, start, *refs, hops, inner):
    gate_sums_kernel(nx, cot, y_in, act, dtl, start, refs[:hops], *refs[hops:], inner=inner)


def mix_kernel(rank, hidden, w, near_ref, away_ref):
    seqs, q, cols = near_ref.shape
    k = pl.program_id(0)
    out = dot(hidden[...].reshape(seqs * q, hidden.shape[2]), w[...], NT).astype(bf16).reshape(seqs, q, cols)

    @pl.when(lax.rem(k, 2) == 0)
    def _():
        near_ref[...] = out

    @pl.when(lax.rem(k, 2) == 1)
    def _():
        away_ref[...] = out


def out_back_kernel(rank, du, rim, nx, z_part, w_in, near_ref, away_ref, gain_ref, own, part):
    seqs, q = du.shape[0], du.shape[1] - HALO
    cols = w_in.shape[0]
    tp = near_ref.shape[2] * 2 // cols
    k = pl.program_id(0)

    @pl.when(k == 0)
    def _():
        for s in range(seqs):
            own[s * q : (s + 1) * q - 16, :] = du[s, HALO:q, :]
            edge = du[s, q : q + HALO, :].astype(f32)
            own[(s + 1) * q - 16 : (s + 1) * q, :] = (edge + rim[s].astype(f32)).astype(bf16)
        part[...] = jnp.zeros_like(part)

    out = dot(own[...], w_in[...], NT)
    gains = jnp.zeros((1, cols), f32)
    for s in range(seqs):
        mine = out[s * q : (s + 1) * q] + z_part[s, HALO:, :].astype(f32)
        prod = mine * nx[s, HALO:, :].astype(f32)
        folded = prod[:, :LANES]
        for lo in range(LANES, cols, LANES):
            folded = folded + prod[:, lo : lo + LANES]
        part[s * q : (s + 1) * q, :] += folded
        gains = gains + jnp.sum(prod, axis=0, keepdims=True)
        for j in range(tp):
            to = slice(j // 2 * cols, (j // 2 + 1) * cols)

            @pl.when(k == j)
            def _():
                (away_ref if j % 2 else near_ref)[s, :q, to] = mine.astype(bf16)

    gain_ref[...] = jnp.broadcast_to(gains, gain_ref.shape)

    @pl.when(k == tp - 1)
    def _():
        ones = jnp.ones((16, LANES), bf16)
        for s in range(seqs):
            total = None
            for t in split(part[s * q : (s + 1) * q, :], 2):
                one = dot(ones, t, NT)
                total = one if total is None else total + one
            total = jnp.concatenate([total, jnp.zeros((16, cols - q), f32)], 1)
            for j in range(tp):
                to = slice(j // 2 * cols, (j // 2 + 1) * cols)
                (away_ref if j % 2 else near_ref)[s, q:, to] = total.astype(bf16)


def pack_kernel(gain, *refs, chunks, inner, conv):
    taps, heads, gates = refs[:chunks], refs[chunks : 2 * chunks], refs[2 * chunks : 3 * chunks]
    tp_ref, own_ref = refs[-2:]
    total = lambda refs: sum(jnp.sum(r[...], axis=0) for r in refs)
    tap = total(taps)
    row = lax.broadcasted_iota(jnp.int32, gain.shape, 0)
    tp_ref[:, : 2 * STATE] = tap[:, inner:]
    tp_ref[:, 2 * STATE :] = jnp.where(row == 0, gain[...], 0.0)
    own_ref[:, :inner] = tap[:, :inner]
    own_ref[:, inner : inner + LANES] = total(heads)
    own_ref[:, inner + LANES :] = total(gates)


def unpack_kernel(
    rank, v, own, come, gain, gather, conv_ref, convb_ref, bc_ref, bcb_ref, dtb_ref, alog_ref, skip_ref, gate_ref, gain_ref
):
    inner, cols = gate_ref.shape[1], gain_ref.shape[1]
    heads = skip_ref.shape[1]
    bc = v[:, : 2 * STATE] + come[:, : 2 * STATE]
    bc_ref[...] = bc[:CONV]
    bcb_ref[...] = bc[CONV : CONV + 1]
    at = pl.multiple_of(2 * STATE + rank[0] * cols, LANES)
    gain_ref[...] = (v[0:1, pl.ds(at, cols)] + come[0:1, pl.ds(at, cols)]) / gain[0:1, :]
    taps = own[:, :inner]
    conv_ref[...] = taps[:CONV]
    convb_ref[...] = taps[CONV : CONV + 1]
    head = own[:, inner : inner + LANES]
    dtb_ref[...] = head[0:1, :heads]
    alog_ref[...] = head[1:2, :heads]
    gate = own[:, inner + LANES :]
    gate_ref[...] = gate[0:1]
    skip_ref[...] = narrow(gate, gather, 3)[1:2, :heads]


def tokens_kernel(near, come, own, cot, inv, gain, out_ref):
    q, cols = out_ref.shape
    total = near[...] + come[...].astype(f32)
    both = jnp.broadcast_to(total[q : q + 8, :q][0:1], (8, q)).T[:, 0:1]
    hat = own[...].astype(f32) * inv[...]
    out_ref[...] = cot[...].astype(f32) + inv[...] * (total[:q] * gain[0:1, :] - hat * (both / D))


def finish_kernel(places, *refs, terms):
    come, rest = refs[terms], refs[terms + 1]
    zx_ref, bc_ref, dt_ref = refs[-3:]
    inner, wide, heads = zx_ref.shape[2], bc_ref.shape[1], dt_ref.shape[1]
    total = sum(r[...].astype(f32) for r in refs[:terms]) + come[...].astype(f32)
    zx_ref[:, 0, :] = rest[...]
    zx_ref[:, 1, :] = total[:, :inner]
    bc_ref[...] = total[:, inner : inner + wide]
    dt_ref[...] = total[:, inner + wide : inner + wide + heads]


def norm_kernel(x, halo, gain, nx_ref, inv_ref):
    wide = x[...].astype(f32)
    width = wide.shape[1]
    inv = lax.rsqrt(jnp.mean(wide * wide, axis=-1, keepdims=True) + NORM_EPS)
    inv_ref[...] = inv
    nx_ref[HALO:, :] = (wide * inv * gain[0:1, :]).astype(bf16)
    edge = halo[...].astype(f32)
    inv = lax.rsqrt(jnp.mean(edge * edge, axis=-1, keepdims=True) + NORM_EPS)
    nx_ref[:HALO, :] = (edge * inv * gain[0:1, :]).astype(bf16)


def gate_kernel(y_in, act, dtl, start, z, dh, sums, rows, spread, *refs, inner):
    hidden_ref, dz_ref, dy_ref, dstate_ref, grads_ref = refs[-5:]
    xh = act[:, :inner].astype(f32)
    y = y_in[...] + rows[0:1, :] * xh
    zz = z[...].astype(f32)
    sig = sigmoid(zz)
    silu = zz * sig
    gated = y * silu
    gain = rows[1:2, :]
    d_hidden = dh[...].astype(f32)
    sums_t = sums[...].T
    inv = lax.rsqrt(sums_t[:, 0:1] / INNER + NORM_EPS)
    back = sums_t[:, 1:2] * (inv * inv * inv) / INNER
    scaled = gated * inv
    hidden_ref[...] = (scaled * gain).astype(bf16)
    dg = inv * (d_hidden * gain) - gated * back
    dy = (dg * silu).astype(bf16)
    dy_ref[...] = dy
    dz_ref[:HALO, :] = jnp.zeros((HALO, inner), bf16)
    dz_ref[HALO:, :] = (dg * y * sig * (1.0 + zz * (1.0 - sig))).astype(bf16)
    gate_row = jnp.sum(d_hidden * scaled, axis=0, keepdims=True)
    dy_wide = dy.astype(f32)
    skip_row = jnp.sum(dy_wide * xh, axis=0, keepdims=True)
    row = lax.broadcasted_iota(jnp.int32, (8, inner), 0)
    grads_ref[...] = jnp.where(row == 0, gate_row, jnp.where(row == 1, skip_row, 0.0))
    into = widen(jnp.where(start[...] < 0, jnp.exp(dtl[:, LANES:]), 0.0), spread)
    c = act[:, inner + STATE : inner + 2 * STATE]
    dstate_ref[...] = dot(c, (into * dy_wide).astype(bf16), TN).astype(bf16)


def local_back_kernel(act, xdt, dtl, start, start_row, dy, *refs, hops, inner):
    state, (spread, dx_ref, dbc_ref) = refs[:hops], refs[hops:]
    q = start.shape[0]
    b = act[:, inner : inner + STATE]
    c = act[:, inner + STATE : inner + 2 * STATE]
    mask = score_mask_t(start_row[...], q)
    scores = jnp.where(mask, dot(b, c, NT), 0.0)
    cum = dtl[:, LANES:]
    cum_t = cum.T
    total = jnp.zeros((q, q), f32)
    for pair in range(inner // LANES):
        cols = slice(pair * LANES, (pair + 1) * LANES)
        dy_pair = dy[:, cols]
        x_even, x_odd = halves(xdt[:, cols])
        dy_even, dy_odd = halves(dy_pair)
        out = None
        for h, x_one, dy_one in ((2 * pair, x_even, dy_even), (2 * pair + 1, x_odd, dy_odd)):
            decay = jnp.exp(jnp.minimum(cum_t[h : h + 1, :] - cum[:, h : h + 1], 0.0))
            total = total + dot(x_one, dy_pair, NT) * decay
            term = dot((decay * scores).astype(bf16), dy_one)
            out = term if out is None else out + term
        dx_ref[:, cols] = out
    d_scores = jnp.where(mask, total, 0.0).astype(bf16)
    into = widen(jnp.where(start[...] < 0, jnp.exp(cum), 0.0), spread)
    weighted = (into * dy[...].astype(f32)).astype(bf16)
    dbc_ref[:, :STATE] = dot(d_scores, c)
    dbc_ref[:, STATE:] = dot(d_scores, b, TN) + dot(weighted, one_of(state), NT)


def conv_back_kernel(act, xdt, dtl, start, dy, y_in, dx, dbc, slope, u, dec, *refs, hops, inner, conv):
    state, later, refs = refs[:hops], refs[hops : 2 * hops], refs[2 * hops :]
    taps, rows, head_par, spread, gather, tri = refs[:6]
    du_ref, rim_ref, tap_ref, head_ref, dact = refs[-5:]
    q = start.shape[0]
    begin = start[...]
    b = act[:, inner : inner + STATE]
    dt, cum = dtl[:, :LANES], dtl[:, LANES:]
    end = cum[q - 1 : q, :]
    begin_last = begin[q - 1 : q, :]
    tail = widen(jnp.where(begin == begin_last, jnp.exp(end - cum), 0.0), spread)
    x_dt = xdt[...].astype(f32)
    d_y = dy[...].astype(f32)
    g = one_of(later)
    dx_tail = tail * dot(b, g)
    dact[:, inner : inner + STATE] = dbc[:, :STATE] + dot((x_dt * tail).astype(bf16), g, NT)
    dact[:, inner + STATE :] = dbc[:, STATE:]
    dx_local = dx[...]
    dx_all = dx_local + dx_tail
    dact[:, :inner] = dx_all * widen(dt, spread) + rows[0:1, :] * d_y
    flux_near = narrow(d_y * y_in[...] - x_dt * dx_local, gather, 3)
    flux_tail = narrow(x_dt * dx_tail, gather, 2)
    d_dt = narrow(dx_all * act[:, :inner].astype(f32), gather, 2)
    through = jnp.sum(dec[...] * (g.astype(f32) * one_of(state).astype(f32)), axis=0, keepdims=True)
    through = narrow(jnp.broadcast_to(through, (8, inner)), gather, 2)[0:1]
    d_log = tri_sum(tri, flux_near, TN) + (tri_sum(tri, flux_tail) - flux_tail) + through
    rate = jnp.exp(head_par[1:2, :])
    d_raw = (d_dt - rate * d_log) * (1.0 - jnp.exp(-dt))
    du_ref[:HALO, conv:] = jnp.zeros((HALO, LANES), bf16)
    rim_ref[:, conv:] = jnp.zeros((HALO, LANES), bf16)
    du_ref[HALO:, conv:] = d_raw.astype(bf16)
    bias_row = jnp.sum(d_raw, axis=0, keepdims=True)
    log_row = -jnp.sum(d_log * dt * rate, axis=0, keepdims=True)
    row = lax.broadcasted_iota(jnp.int32, (8, LANES), 0)
    head_ref[...] = jnp.where(row == 0, bias_row, jnp.where(row == 1, log_row, 0.0))
    since = lax.broadcasted_iota(jnp.int32, (q, LANES), 0) - begin
    keep = [jnp.where(since >= j, 1.0, 0.0) for j in range(CONV)]
    zeros = jnp.zeros((HALO, LANES), f32)
    for lo in range(0, conv, LANES):
        cols = slice(lo, lo + LANES)
        dp = dact[:, cols] * slope[:, cols].astype(f32)
        ut = u[:, cols].astype(f32)
        moved = jnp.concatenate([zeros, dp], 0)
        total = taps[CONV - 1 : CONV, cols] * moved
        tap_rows = [jnp.sum(dp * ut[HALO:], axis=0, keepdims=True)]
        for j in range(1, CONV):
            moved = jnp.concatenate([zeros, dp * keep[j], zeros], 0)[j : j + q + HALO]
            tap_rows.append(jnp.sum(moved * ut, axis=0, keepdims=True))
            total = total + taps[CONV - 1 - j : CONV - j, cols] * moved
        du_ref[:, cols] = total.astype(bf16)
        rim_ref[:, cols] = total[:HALO].astype(bf16)
        out = jnp.sum(dp, axis=0, keepdims=True)
        for j in range(CONV):
            out = jnp.where(row == CONV - 1 - j, tap_rows[j], jnp.where(row == CONV, out, 0.0) if j == 0 else out)
        tap_ref[:, cols] = out


def call(kernel, first, count, ins, outs, shared=(), scalar=None, scratch=(), into=None, deps=(), vmem=34):
    def spec(shape, base):
        block = (None,) + tuple(shape[1:])
        rest = (0,) * (len(shape) - 1)
        return pl.BlockSpec(block, lambda s: (s + base,) + rest)

    in_specs = [spec(a.shape, o) for a, o in ins]
    in_specs += [
        pl.BlockSpec(a.shape, lambda s, n=a.ndim: (0,) * n, pipeline_mode=pl.Buffered(1)) for a in shared
    ]
    operands = [a for a, _ in ins] + list(shared)
    if scalar is not None:
        in_specs.insert(0, pl.BlockSpec(memory_space=pltpu.SMEM))
        operands.insert(0, scalar)
    n_args = len(operands)
    operands += list(deps)
    in_specs += [pl.BlockSpec(memory_space=pl.ANY)] * len(deps)
    aliases = {}
    if into is not None:
        for i, buf in enumerate(into):
            if buf is not None:
                aliases[len(operands)] = i
                operands.append(buf)
                in_specs.append(pl.BlockSpec(memory_space=pl.ANY))
    n_in = len(operands)

    def run(*refs):
        kernel(*refs[:n_args], *refs[n_in:])

    return pl.pallas_call(
        run,
        grid=(count,),
        in_specs=in_specs,
        out_specs=[spec(s, first if whole else 0) if whole is not None else pl.BlockSpec(s, lambda i, n=len(s): (0,) * n) for s, _, whole in outs],
        out_shape=[jax.ShapeDtypeStruct(s, d) for s, d, _ in outs],
        scratch_shapes=list(scratch),
        input_output_aliases=aliases,
        compiler_params=pltpu.CompilerParams(vmem_limit_bytes=vmem * 2**20),
        cost_estimate=COST,
    )(*operands)


def call_slices(kernel, rank, tp, wholes, weights, outs, scratch=(), deps=()):
    specs, operands = [], []
    for a, cut in wholes:
        if cut:
            block = a.shape[:-1] + (a.shape[-1] // tp,)
            specs.append(pl.BlockSpec(block, lambda k, r, n=a.ndim: (0,) * (n - 1) + (r[0] ^ k,)))
        else:
            specs.append(pl.BlockSpec(a.shape, lambda k, r, n=a.ndim: (0,) * n))
        operands.append(a)
    for a, at, cols in weights:
        specs.append(pl.BlockSpec((a.shape[0] // tp, cols), lambda k, r, j=at // cols: (r[0] ^ k, j)))
        operands.append(a)
    n_args = len(operands) + 1
    operands += list(deps)
    specs += [pl.BlockSpec(memory_space=pl.ANY)] * len(deps)
    n_in = len(operands) + 1

    def run(*refs):
        kernel(*refs[:n_args], *refs[n_in:])

    out_specs = []
    for shape, _, cut in outs:
        n = len(shape)
        if cut is None:
            out_specs.append(pl.BlockSpec((shape[0], shape[1] // tp), lambda k, r: (0, r[0] ^ k)))
        elif cut:
            out_specs.append(
                pl.BlockSpec(shape[:-1] + (shape[-1] * 2 // tp,), lambda k, r, n=n: (0,) * (n - 1) + (k // 2,))
            )
        else:
            out_specs.append(pl.BlockSpec(shape, lambda k, r, n=n: (0,) * n))
    return pl.pallas_call(
        run,
        grid_spec=pltpu.PrefetchScalarGridSpec(
            num_scalar_prefetch=1,
            grid=(tp,),
            in_specs=specs,
            out_specs=out_specs,
            scratch_shapes=list(scratch),
        ),
        out_shape=[jax.ShapeDtypeStruct(s, d) for s, d, _ in outs],
        compiler_params=pltpu.CompilerParams(vmem_limit_bytes=34 * 2**20),
        cost_estimate=COST,
    )(rank, *operands)


def pack(taps, heads, gates, gain, order, inner, conv):
    out = small_call(
        functools.partial(pack_kernel, chunks=len(taps), inner=inner, conv=conv),
        [gain, *taps, *heads, *gates],
        [((8, 2 * STATE + gain.shape[1]), f32), ((8, 2 * inner + LANES), f32)],
        order,
    )
    order.leave(out[0])
    return out


def per_device(
    tokens,
    segment_ids,
    in_gain,
    w_zx,
    w_bc,
    w_dt,
    dt_bias,
    a_log,
    skip_gain,
    conv_x,
    conv_x_bias,
    conv_bc,
    conv_bc_bias,
    gate_gain,
    w_out,
    cotangent,
):
    tp_count, tp_rank = lax.axis_size("tp"), lax.axis_index("tp")
    ctx_rank = lax.axis_index("ctx")
    seqs, q, width = tokens.shape
    inner = w_zx.shape[2]
    heads = w_dt.shape[1]
    conv = inner + 2 * STATE
    cols = width // tp_count
    n_tok = seqs * q
    chunks = 2 if seqs % 2 == 0 else 1
    per = seqs // chunks

    n_ctx = lax.axis_size("ctx")
    rank = tp_rank.astype(jnp.int32)[None]
    shape = lambda *s: (seqs,) + s
    part = lambda *s: (per,) + s
    order = Order()

    first_w = jnp.concatenate(
        [w_zx[:, 1, :], w_bc, jnp.pad(w_dt, ((0, 0), (0, LANES - heads)))], axis=1
    )
    ring_in = ring_pieces(first_w)
    halo = shift(jnp.pad(tokens[:, q - 8 :, :], ((0, 0), (8, 0), (0, 0))), "ctx", 1)
    pieces_in, places = all_pieces(ring_in)
    in_kernel = first_w.shape[0] % 16 == 0
    second_w = jnp.concatenate([after(w_zx, first_w)[:, 0, :], w_out.T], axis=1)
    ring_rest = ring_pieces(after(second_w, ring_in[-1]))
    pieces_rest, _ = all_pieces(ring_rest, pieces_in[-1])
    spread, gather, tri = constants(inner, q)
    if not in_kernel:
        w_in, w_rest = assemble(pieces_in, places), assemble(pieces_rest, places)

    gain = jnp.broadcast_to(in_gain.astype(f32)[None], (8, width))
    bulk = None
    order.land(halo)
    for g in range(chunks):
        order.land(*ring_in[g + 1 : g + 2], *pieces_in[2 * g + 1 : 2 * g + 2])
        bulk = call(
            norm_kernel,
            g * per,
            per,
            [(tokens, g * per), (halo, g * per)],
            deps=order.deps(),
            vmem=16,
            outs=[(shape(q + HALO, width), bf16, True), (shape(q, 1), f32, True)],
            shared=(gain,),
            into=bulk,
        )
        order.leave(bulk[1])
    nx, inv_rms = bulk

    begin = segment_ids - ctx_rank * q
    start = begin[:, :, None]
    start_row = begin[:, None, :]
    taps = jnp.concatenate([conv_x, conv_bc], axis=1).astype(f32)
    bias = jnp.concatenate([conv_x_bias, conv_bc_bias]).astype(f32)[None]
    head_par = jnp.pad(jnp.stack([dt_bias, a_log]), ((0, 6), (0, LANES - heads)))
    rows = jnp.pad(jnp.stack([jnp.repeat(skip_gain, HEADDIM), gate_gain.astype(f32)]), ((0, 6), (0, 0)))

    states, decs, kept, y_local = [], [], [], []
    landing = lambda i: pieces_rest[min(i, len(pieces_rest) - 1)]
    for g in range(chunks):
        o = g * per
        order.land(ring_rest[min(g + 1, n_ctx - 1)])
        if g:
            order.land(landing(2 * g - 1))
        first = g == 0 and in_kernel
        given = [taps, bias, head_par, spread, tri]
        outs = [
            (part(q + HALO, conv), bf16, False),
            (part(q, conv), bf16, False),
            (part(q, conv), bf16, False),
            (part(q, inner), bf16, False),
            (part(q, 2 * LANES), f32, False),
            (part(STATE, inner), bf16, False),
            (part(1, inner), f32, False),
        ]
        if first:
            kernel = functools.partial(project_first_kernel, pieces=len(pieces_in), inner=inner, conv=conv)
        else:
            kernel = functools.partial(project_kernel, inner=inner, conv=conv)
        out = call(
            kernel,
            o,
            per,
            [(nx, o), (start, o)],
            outs + [((width, conv + LANES), bf16, None)] if first else outs,
            shared=given + pieces_in if first else [w_in] + given,
            scalar=places if first else None,
            deps=order.deps(),
            vmem=34,
        )
        if first:
            w_in = out[7]
        kept.append(out[:5])
        decs.append(order.leave(out[6]))
        states.append(Chain(out[5], out[6], False))
        states[-1].send(order)

    if n_ctx > 2:
        states[0].send(order)
    for g in range(chunks):
        u, slope, act, xdt, dtl = kept[g]
        if g == 0:
            order.land(ring_rest[min(chunks + 1, n_ctx - 1)], landing(2 * chunks - 1))
        y_local.append(
            order.leave(
                call(
                    functools.partial(local_kernel, inner=inner),
                    0,
                    per,
                    [(act, 0), (xdt, 0), (dtl, 0), (start, g * per)],
                    deps=order.deps(),
            vmem=16,
                    outs=[(part(q, inner), f32, False)],
                )[0]
            )
        )
    if n_ctx > 2:
        for one in states[1:]:
            one.send(order)
    for hop in range(3, n_ctx):
        for i, one in enumerate(states):
            if hop == 3:
                order.land(landing(2 * chunks + 1 + 2 * i))
            one.send(order)

    scans = []
    for g in range(chunks):
        o = g * per
        u, slope, act, xdt, dtl = kept[g]
        first = g == 0 and in_kernel
        hops = len(states[g].entering)
        outs = [
            (part(q, inner), f32, False),
            (part(q, inner), f32, False),
            (part(q, inner), f32, False),
            (part(8, q), f32, False),
        ]
        if first:
            kernel = functools.partial(gate_sums_first_kernel, pieces=len(pieces_rest), hops=hops, inner=inner)
            given = [rows, spread] + pieces_rest
            outs = outs + [((width, width), bf16, None)]
        else:
            kernel = functools.partial(gate_sums_next_kernel, hops=hops, inner=inner)
            given = [w_rest, rows, spread]
        out = call(
            kernel,
            o,
            per,
            [(nx, o), (cotangent, o), (y_local[g], 0), (act, 0), (dtl, 0), (start, o)]
            + [(v, 0) for v in states[g].entering],
            outs,
            shared=given,
            scalar=places if first else None,
            deps=order.deps(),
            vmem=56,
        )
        if first:
            w_rest = out[4]
        scans.append(out[:4])
        order.leave(out[3])
    sums = cube_sum(jnp.concatenate([one[3] for one in scans]), "tp")

    bulk = [None] * 2
    d_ys = []
    chains, gate_rows = [], []
    for g in range(chunks):
        o = g * per
        u, slope, act, xdt, dtl = kept[g]
        y_scan, z, d_hidden, _ = scans[g]
        out = call(
            functools.partial(gate_kernel, inner=inner),
            o,
            per,
            [(y_scan, 0), (act, 0), (dtl, 0), (start, o), (z, 0), (d_hidden, 0), (sums, o)],
            deps=order.deps(),
            vmem=34,
            outs=[
                (shape(q, inner), bf16, True),
                (shape(q + HALO, inner), bf16, True),
                (part(q, inner), bf16, False),
                (part(STATE, inner), bf16, False),
                (part(8, inner), f32, False),
            ],
            shared=(rows, spread),
            into=None if g == 0 else bulk,
        )
        bulk = list(out[:2])
        d_ys.append(out[2])
        order.leave(out[3])
        chains.append(Chain(out[3], decs[g], True))
        chains[-1].send(order)
        gate_rows.append(out[4])
    hidden, d_z = bulk

    def hop(i):
        if i < len(chains):
            chains[i].send(order)

    def back_local(g):
        o = g * per
        u, slope, act, xdt, dtl = kept[g]
        out = call(
            functools.partial(local_back_kernel, hops=n_ctx - 1, inner=inner),
            0,
            per,
            [(act, 0), (xdt, 0), (dtl, 0), (start, o), (start_row, o), (d_ys[g], 0)]
            + [(v, 0) for v in states[g].entering],
            deps=order.deps(),
            vmem=16,
            outs=[(part(q, inner), f32, False), (part(q, 2 * STATE), f32, False)],
            shared=(spread,),
        )
        order.leave(out[1])
        return out

    nx2 = nx.reshape(seqs * (q + HALO), width)
    steps = tuple(range(1, n_ctx + 1))
    grad = order.leave(dot(nx2, order.enter(d_z).reshape(seqs * (q + HALO), inner), TN).astype(bf16))
    rest_z = Spread(grad, [steps])
    hop(0)
    hop(1)
    grad = order.leave(
        dot(cotangent.reshape(n_tok, width), order.enter(hidden).reshape(n_tok, inner), TN).astype(bf16)
    )
    rest_o = Spread(grad, [steps])
    back = [back_local(0)]
    hop(0)
    hop(1)
    back += [back_local(g) for g in range(1, chunks)]
    for _ in range(3, n_ctx):
        hop(0)
        hop(1)
    z_part = order.leave(dot(order.enter(d_z).reshape(seqs * (q + HALO), inner), w_rest[:, :inner], NT).astype(bf16))
    z_part = z_part.reshape(seqs, q + HALO, width)
    own = lax.dynamic_slice_in_dim(tokens, tp_rank * cols, cols, 2)

    bulk = [None] * 2
    tap_rows, head_rows = [], []
    for g in range(chunks):
        have = 0 if g == 0 else 1
        o = g * per
        u, slope, act, xdt, dtl = kept[g]
        chains[g].land(order)
        out = call(
            functools.partial(conv_back_kernel, hops=n_ctx - 1, inner=inner, conv=conv),
            o,
            per,
            [(act, 0), (xdt, 0), (dtl, 0), (start, o), (d_ys[g], 0), (scans[g][0], 0), (back[g][0], 0), (back[g][1], 0), (slope, 0), (u, 0), (decs[g], 0)]
            + [(v, 0) for v in states[g].entering + chains[g].entering],
            deps=order.deps(),
            outs=[
                (shape(q + HALO, conv + LANES), bf16, True),
                (shape(HALO, conv + LANES), bf16, True),
                (part(8, conv), f32, False),
                (part(8, LANES), f32, False),
            ],
            shared=(taps, rows, head_par, spread, gather, tri),
            scratch=[pltpu.VMEM((q, conv), f32)],
            into=None if g == 0 else bulk,
        )
        bulk = list(out[:2])
        tap_rows.append(out[2])
        head_rows.append(out[3])
        order.leave(out[3])
        if g == 0:
            ring = Ring([rest_z, rest_o], order)
    du = bulk[0]
    rim = rotate(bulk[1], "ctx", -1)

    grad = order.leave(dot(nx2, du.reshape(seqs * (q + HALO), conv + LANES), TN).astype(bf16))
    spread_in = Spread(grad, [steps[:1]])
    ring.step(order)
    spread_in.more(steps[1:], order)
    order.land(spread_in.sent)

    near, away = call_slices(
        mix_kernel,
        rank,
        tp_count,
        [(hidden, False)],
        deps=order.deps(),
        weights=[(w_rest, inner, inner)],
        outs=[(shape(q, width // 2), bf16, True), (shape(q, width // 2), bf16, True)],
    )
    order.leave(near)
    cube_mix = Cube(near, away)
    ring_in = Ring([spread_in], order)

    in_gain_own = lax.dynamic_slice_in_dim(in_gain, tp_rank * cols, cols, 0).astype(f32)
    order.land(rim)
    near, away, gain_part = call_slices(
        out_back_kernel,
        rank,
        tp_count,
        [(du, False), (rim, False), (nx, True), (z_part, True)],
        [(w_in, 0, conv + LANES)],
        deps=order.deps(),
        outs=[
            (shape(q + HALO, width // 2), bf16, False),
            (shape(q + HALO, width // 2), bf16, False),
            ((8, width), f32, None),
        ],
        scratch=[pltpu.VMEM((n_tok, conv + LANES), bf16), pltpu.VMEM((n_tok, LANES), f32)],
    )
    order.leave(gain_part)
    cube = Cube(near, away)

    ring.step(order)
    cube.halve(order)
    ring_in.step(order)
    while not ring.done():
        ring.step(order)
    grad_wz, grad_wo = ring.total
    cube_mix.halve(order)
    small = Hops(*pack(tap_rows, head_rows, gate_rows, gain_part, order, inner, conv))
    small.go(order)
    while ring_in.at < n_ctx - 1:
        ring_in.step(order)
    small.go(order)
    gain_row = jnp.broadcast_to(in_gain_own[None], (8, cols))
    own_cot = lax.dynamic_slice_in_dim(cotangent, tp_rank * cols, cols, 2)
    order.land(cube.come)
    (grad_tokens,) = call(
        tokens_kernel,
        0,
        seqs,
        [(cube.near, 0), (cube.come, 0), (own, 0), (own_cot, 0), (inv_rms, 0)],
        [(shape(q, cols), f32, True)],
        shared=(gain_row,),
        deps=order.deps(),
            vmem=16,
    )
    order.leave(grad_tokens)
    small.go(order)
    order.land(cube_mix.come)
    mixed = order.leave((order.enter(own).astype(f32) + cube_mix.total()).astype(bf16))
    small.go(order)
    rows_own = grad_wz.shape[0]
    grad_zx, grad_bc, grad_dt = finish(
        ring_in, grad_wz, [(rows_own, 2, inner), (rows_own, 2 * STATE), (rows_own, heads)], order
    )
    bc_hops = Hops(grad_bc, None, ["tp"])
    bc_hops.go(order)
    while small.todo:
        small.go(order)
    order.land(small.come)
    one = lambda n: ((1, n), f32)
    conv_own, convb_own, conv_all, convb_all, dtb, alog, skip, gate, gain_row = small_call(
        unpack_kernel,
        [small.v, small.own, small.come, gain_row, gather],
        [((CONV, inner), f32), one(inner), ((CONV, 2 * STATE), f32), one(2 * STATE), one(heads), one(heads), one(heads), one(inner), one(cols)],
        order,
        scalar=rank,
    )
    grad_bc = bc_hops.end(order)

    return (
        mixed,
        grad_tokens,
        gain_row[0],
        grad_zx,
        grad_bc,
        grad_dt,
        dtb[0],
        alog[0],
        skip[0],
        conv_own,
        convb_own[0],
        conv_all,
        convb_all[0],
        gate[0],
        grad_wo.T,
    )


def solution(mesh):
    return jax.shard_map(
        per_device,
        mesh=mesh,
        in_specs=(
            P("fsdp", "ctx", None),
            P("fsdp", "ctx"),
            P(),
            P(("fsdp", "ctx"), None, "tp"),
            P(("fsdp", "ctx"), None),
            P(("fsdp", "ctx"), "tp"),
            P("tp"),
            P("tp"),
            P("tp"),
            P(None, "tp"),
            P("tp"),
            P(),
            P(),
            P("tp"),
            P("tp", ("fsdp", "ctx")),
            P("fsdp", "ctx", None),
        ),
        out_specs=(
            P("fsdp", "ctx", "tp"),
            P("fsdp", "ctx", "tp"),
            P("tp"),
            P(("fsdp", "ctx"), None, "tp"),
            P(("fsdp", "ctx"), None),
            P(("fsdp", "ctx"), "tp"),
            P("tp"),
            P("tp"),
            P("tp"),
            P(None, "tp"),
            P("tp"),
            P(),
            P(),
            P("tp"),
            P("tp", ("fsdp", "ctx")),
        ),
        check_vma=False,
    )
```

```python
import functools

import jax
import jax.numpy as jnp
from jax import lax
from jax.experimental import pallas as pl
from jax.experimental.pallas import tpu as pltpu
from jax.sharding import PartitionSpec as P

D = 1536
HEADDIM = 64
STATE = 128
CONV = 4
INNER = 3072
NORM_EPS = 1e-05
LANES = 128
HALO = 16
COST = pl.CostEstimate(flops=2 * 10**12, bytes_accessed=8 * 10**9, transcendentals=0)

bf16 = jnp.bfloat16
f32 = jnp.float32
NN = (((1,), (0,)), ((), ()))
NT = (((1,), (1,)), ((), ()))
TN = (((0,), (0,)), ((), ()))


def rotate(v, axis, steps):
    n = lax.axis_size(axis)
    return lax.ppermute(v, axis, [(i, (i + steps) % n) for i in range(n)])


def shift(v, axis, steps):
    n = lax.axis_size(axis)
    return lax.ppermute(v, axis, [(i, i + steps) for i in range(n) if 0 <= i + steps < n])


def flip(v, axis, mask):
    n = lax.axis_size(axis)
    return lax.ppermute(v, axis, [(i, i ^ mask) for i in range(n)])


def cube_sum(v, axis):
    mask = 1
    while mask < lax.axis_size(axis):
        v = v + flip(v, axis, mask)
        mask *= 2
    return v


def after(v, *deps):
    return lax.optimization_barrier((v,) + deps)[0]


def ring_pieces(v):
    out = [v]
    for _ in range(1, lax.axis_size("ctx")):
        out.append(rotate(out[-1], "ctx", 1))
    return out


def all_pieces(ring, *start):
    nc, nf = lax.axis_size("ctx"), lax.axis_size("fsdp")
    c, f = lax.axis_index("ctx"), lax.axis_index("fsdp")
    pieces, places = [], []
    for step, piece in enumerate(ring):
        owner = lax.rem(c - step + nc, nc)
        if start:
            piece = after(piece, *start)
        for j in range(nf):
            if j:
                piece = rotate(piece, "fsdp", 1)
            pieces.append(piece)
            places.append(lax.rem(f - j + nf, nf) * nc + owner)
    return pieces, jnp.stack(places).astype(jnp.int32)


def assemble(pieces, places):
    rows = pieces[0].shape[0]
    whole = jnp.zeros((rows * len(pieces), pieces[0].shape[1]), pieces[0].dtype)
    for i, piece in enumerate(pieces):
        whole = lax.dynamic_update_slice_in_dim(whole, piece, places[i] * rows, 0)
    return whole


class Spread:
    def __init__(self, g, runs):
        nc, nf = lax.axis_size("ctx"), lax.axis_size("fsdp")
        c, f = lax.axis_index("ctx"), lax.axis_index("fsdp")
        self.g, self.rows, self.runs = g, g.shape[0] // (nc * nf), runs
        self.place = lambda k, step: lax.rem(f + k, nf) * nc + lax.rem(c - step + nc, nc)
        self.come = []
        for run in runs:
            self.send(g, run)

    def more(self, run, order):
        waits = list(order.waits)
        self.send(order.enter(self.g), run)
        order.waits = waits

    def send(self, g, run):
        nc, nf, f = lax.axis_size("ctx"), lax.axis_size("fsdp"), lax.axis_index("fsdp")
        take = lambda at, count: lax.dynamic_slice_in_dim(g, at * self.rows, count * self.rows, 0)
        for k in range(1, nf):
            if len(run) == nc:
                sent = take(lax.rem(f + k, nf) * nc, nc)
            else:
                sent = jnp.concatenate([take(self.place(k, step), 1) for step in run])
            self.sent = sent
            self.come.append((run, rotate(sent, "fsdp", k)))

    def landed(self, step):
        return [v for run, v in self.come if step in run]

    def terms(self, step):
        nc, c = lax.axis_size("ctx"), lax.axis_index("ctx")
        out = [(self.g, self.place(0, step))]
        for run, v in self.come:
            if step in run:
                out.append((v, lax.rem(c - step + nc, nc) if len(run) == nc else run.index(step)))
        return out


def block_sum(groups, last, rows, dtype, order, apart=False):
    arrays = [a for group in groups for a, _ in group]
    places = jnp.stack([jnp.asarray(at, jnp.int32) for group in groups for _, at in group])
    widths = [group[0][0].shape[1] for group in groups]
    specs = [pl.BlockSpec((rows, a.shape[1]), lambda i, p, j=j: (p[j], 0)) for j, a in enumerate(arrays)]
    if last is not None:
        arrays.append(last)
        specs.append(pl.BlockSpec(last.shape, lambda i, p: (0, 0)))
        order.land(last)
    deps = order.deps()
    outs = widths if apart else [sum(widths)]

    def kernel(places_ref, *refs):
        at, lo = 0, 0
        for i, (group, width) in enumerate(zip(groups, widths)):
            total = sum(r[...].astype(f32) for r in refs[at : at + len(group)])
            if last is not None:
                total = total + refs[len(arrays) - 1][:, lo : lo + width].astype(f32)
            if apart:
                refs[i - len(groups)][...] = total.astype(dtype)
            else:
                refs[-1][:, lo : lo + width] = total.astype(dtype)
            at, lo = at + len(group), lo + width

    out = pl.pallas_call(
        kernel,
        grid_spec=pltpu.PrefetchScalarGridSpec(
            num_scalar_prefetch=1,
            grid=(1,),
            in_specs=specs + [pl.BlockSpec(memory_space=pl.ANY)] * len(deps),
            out_specs=[pl.BlockSpec((rows, w), lambda i, p: (0, 0)) for w in outs],
        ),
        out_shape=[jax.ShapeDtypeStruct((rows, w), dtype) for w in outs],
        compiler_params=pltpu.CompilerParams(vmem_limit_bytes=16 * 2**20),
        cost_estimate=COST,
    )(places, *arrays, *deps)
    order.leave(out[0])
    return out if apart else out[0]


def finish(ring, rest, shapes, order):
    ring.at += 1
    terms = [t for one in ring.spreads for t in one.terms(ring.at)]
    rows = ring.spreads[0].rows
    order.land(ring.come)
    deps = order.deps()
    places = jnp.stack([jnp.asarray(at, jnp.int32) for _, at in terms])
    specs = [pl.BlockSpec((rows, a.shape[1]), lambda i, p, j=j: (p[j], 0)) for j, (a, _) in enumerate(terms)]
    whole = lambda shape: pl.BlockSpec(shape, lambda i, p, n=len(shape): (0,) * n)

    def kernel(*refs):
        n = 3 + len(terms)
        finish_kernel(*refs[:n], *refs[n + len(deps) :], terms=len(terms))

    return pl.pallas_call(
        kernel,
        grid_spec=pltpu.PrefetchScalarGridSpec(
            num_scalar_prefetch=1,
            grid=(1,),
            in_specs=specs
            + [whole(ring.come.shape), whole(rest.shape)]
            + [pl.BlockSpec(memory_space=pl.ANY)] * len(deps),
            out_specs=[whole(s) for s in shapes],
        ),
        out_shape=[jax.ShapeDtypeStruct(s, f32) for s in shapes],
        compiler_params=pltpu.CompilerParams(vmem_limit_bytes=16 * 2**20),
        cost_estimate=COST,
    )(places, *[a for a, _ in terms], ring.come, rest, *deps)


class Ring:
    def __init__(self, spreads, order):
        self.spreads, self.at = spreads, 0
        self.total, self.come = None, None
        self.step(order)

    def done(self):
        return self.at == lax.axis_size("ctx")

    def step(self, order):
        if self.done():
            return
        self.at += 1
        groups = [one.terms(self.at) for one in self.spreads]
        last = lax.axis_size("ctx") == self.at
        self.total = block_sum(groups, self.come, self.spreads[0].rows, f32 if last else bf16, order, last)
        if not last:
            self.come = rotate(self.total, "ctx", 1)


def halve_kernel(near, come, near_ref, away_ref):
    total = near[...].astype(f32) + come[...].astype(f32)
    near_ref[...] = total[:, : near_ref.shape[1]]
    away_ref[...] = total[:, near_ref.shape[1] :].astype(bf16)


def add_kernel(a, b, out_ref):
    out_ref[...] = a[...] + b[...]


def add_both_kernel(a, b, come, a_ref, b_ref):
    wide = a_ref.shape[1]
    a_ref[...] = a[...] + come[:, :wide]
    b_ref[...] = b[...] + come[:, wide:]


class Cube:
    def __init__(self, near, away):
        self.near, self.away, self.mask = near, away, 1
        self.come = flip(away, "tp", 1)

    def halve(self, order):
        seqs, rows, wide = self.near.shape
        while self.mask * 2 < lax.axis_size("tp"):
            wide //= 2
            order.land(self.come)
            out = (seqs, rows, wide)
            self.near, self.away = call(
                halve_kernel,
                0,
                seqs,
                [(self.near, 0), (self.come, 0)],
                [(out, f32, True), (out, bf16, True)],
                deps=order.deps(),
            vmem=16,
            )
            order.leave(self.away)
            self.mask *= 2
            self.come = flip(self.away, "tp", self.mask)

    def total(self):
        return self.near + self.come.astype(f32)


class Hops:
    def __init__(self, v, own, axes=("tp", "fsdp", "ctx")):
        self.v, self.own = v, own
        hops = {axis: [(axis, 1 << i) for i in range(lax.axis_size(axis).bit_length() - 1)] for axis in axes}
        self.todo = [hop for axis in axes for hop in hops[axis]]
        self.come, self.both = None, False

    def go(self, order):
        if self.come is not None:
            order.land(self.come)
            if self.both:
                self.v, self.own = small_call(
                    add_both_kernel, [self.v, self.own, self.come], [(self.v.shape, f32), (self.own.shape, f32)], order
                )
            else:
                self.v = small_call(add_kernel, [self.v, self.come], [(self.v.shape, f32)], order)[0]
            order.leave(self.v)
            self.come = None
        if self.todo:
            axis, mask = self.todo.pop(0)
            self.both = axis != "tp" and self.own is not None
            self.come = flip(jnp.concatenate([self.v, self.own], 1) if self.both else self.v, axis, mask)

    def end(self, order):
        while self.come is not None:
            self.go(order)
        return self.v


def small_call(kernel, operands, outs, order, scalar=None, scratch=()):
    deps = order.deps()
    n_in = len(operands) + (scalar is not None)

    def run(*refs):
        kernel(*refs[:n_in], *refs[n_in + len(deps) :])

    vmem = pl.BlockSpec(memory_space=pltpu.VMEM)
    return pl.pallas_call(
        run,
        in_specs=([] if scalar is None else [pl.BlockSpec(memory_space=pltpu.SMEM)])
        + [vmem] * len(operands)
        + [pl.BlockSpec(memory_space=pl.ANY)] * len(deps),
        out_specs=[vmem] * len(outs),
        out_shape=[jax.ShapeDtypeStruct(*o) for o in outs],
        scratch_shapes=list(scratch),
        compiler_params=pltpu.CompilerParams(vmem_limit_bytes=16 * 2**20),
        cost_estimate=COST,
    )(*([] if scalar is None else [scalar]), *operands, *deps)


class Chain:
    def __init__(self, parts, decay, reverse):
        self.parts, self.decay, self.reverse = parts, decay, reverse
        self.hop, self.last, self.entering = 0, None, []

    def send(self, order):
        n = lax.axis_size("ctx")
        self.hop += 1
        if self.hop >= n:
            return
        out = self.parts
        if self.last is not None:
            order.land(self.last)
            out = small_call(
                combine_kernel, [self.parts, self.decay, self.last], [(out.shape, bf16)], order
            )[0]
            order.leave(out)
        hop = self.hop
        pair = (n - hop, n - hop - 1) if self.reverse else (hop - 1, hop)
        self.last = lax.ppermute(out, "ctx", [pair])
        self.entering.append(self.last)

    def land(self, order):
        order.land(self.last)


class Order:
    def __init__(self):
        self.waits = []

    def land(self, *arrays):
        self.waits += arrays

    def enter(self, v):
        v = after(v, *self.waits)
        self.waits = []
        return v

    def deps(self):
        waits, self.waits = self.waits, []
        return waits

    def leave(self, v):
        self.waits = self.waits + [v]
        return v


def dot(a, b, dims=NN):
    return lax.dot_general(a, b, dims, preferred_element_type=f32)


def split(v, terms):
    out = []
    for i in range(terms):
        t = v.astype(bf16)
        out.append(t)
        if i + 1 < terms:
            v = v - t.astype(f32)
    return out


def constants(inner, q):
    heads = jnp.arange(LANES, dtype=jnp.int32)[:, None] == jnp.arange(inner, dtype=jnp.int32)[None] // HEADDIM
    spread = heads.astype(bf16)
    tri = jnp.arange(q, dtype=jnp.int32)[None] <= jnp.arange(q, dtype=jnp.int32)[:, None]
    return jnp.concatenate([spread, spread]), spread.T, tri.astype(bf16)


def widen(v, spread):
    return dot(jnp.concatenate(split(v, 2), 1), spread[...])


def narrow(v, gather, terms):
    out = None
    for t in split(v, terms):
        s = dot(t, gather[...])
        out = s if out is None else out + s
    return out


def tri_sum(tri, v, dims=NN):
    out = None
    for t in split(v, 3):
        s = dot(tri[...], t, dims)
        out = s if out is None else out + s
    return out


def one_of(refs):
    total = refs[0][...]
    for r in refs[1:]:
        total = total + r[...]
    return total


def halves(v):
    lane = lax.broadcasted_iota(jnp.int32, v.shape, 1)
    zero = jnp.zeros_like(v)
    return jnp.where(lane < HEADDIM, v, zero), jnp.where(lane >= HEADDIM, v, zero)


def sigmoid(v):
    return lax.logistic(v)


def gather_rows(places, pieces, whole):
    rows = pieces[0].shape[0]
    for i, piece in enumerate(pieces):
        whole[pl.ds(pl.multiple_of(places[i] * rows, 16), rows), :] = piece[...]


def project_kernel(nx, start, w, taps, bias, head_par, spread, tri, *refs, inner, conv):
    u_ref, slope_ref, act_ref, xdt_ref, dtl_ref, state_ref, dec_ref = refs[-7:]
    q = start.shape[0]
    u = dot(nx[...], w[...])
    u_ref[...] = u[:, :conv].astype(bf16)
    at = lax.broadcasted_iota(jnp.int32, (q, 1), 0)
    begin = start[...]
    since = jnp.broadcast_to(at - begin, (q, LANES))
    keep = [jnp.where(since >= j, 1.0, 0.0) for j in range(CONV)]
    for lo in range(0, conv, LANES):
        cols = slice(lo, lo + LANES)
        ut = u[:, cols]
        acc = bias[0:1, cols] + taps[CONV - 1 : CONV, cols] * ut[HALO:]
        for j in range(1, CONV):
            window = ut[HALO - j : HALO - j + q]
            acc = acc + taps[CONV - 1 - j : CONV - j, cols] * (window * keep[j])
        sig = sigmoid(acc)
        silu = acc * sig
        act_ref[:, cols] = silu.astype(bf16)
        slope_ref[:, cols] = (sig + silu * (1.0 - sig)).astype(bf16)
    v = u[HALO:, conv:] + head_par[0:1, :]
    dt = jnp.maximum(v, 0.0) + jnp.log1p(jnp.exp(-jnp.abs(v)))
    cum = tri_sum(tri, -dt * jnp.exp(head_par[1:2, :]))
    dtl_ref[:, :LANES] = dt
    dtl_ref[:, LANES:] = cum
    end = cum[q - 1 : q, :]
    begin_last = begin[q - 1 : q, :]
    tail = jnp.where(begin == begin_last, jnp.exp(end - cum), 0.0)
    xh = act_ref[:, :inner].astype(f32)
    xdt = (xh * widen(dt, spread)).astype(bf16)
    xdt_ref[...] = xdt
    weighted = (xdt.astype(f32) * widen(tail, spread)).astype(bf16)
    b = act_ref[:, inner : inner + STATE]
    state_ref[...] = dot(b, weighted, TN).astype(bf16)
    total = jnp.where(begin_last < 0, jnp.exp(end), 0.0)
    dec_ref[...] = widen(jnp.broadcast_to(total, (8, LANES)), spread)[0:1]


def project_first_kernel(places, nx, start, taps, bias, head_par, spread, tri, *refs, pieces, inner, conv):
    w = refs[-1]

    @pl.when(pl.program_id(0) == 0)
    def _():
        gather_rows(places, refs[:pieces], w)

    project_kernel(nx, start, w, taps, bias, head_par, spread, tri, *refs[pieces:-1], inner=inner, conv=conv)


def combine_kernel(parts, decay, last, out_ref):
    out_ref[...] = (parts[...].astype(f32) + decay[...] * last[...].astype(f32)).astype(bf16)


def score_mask(begin_col, q):
    r = lax.broadcasted_iota(jnp.int32, (q, q), 0)
    c = lax.broadcasted_iota(jnp.int32, (q, q), 1)
    return (c <= r) & (c >= begin_col)


def score_mask_t(begin_row, q):
    r = lax.broadcasted_iota(jnp.int32, (q, q), 0)
    c = lax.broadcasted_iota(jnp.int32, (q, q), 1)
    return (r <= c) & (r >= begin_row)


def local_kernel(act, xdt, dtl, start, y_ref, *, inner):
    q = start.shape[0]
    b = act[:, inner : inner + STATE]
    c = act[:, inner + STATE : inner + 2 * STATE]
    scores = jnp.where(score_mask(start[...], q), dot(c, b, NT), 0.0)
    cum = dtl[:, LANES:]
    cum_t = cum.T
    for pair in range(inner // LANES):
        cols = slice(pair * LANES, (pair + 1) * LANES)
        weights = []
        for h in (2 * pair, 2 * pair + 1):
            gap = jnp.minimum(cum[:, h : h + 1] - cum_t[h : h + 1, :], 0.0)
            weights.append((jnp.exp(gap) * scores).astype(bf16))
        even, odd = halves(xdt[:, cols])
        y_ref[:, cols] = dot(weights[0], even) + dot(weights[1], odd)


def gate_sums_kernel(nx, cot, y_in, act, dtl, start, state, w, rows, spread, y_ref, z_ref, dh_ref, sums_ref, *, inner):
    q = start.shape[0]
    c = act[:, inner + STATE : inner + 2 * STATE]
    zz = dot(nx[HALO:], w[:, :inner])
    z_ref[...] = zz
    d_hidden = dot(cot[...], w[:, inner:])
    dh_ref[...] = d_hidden
    into = widen(jnp.where(start[...] < 0, jnp.exp(dtl[:, LANES:]), 0.0), spread)
    y = y_in[...] + into * dot(c, one_of(state))
    y_ref[...] = y
    gated = (y + rows[0:1, :] * act[:, :inner].astype(f32)) * (zz * sigmoid(zz))
    e = d_hidden * rows[1:2, :]
    ones = jnp.ones((8, inner), bf16)
    sq = dot(ones, (gated * gated).astype(bf16), NT)
    eg = dot(ones, (e * gated).astype(bf16), NT)
    row = lax.broadcasted_iota(jnp.int32, (8, q), 0)
    sums_ref[...] = jnp.where(row == 0, sq, eg)


def gate_sums_first_kernel(places, nx, cot, y_in, act, dtl, start, *refs, pieces, hops, inner):
    state, (rows, spread), refs = refs[:hops], refs[hops : hops + 2], refs[hops + 2 :]
    y_ref, z_ref, dh_ref, sums_ref, w = refs[pieces], refs[pieces + 1], refs[pieces + 2], refs[pieces + 3], refs[-1]

    @pl.when(pl.program_id(0) == 0)
    def _():
        gather_rows(places, refs[:pieces], w)

    gate_sums_kernel(
        nx, cot, y_in, act, dtl, start, state, w, rows, spread, y_ref, z_ref, dh_ref, sums_ref, inner=inner
    )


def gate_sums_next_kernel(nx, cot, y_in, act, dtl, start, *refs, hops, inner):
    gate_sums_kernel(nx, cot, y_in, act, dtl, start, refs[:hops], *refs[hops:], inner=inner)


def mix_kernel(rank, hidden, w, near_ref, away_ref):
    seqs, q, cols = near_ref.shape
    k = pl.program_id(0)
    out = dot(hidden[...].reshape(seqs * q, hidden.shape[2]), w[...], NT).astype(bf16).reshape(seqs, q, cols)

    @pl.when(lax.rem(k, 2) == 0)
    def _():
        near_ref[...] = out

    @pl.when(lax.rem(k, 2) == 1)
    def _():
        away_ref[...] = out


def out_back_kernel(rank, du, rim, tap, nx, z_part, w_in, near_ref, away_ref, own, part):
    seqs, q = du.shape[0], du.shape[1] - HALO
    cols = w_in.shape[0]
    tp = near_ref.shape[2] * 2 // cols
    k = pl.program_id(0)

    @pl.when(k == 0)
    def _():
        for s in range(seqs):
            own[s * q : (s + 1) * q - 16, :] = du[s, HALO:q, :]
            edge = du[s, q : q + HALO, :].astype(f32)
            own[(s + 1) * q - 16 : (s + 1) * q, :] = (edge + rim[s].astype(f32)).astype(bf16)
        part[...] = jnp.zeros_like(part)

    out = dot(own[...], w_in[...], NT)
    row16 = lax.broadcasted_iota(jnp.int32, (16, cols), 0)
    inner = tap.shape[2] - 2 * STATE
    for s in range(seqs):
        mine = out[s * q : (s + 1) * q] + z_part[s, HALO:, :].astype(f32)
        prod = mine * nx[s, HALO:, :].astype(f32)
        folded = prod[:, :LANES]
        for lo in range(LANES, cols, LANES):
            folded = folded + prod[:, lo : lo + LANES]
        part[s * q : (s + 1) * q, :] += folded
        gains = jnp.broadcast_to(jnp.sum(prod, axis=0, keepdims=True), (8, cols))
        bc_taps = jnp.concatenate([tap[s][:, inner:], jnp.zeros((8, cols - 2 * STATE), f32)], 1)
        extra = jnp.concatenate([gains, bc_taps], 0).astype(bf16)
        for j in range(tp):
            to = slice(j // 2 * cols, (j // 2 + 1) * cols)

            @pl.when(k == j)
            def _():
                (away_ref if j % 2 else near_ref)[s, :q, to] = mine.astype(bf16)
                (away_ref if j % 2 else near_ref)[s, q:, to] = extra

    @pl.when(k == tp - 1)
    def _():
        ones = jnp.ones((16, LANES), bf16)
        for s in range(seqs):
            total = None
            for t in split(part[s * q : (s + 1) * q, :], 2):
                one = dot(ones, t, NT)
                total = one if total is None else total + one
            total = jnp.concatenate([total, jnp.zeros((16, cols - q), f32)], 1)
            for j in range(tp):
                to = slice(j // 2 * cols, (j // 2 + 1) * cols)
                ref = away_ref if j % 2 else near_ref
                ref[s, q:, to] = jnp.where(row16 == 0, total, ref[s, q:, to].astype(f32)).astype(bf16)


def pack_kernel(extra, *refs, chunks, inner):
    taps, heads, gates = refs[:chunks], refs[chunks : 2 * chunks], refs[2 * chunks : 3 * chunks]
    out = refs[-1]
    total = lambda refs: sum(jnp.sum(r[...], axis=0) for r in refs)
    more = jnp.sum(extra[...], axis=0)
    cols = more.shape[1]
    out[:, :inner] = total(taps)[:, :inner]
    out[:, inner : inner + LANES] = total(heads)
    out[:, inner + LANES : 2 * inner + LANES] = total(gates)
    out[:, 2 * inner + LANES : 2 * inner + LANES + cols] = more[:8]
    out[:, 2 * inner + LANES + cols :] = more[8:, : 2 * STATE]


def unpack_kernel(
    v, come, gain, gather, conv_ref, convb_ref, bc_ref, bcb_ref, dtb_ref, alog_ref, skip_ref, gate_ref, gain_ref
):
    inner, cols = gate_ref.shape[1], gain_ref.shape[1]
    heads = skip_ref.shape[1]
    own = v[...] + come[...]
    taps = own[:, :inner]
    conv_ref[...] = taps[:CONV]
    convb_ref[...] = taps[CONV : CONV + 1]
    head = own[:, inner : inner + LANES]
    dtb_ref[...] = head[0:1, :heads]
    alog_ref[...] = head[1:2, :heads]
    lo = 2 * inner + LANES
    gate = own[:, inner + LANES : lo]
    gate_ref[...] = gate[0:1]
    skip_ref[...] = narrow(gate, gather, 3)[1:2, :heads]
    gain_ref[...] = own[1:2, lo : lo + cols] / gain[0:1, :]
    bc = own[:, lo + cols :]
    bc_ref[...] = bc[:CONV]
    bcb_ref[...] = bc[CONV : CONV + 1]


def tokens_kernel(near, come, own, cot, inv, gain, out_ref, extra_ref):
    q, cols = out_ref.shape
    total = near[...] + come[...].astype(f32)
    extra_ref[...] = total[q:]
    both = jnp.broadcast_to(total[q : q + 8, :q][0:1], (8, q)).T[:, 0:1]
    hat = own[...].astype(f32) * inv[...]
    out_ref[...] = cot[...].astype(f32) + inv[...] * (total[:q] * gain[0:1, :] - hat * (both / D))


def finish_kernel(places, *refs, terms):
    come, rest = refs[terms], refs[terms + 1]
    zx_ref, bc_ref, dt_ref = refs[-3:]
    inner, wide, heads = zx_ref.shape[2], bc_ref.shape[1], dt_ref.shape[1]
    total = sum(r[...].astype(f32) for r in refs[:terms]) + come[...].astype(f32)
    zx_ref[:, 0, :] = rest[...]
    zx_ref[:, 1, :] = total[:, :inner]
    bc_ref[...] = total[:, inner : inner + wide]
    dt_ref[...] = total[:, inner + wide : inner + wide + heads]


def norm_kernel(x, halo, gain, nx_ref, inv_ref):
    wide = x[...].astype(f32)
    width = wide.shape[1]
    inv = lax.rsqrt(jnp.mean(wide * wide, axis=-1, keepdims=True) + NORM_EPS)
    inv_ref[...] = inv
    nx_ref[HALO:, :] = (wide * inv * gain[0:1, :]).astype(bf16)
    edge = halo[...].astype(f32)
    inv = lax.rsqrt(jnp.mean(edge * edge, axis=-1, keepdims=True) + NORM_EPS)
    nx_ref[:HALO, :] = (edge * inv * gain[0:1, :]).astype(bf16)


def gate_kernel(y_in, act, dtl, start, z, dh, sums, rows, spread, *refs, inner):
    hidden_ref, dz_ref, dy_ref, dstate_ref, grads_ref = refs[-5:]
    xh = act[:, :inner].astype(f32)
    y = y_in[...] + rows[0:1, :] * xh
    zz = z[...].astype(f32)
    sig = sigmoid(zz)
    silu = zz * sig
    gated = y * silu
    gain = rows[1:2, :]
    d_hidden = dh[...].astype(f32)
    sums_t = sums[...].T
    inv = lax.rsqrt(sums_t[:, 0:1] / INNER + NORM_EPS)
    back = sums_t[:, 1:2] * (inv * inv * inv) / INNER
    scaled = gated * inv
    hidden_ref[...] = (scaled * gain).astype(bf16)
    dg = inv * (d_hidden * gain) - gated * back
    dy = (dg * silu).astype(bf16)
    dy_ref[...] = dy
    dz_ref[:HALO, :] = jnp.zeros((HALO, inner), bf16)
    dz_ref[HALO:, :] = (dg * y * sig * (1.0 + zz * (1.0 - sig))).astype(bf16)
    gate_row = jnp.sum(d_hidden * scaled, axis=0, keepdims=True)
    dy_wide = dy.astype(f32)
    skip_row = jnp.sum(dy_wide * xh, axis=0, keepdims=True)
    row = lax.broadcasted_iota(jnp.int32, (8, inner), 0)
    grads_ref[...] = jnp.where(row == 0, gate_row, jnp.where(row == 1, skip_row, 0.0))
    into = widen(jnp.where(start[...] < 0, jnp.exp(dtl[:, LANES:]), 0.0), spread)
    c = act[:, inner + STATE : inner + 2 * STATE]
    dstate_ref[...] = dot(c, (into * dy_wide).astype(bf16), TN).astype(bf16)


def local_back_kernel(act, xdt, dtl, start, start_row, dy, *refs, hops, inner):
    state, (spread, dx_ref, dbc_ref) = refs[:hops], refs[hops:]
    q = start.shape[0]
    b = act[:, inner : inner + STATE]
    c = act[:, inner + STATE : inner + 2 * STATE]
    mask = score_mask_t(start_row[...], q)
    scores = jnp.where(mask, dot(b, c, NT), 0.0)
    cum = dtl[:, LANES:]
    cum_t = cum.T
    total = jnp.zeros((q, q), f32)
    for pair in range(inner // LANES):
        cols = slice(pair * LANES, (pair + 1) * LANES)
        dy_pair = dy[:, cols]
        x_even, x_odd = halves(xdt[:, cols])
        dy_even, dy_odd = halves(dy_pair)
        out = None
        for h, x_one, dy_one in ((2 * pair, x_even, dy_even), (2 * pair + 1, x_odd, dy_odd)):
            decay = jnp.exp(jnp.minimum(cum_t[h : h + 1, :] - cum[:, h : h + 1], 0.0))
            total = total + dot(x_one, dy_pair, NT) * decay
            term = dot((decay * scores).astype(bf16), dy_one)
            out = term if out is None else out + term
        dx_ref[:, cols] = out
    d_scores = jnp.where(mask, total, 0.0).astype(bf16)
    into = widen(jnp.where(start[...] < 0, jnp.exp(cum), 0.0), spread)
    weighted = (into * dy[...].astype(f32)).astype(bf16)
    dbc_ref[:, :STATE] = dot(d_scores, c)
    dbc_ref[:, STATE:] = dot(d_scores, b, TN) + dot(weighted, one_of(state), NT)


def conv_back_kernel(act, xdt, dtl, start, dy, y_in, dx, dbc, slope, u, dec, *refs, hops, inner, conv):
    state, later, refs = refs[:hops], refs[hops : 2 * hops], refs[2 * hops :]
    taps, rows, head_par, spread, gather, tri = refs[:6]
    du_ref, rim_ref, tap_ref, head_ref, dact = refs[-5:]
    q = start.shape[0]
    begin = start[...]
    b = act[:, inner : inner + STATE]
    dt, cum = dtl[:, :LANES], dtl[:, LANES:]
    end = cum[q - 1 : q, :]
    begin_last = begin[q - 1 : q, :]
    tail = widen(jnp.where(begin == begin_last, jnp.exp(end - cum), 0.0), spread)
    x_dt = xdt[...].astype(f32)
    d_y = dy[...].astype(f32)
    g = one_of(later)
    dx_tail = tail * dot(b, g)
    dact[:, inner : inner + STATE] = dbc[:, :STATE] + dot((x_dt * tail).astype(bf16), g, NT)
    dact[:, inner + STATE :] = dbc[:, STATE:]
    dx_local = dx[...]
    dx_all = dx_local + dx_tail
    dact[:, :inner] = dx_all * widen(dt, spread) + rows[0:1, :] * d_y
    flux_near = narrow(d_y * y_in[...] - x_dt * dx_local, gather, 3)
    flux_tail = narrow(x_dt * dx_tail, gather, 2)
    d_dt = narrow(dx_all * act[:, :inner].astype(f32), gather, 2)
    through = jnp.sum(dec[...] * (g.astype(f32) * one_of(state).astype(f32)), axis=0, keepdims=True)
    through = narrow(jnp.broadcast_to(through, (8, inner)), gather, 2)[0:1]
    d_log = tri_sum(tri, flux_near, TN) + (tri_sum(tri, flux_tail) - flux_tail) + through
    rate = jnp.exp(head_par[1:2, :])
    d_raw = (d_dt - rate * d_log) * (1.0 - jnp.exp(-dt))
    du_ref[:HALO, conv:] = jnp.zeros((HALO, LANES), bf16)
    rim_ref[:, conv:] = jnp.zeros((HALO, LANES), bf16)
    du_ref[HALO:, conv:] = d_raw.astype(bf16)
    bias_row = jnp.sum(d_raw, axis=0, keepdims=True)
    log_row = -jnp.sum(d_log * dt * rate, axis=0, keepdims=True)
    row = lax.broadcasted_iota(jnp.int32, (8, LANES), 0)
    head_ref[...] = jnp.where(row == 0, bias_row, jnp.where(row == 1, log_row, 0.0))
    since = lax.broadcasted_iota(jnp.int32, (q, LANES), 0) - begin
    keep = [jnp.where(since >= j, 1.0, 0.0) for j in range(CONV)]
    zeros = jnp.zeros((HALO, LANES), f32)
    for lo in range(0, conv, LANES):
        cols = slice(lo, lo + LANES)
        dp = dact[:, cols] * slope[:, cols].astype(f32)
        ut = u[:, cols].astype(f32)
        moved = jnp.concatenate([zeros, dp], 0)
        total = taps[CONV - 1 : CONV, cols] * moved
        tap_rows = [jnp.sum(dp * ut[HALO:], axis=0, keepdims=True)]
        for j in range(1, CONV):
            moved = jnp.concatenate([zeros, dp * keep[j], zeros], 0)[j : j + q + HALO]
            tap_rows.append(jnp.sum(moved * ut, axis=0, keepdims=True))
            total = total + taps[CONV - 1 - j : CONV - j, cols] * moved
        du_ref[:, cols] = total.astype(bf16)
        rim_ref[:, cols] = total[:HALO].astype(bf16)
        out = jnp.sum(dp, axis=0, keepdims=True)
        for j in range(CONV):
            out = jnp.where(row == CONV - 1 - j, tap_rows[j], jnp.where(row == CONV, out, 0.0) if j == 0 else out)
        tap_ref[:, cols] = out


def call(kernel, first, count, ins, outs, shared=(), scalar=None, scratch=(), into=None, deps=(), vmem=34):
    def spec(shape, base):
        block = (None,) + tuple(shape[1:])
        rest = (0,) * (len(shape) - 1)
        return pl.BlockSpec(block, lambda s: (s + base,) + rest)

    in_specs = [spec(a.shape, o) for a, o in ins]
    in_specs += [
        pl.BlockSpec(a.shape, lambda s, n=a.ndim: (0,) * n, pipeline_mode=pl.Buffered(1)) for a in shared
    ]
    operands = [a for a, _ in ins] + list(shared)
    if scalar is not None:
        in_specs.insert(0, pl.BlockSpec(memory_space=pltpu.SMEM))
        operands.insert(0, scalar)
    n_args = len(operands)
    operands += list(deps)
    in_specs += [pl.BlockSpec(memory_space=pl.ANY)] * len(deps)
    aliases = {}
    if into is not None:
        for i, buf in enumerate(into):
            if buf is not None:
                aliases[len(operands)] = i
                operands.append(buf)
                in_specs.append(pl.BlockSpec(memory_space=pl.ANY))
    n_in = len(operands)

    def run(*refs):
        kernel(*refs[:n_args], *refs[n_in:])

    return pl.pallas_call(
        run,
        grid=(count,),
        in_specs=in_specs,
        out_specs=[spec(s, first if whole else 0) if whole is not None else pl.BlockSpec(s, lambda i, n=len(s): (0,) * n) for s, _, whole in outs],
        out_shape=[jax.ShapeDtypeStruct(s, d) for s, d, _ in outs],
        scratch_shapes=list(scratch),
        input_output_aliases=aliases,
        compiler_params=pltpu.CompilerParams(vmem_limit_bytes=vmem * 2**20),
        cost_estimate=COST,
    )(*operands)


def call_slices(kernel, rank, tp, wholes, weights, outs, scratch=(), deps=()):
    specs, operands = [], []
    for a, cut in wholes:
        if cut:
            block = a.shape[:-1] + (a.shape[-1] // tp,)
            specs.append(pl.BlockSpec(block, lambda k, r, n=a.ndim: (0,) * (n - 1) + (r[0] ^ k,)))
        else:
            specs.append(pl.BlockSpec(a.shape, lambda k, r, n=a.ndim: (0,) * n))
        operands.append(a)
    for a, at, cols in weights:
        specs.append(pl.BlockSpec((a.shape[0] // tp, cols), lambda k, r, j=at // cols: (r[0] ^ k, j)))
        operands.append(a)
    n_args = len(operands) + 1
    operands += list(deps)
    specs += [pl.BlockSpec(memory_space=pl.ANY)] * len(deps)
    n_in = len(operands) + 1

    def run(*refs):
        kernel(*refs[:n_args], *refs[n_in:])

    out_specs = []
    for shape, _, cut in outs:
        n = len(shape)
        if cut is None:
            out_specs.append(pl.BlockSpec((shape[0], shape[1] // tp), lambda k, r: (0, r[0] ^ k)))
        elif cut:
            out_specs.append(
                pl.BlockSpec(shape[:-1] + (shape[-1] * 2 // tp,), lambda k, r, n=n: (0,) * (n - 1) + (k // 2,))
            )
        else:
            out_specs.append(pl.BlockSpec(shape, lambda k, r, n=n: (0,) * n))
    return pl.pallas_call(
        run,
        grid_spec=pltpu.PrefetchScalarGridSpec(
            num_scalar_prefetch=1,
            grid=(tp,),
            in_specs=specs,
            out_specs=out_specs,
            scratch_shapes=list(scratch),
        ),
        out_shape=[jax.ShapeDtypeStruct(s, d) for s, d, _ in outs],
        compiler_params=pltpu.CompilerParams(vmem_limit_bytes=28 * 2**20),
        cost_estimate=COST,
    )(rank, *operands)


def pack(taps, heads, gates, extra, order, inner):
    width = 2 * inner + LANES + extra.shape[2] + 2 * STATE
    (out,) = small_call(
        functools.partial(pack_kernel, chunks=len(taps), inner=inner),
        [extra, *taps, *heads, *gates],
        [((8, width), f32)],
        order,
    )
    return order.leave(out)


def per_device(
    tokens,
    segment_ids,
    in_gain,
    w_zx,
    w_bc,
    w_dt,
    dt_bias,
    a_log,
    skip_gain,
    conv_x,
    conv_x_bias,
    conv_bc,
    conv_bc_bias,
    gate_gain,
    w_out,
    cotangent,
):
    tp_count, tp_rank = lax.axis_size("tp"), lax.axis_index("tp")
    ctx_rank = lax.axis_index("ctx")
    seqs, q, width = tokens.shape
    inner = w_zx.shape[2]
    heads = w_dt.shape[1]
    conv = inner + 2 * STATE
    cols = width // tp_count
    n_tok = seqs * q
    chunks = 2 if seqs % 2 == 0 else 1
    per = seqs // chunks

    n_ctx = lax.axis_size("ctx")
    rank = tp_rank.astype(jnp.int32)[None]
    shape = lambda *s: (seqs,) + s
    part = lambda *s: (per,) + s
    order = Order()

    first_w = jnp.concatenate(
        [w_zx[:, 1, :], w_bc, jnp.pad(w_dt, ((0, 0), (0, LANES - heads)))], axis=1
    )
    ring_in = ring_pieces(first_w)
    halo = shift(jnp.pad(tokens[:, q - 8 :, :], ((0, 0), (8, 0), (0, 0))), "ctx", 1)
    pieces_in, places = all_pieces(ring_in)
    in_kernel = first_w.shape[0] % 16 == 0
    second_w = jnp.concatenate([after(w_zx, first_w)[:, 0, :], w_out.T], axis=1)
    ring_rest = ring_pieces(after(second_w, ring_in[-1]))
    pieces_rest, _ = all_pieces(ring_rest, pieces_in[-1])
    spread, gather, tri = constants(inner, q)
    if not in_kernel:
        w_in, w_rest = assemble(pieces_in, places), assemble(pieces_rest, places)

    gain = jnp.broadcast_to(in_gain.astype(f32)[None], (8, width))
    bulk = None
    order.land(halo)
    for g in range(chunks):
        order.land(*ring_in[g + 1 : g + 2], *pieces_in[2 * g + 1 : 2 * g + 2])
        bulk = call(
            norm_kernel,
            g * per,
            per,
            [(tokens, g * per), (halo, g * per)],
            deps=order.deps(),
            vmem=16,
            outs=[(shape(q + HALO, width), bf16, True), (shape(q, 1), f32, True)],
            shared=(gain,),
            into=bulk,
        )
        order.leave(bulk[1])
    nx, inv_rms = bulk

    begin = segment_ids - ctx_rank * q
    start = begin[:, :, None]
    start_row = begin[:, None, :]
    taps = jnp.concatenate([conv_x, conv_bc], axis=1).astype(f32)
    bias = jnp.concatenate([conv_x_bias, conv_bc_bias]).astype(f32)[None]
    head_par = jnp.pad(jnp.stack([dt_bias, a_log]), ((0, 6), (0, LANES - heads)))
    rows = jnp.pad(jnp.stack([jnp.repeat(skip_gain, HEADDIM), gate_gain.astype(f32)]), ((0, 6), (0, 0)))

    states, decs, kept, y_local = [], [], [], []
    landing = lambda i: pieces_rest[min(i, len(pieces_rest) - 1)]
    for g in range(chunks):
        o = g * per
        order.land(ring_rest[min(g + 1, n_ctx - 1)])
        if g:
            order.land(landing(2 * g - 1))
        first = g == 0 and in_kernel
        given = [taps, bias, head_par, spread, tri]
        outs = [
            (part(q + HALO, conv), bf16, False),
            (part(q, conv), bf16, False),
            (part(q, conv), bf16, False),
            (part(q, inner), bf16, False),
            (part(q, 2 * LANES), f32, False),
            (part(STATE, inner), bf16, False),
            (part(1, inner), f32, False),
        ]
        if first:
            kernel = functools.partial(project_first_kernel, pieces=len(pieces_in), inner=inner, conv=conv)
        else:
            kernel = functools.partial(project_kernel, inner=inner, conv=conv)
        out = call(
            kernel,
            o,
            per,
            [(nx, o), (start, o)],
            outs + [((width, conv + LANES), bf16, None)] if first else outs,
            shared=given + pieces_in if first else [w_in] + given,
            scalar=places if first else None,
            deps=order.deps(),
            vmem=34,
        )
        if first:
            w_in = out[7]
        kept.append(out[:5])
        decs.append(order.leave(out[6]))
        states.append(Chain(out[5], out[6], False))
        states[-1].send(order)

    if n_ctx > 2:
        states[0].send(order)
    for g in range(chunks):
        u, slope, act, xdt, dtl = kept[g]
        if g == 0:
            order.land(ring_rest[min(chunks + 1, n_ctx - 1)], landing(2 * chunks - 1))
        y_local.append(
            order.leave(
                call(
                    functools.partial(local_kernel, inner=inner),
                    0,
                    per,
                    [(act, 0), (xdt, 0), (dtl, 0), (start, g * per)],
                    deps=order.deps(),
            vmem=16,
                    outs=[(part(q, inner), f32, False)],
                )[0]
            )
        )
    if n_ctx > 2:
        for one in states[1:]:
            one.send(order)
    for hop in range(3, n_ctx):
        for i, one in enumerate(states):
            if hop == 3:
                order.land(landing(2 * chunks + 1 + 2 * i))
            one.send(order)

    scans = []
    for g in range(chunks):
        o = g * per
        u, slope, act, xdt, dtl = kept[g]
        first = g == 0 and in_kernel
        hops = len(states[g].entering)
        outs = [
            (part(q, inner), f32, False),
            (part(q, inner), f32, False),
            (part(q, inner), f32, False),
            (part(8, q), f32, False),
        ]
        if first:
            kernel = functools.partial(gate_sums_first_kernel, pieces=len(pieces_rest), hops=hops, inner=inner)
            given = [rows, spread] + pieces_rest
            outs = outs + [((width, width), bf16, None)]
        else:
            kernel = functools.partial(gate_sums_next_kernel, hops=hops, inner=inner)
            given = [w_rest, rows, spread]
        out = call(
            kernel,
            o,
            per,
            [(nx, o), (cotangent, o), (y_local[g], 0), (act, 0), (dtl, 0), (start, o)]
            + [(v, 0) for v in states[g].entering],
            outs,
            shared=given,
            scalar=places if first else None,
            deps=order.deps(),
            vmem=56,
        )
        if first:
            w_rest = out[4]
        scans.append(out[:4])
        order.leave(out[3])
    sums = cube_sum(jnp.concatenate([one[3] for one in scans]), "tp")

    bulk = [None] * 2
    d_ys = []
    chains, gate_rows = [], []
    for g in range(chunks):
        o = g * per
        u, slope, act, xdt, dtl = kept[g]
        y_scan, z, d_hidden, _ = scans[g]
        out = call(
            functools.partial(gate_kernel, inner=inner),
            o,
            per,
            [(y_scan, 0), (act, 0), (dtl, 0), (start, o), (z, 0), (d_hidden, 0), (sums, o)],
            deps=order.deps(),
            vmem=34,
            outs=[
                (shape(q, inner), bf16, True),
                (shape(q + HALO, inner), bf16, True),
                (part(q, inner), bf16, False),
                (part(STATE, inner), bf16, False),
                (part(8, inner), f32, False),
            ],
            shared=(rows, spread),
            into=None if g == 0 else bulk,
        )
        bulk = list(out[:2])
        d_ys.append(out[2])
        order.leave(out[3])
        chains.append(Chain(out[3], decs[g], True))
        chains[-1].send(order)
        gate_rows.append(out[4])
    hidden, d_z = bulk

    def hop(i):
        if i < len(chains):
            chains[i].send(order)

    def back_local(g):
        o = g * per
        u, slope, act, xdt, dtl = kept[g]
        out = call(
            functools.partial(local_back_kernel, hops=n_ctx - 1, inner=inner),
            0,
            per,
            [(act, 0), (xdt, 0), (dtl, 0), (start, o), (start_row, o), (d_ys[g], 0)]
            + [(v, 0) for v in states[g].entering],
            deps=order.deps(),
            vmem=16,
            outs=[(part(q, inner), f32, False), (part(q, 2 * STATE), f32, False)],
            shared=(spread,),
        )
        order.leave(out[1])
        return out

    nx2 = nx.reshape(seqs * (q + HALO), width)
    steps = tuple(range(1, n_ctx + 1))
    grad = order.leave(dot(nx2, order.enter(d_z).reshape(seqs * (q + HALO), inner), TN).astype(bf16))
    rest_z = Spread(grad, [steps])
    hop(0)
    hop(1)
    grad = order.leave(
        dot(cotangent.reshape(n_tok, width), order.enter(hidden).reshape(n_tok, inner), TN).astype(bf16)
    )
    rest_o = Spread(grad, [steps])
    back = [back_local(0)]
    hop(0)
    hop(1)
    back += [back_local(g) for g in range(1, chunks)]
    for _ in range(3, n_ctx):
        hop(0)
        hop(1)
    z_part = order.leave(dot(order.enter(d_z).reshape(seqs * (q + HALO), inner), w_rest[:, :inner], NT).astype(bf16))
    z_part = z_part.reshape(seqs, q + HALO, width)
    own = lax.dynamic_slice_in_dim(tokens, tp_rank * cols, cols, 2)

    bulk = [None] * 2
    tap_rows, head_rows = [], []
    for g in range(chunks):
        have = 0 if g == 0 else 1
        o = g * per
        u, slope, act, xdt, dtl = kept[g]
        chains[g].land(order)
        out = call(
            functools.partial(conv_back_kernel, hops=n_ctx - 1, inner=inner, conv=conv),
            o,
            per,
            [(act, 0), (xdt, 0), (dtl, 0), (start, o), (d_ys[g], 0), (scans[g][0], 0), (back[g][0], 0), (back[g][1], 0), (slope, 0), (u, 0), (decs[g], 0)]
            + [(v, 0) for v in states[g].entering + chains[g].entering],
            deps=order.deps(),
            outs=[
                (shape(q + HALO, conv + LANES), bf16, True),
                (shape(HALO, conv + LANES), bf16, True),
                (part(8, conv), f32, False),
                (part(8, LANES), f32, False),
            ],
            shared=(taps, rows, head_par, spread, gather, tri),
            scratch=[pltpu.VMEM((q, conv), f32)],
            into=None if g == 0 else bulk,
        )
        bulk = list(out[:2])
        tap_rows.append(out[2])
        head_rows.append(out[3])
        order.leave(out[3])
        if g == 0:
            ring = Ring([rest_z, rest_o], order)
    du = bulk[0]
    rim = rotate(bulk[1], "ctx", -1)

    grad = order.leave(dot(nx2, du.reshape(seqs * (q + HALO), conv + LANES), TN).astype(bf16))
    spread_in = Spread(grad, [steps[:1]])
    ring.step(order)
    spread_in.more(steps[1:], order)
    order.land(spread_in.sent)

    near, away = call_slices(
        mix_kernel,
        rank,
        tp_count,
        [(hidden, False)],
        deps=order.deps(),
        weights=[(w_rest, inner, inner)],
        outs=[(shape(q, width // 2), bf16, True), (shape(q, width // 2), bf16, True)],
    )
    order.leave(near)
    cube_mix = Cube(near, away)
    ring_in = Ring([spread_in], order)

    in_gain_own = lax.dynamic_slice_in_dim(in_gain, tp_rank * cols, cols, 0).astype(f32)
    order.land(rim)
    near, away = call_slices(
        out_back_kernel,
        rank,
        tp_count,
        [(du, False), (rim, False), (jnp.concatenate(tap_rows), False), (nx, True), (z_part, True)],
        [(w_in, 0, conv + LANES)],
        deps=order.deps(),
        outs=[
            (shape(q + HALO, width // 2), bf16, False),
            (shape(q + HALO, width // 2), bf16, False),
        ],
        scratch=[pltpu.VMEM((n_tok, conv + LANES), bf16), pltpu.VMEM((n_tok, LANES), f32)],
    )
    order.leave(near)
    cube = Cube(near, away)

    ring.step(order)
    cube.halve(order)
    ring_in.step(order)
    cube_mix.halve(order)
    while not ring.done():
        ring.step(order)
    grad_wz, grad_wo = ring.total
    while ring_in.at < n_ctx - 1:
        ring_in.step(order)
    gain_row = jnp.broadcast_to(in_gain_own[None], (8, cols))
    own_cot = lax.dynamic_slice_in_dim(cotangent, tp_rank * cols, cols, 2)
    order.land(cube.come)
    grad_tokens, extra = call(
        tokens_kernel,
        0,
        seqs,
        [(cube.near, 0), (cube.come, 0), (own, 0), (own_cot, 0), (inv_rms, 0)],
        [(shape(q, cols), f32, True), (shape(HALO, cols), f32, True)],
        shared=(gain_row,),
        deps=order.deps(),
        vmem=16,
    )
    order.leave(extra)
    small = Hops(pack(tap_rows, head_rows, gate_rows, extra, order, inner), None, ["fsdp", "ctx"])
    small.go(order)
    rows_own = grad_wz.shape[0]
    grad_zx, grad_bc, grad_dt = finish(
        ring_in, grad_wz, [(rows_own, 2, inner), (rows_own, 2 * STATE), (rows_own, heads)], order
    )
    bc_hops = Hops(grad_bc, None, ["tp"])
    bc_hops.go(order)
    small.go(order)
    order.land(cube_mix.come)
    mixed = order.leave((order.enter(own).astype(f32) + cube_mix.total()).astype(bf16))
    bc_hops.go(order)
    while small.todo:
        small.go(order)
    order.land(small.come)
    one = lambda n: ((1, n), f32)
    conv_own, convb_own, conv_all, convb_all, dtb, alog, skip, gate, gain_row = small_call(
        unpack_kernel,
        [small.v, small.come, gain_row, gather],
        [((CONV, inner), f32), one(inner), ((CONV, 2 * STATE), f32), one(2 * STATE), one(heads), one(heads), one(heads), one(inner), one(cols)],
        order,
    )
    grad_bc = bc_hops.end(order)

    return (
        mixed,
        grad_tokens,
        gain_row[0],
        grad_zx,
        grad_bc,
        grad_dt,
        dtb[0],
        alog[0],
        skip[0],
        conv_own,
        convb_own[0],
        conv_all,
        convb_all[0],
        gate[0],
        grad_wo.T,
    )


def solution(mesh):
    return jax.shard_map(
        per_device,
        mesh=mesh,
        in_specs=(
            P("fsdp", "ctx", None),
            P("fsdp", "ctx"),
            P(),
            P(("fsdp", "ctx"), None, "tp"),
            P(("fsdp", "ctx"), None),
            P(("fsdp", "ctx"), "tp"),
            P("tp"),
            P("tp"),
            P("tp"),
            P(None, "tp"),
            P("tp"),
            P(),
            P(),
            P("tp"),
            P("tp", ("fsdp", "ctx")),
            P("fsdp", "ctx", None),
        ),
        out_specs=(
            P("fsdp", "ctx", "tp"),
            P("fsdp", "ctx", "tp"),
            P("tp"),
            P(("fsdp", "ctx"), None, "tp"),
            P(("fsdp", "ctx"), None),
            P(("fsdp", "ctx"), "tp"),
            P("tp"),
            P("tp"),
            P("tp"),
            P(None, "tp"),
            P("tp"),
            P(),
            P(),
            P("tp"),
            P("tp", ("fsdp", "ctx")),
        ),
        check_vma=False,
    )
```

```python
import functools

import jax
import jax.numpy as jnp
from jax import lax
from jax.experimental import pallas as pl
from jax.experimental.pallas import tpu as pltpu
from jax.sharding import PartitionSpec as P

D = 1536
HEADDIM = 64
STATE = 128
CONV = 4
INNER = 3072
NORM_EPS = 1e-05
LANES = 128
HALO = 16
COST = pl.CostEstimate(flops=2 * 10**12, bytes_accessed=8 * 10**9, transcendentals=0)

bf16 = jnp.bfloat16
f32 = jnp.float32
NN = (((1,), (0,)), ((), ()))
NT = (((1,), (1,)), ((), ()))
TN = (((0,), (0,)), ((), ()))


def rotate(v, axis, steps):
    n = lax.axis_size(axis)
    return lax.ppermute(v, axis, [(i, (i + steps) % n) for i in range(n)])


def shift(v, axis, steps):
    n = lax.axis_size(axis)
    return lax.ppermute(v, axis, [(i, i + steps) for i in range(n) if 0 <= i + steps < n])


def flip(v, axis, mask):
    n = lax.axis_size(axis)
    return lax.ppermute(v, axis, [(i, i ^ mask) for i in range(n)])


def cube_sum(v, axis):
    mask = 1
    while mask < lax.axis_size(axis):
        v = v + flip(v, axis, mask)
        mask *= 2
    return v


def after(v, *deps):
    return lax.optimization_barrier((v,) + deps)[0]


def ring_pieces(v):
    out = [v]
    for _ in range(1, lax.axis_size("ctx")):
        out.append(rotate(out[-1], "ctx", 1))
    return out


def all_pieces(ring, *start):
    nc, nf = lax.axis_size("ctx"), lax.axis_size("fsdp")
    c, f = lax.axis_index("ctx"), lax.axis_index("fsdp")
    pieces, places = [], []
    for step, piece in enumerate(ring):
        owner = lax.rem(c - step + nc, nc)
        if start:
            piece = after(piece, *start)
        for j in range(nf):
            if j:
                piece = rotate(piece, "fsdp", 1)
            pieces.append(piece)
            places.append(lax.rem(f - j + nf, nf) * nc + owner)
    return pieces, jnp.stack(places).astype(jnp.int32)


def assemble(pieces, places):
    rows = pieces[0].shape[0]
    whole = jnp.zeros((rows * len(pieces), pieces[0].shape[1]), pieces[0].dtype)
    for i, piece in enumerate(pieces):
        whole = lax.dynamic_update_slice_in_dim(whole, piece, places[i] * rows, 0)
    return whole


class Spread:
    def __init__(self, g, runs):
        nc, nf = lax.axis_size("ctx"), lax.axis_size("fsdp")
        c, f = lax.axis_index("ctx"), lax.axis_index("fsdp")
        self.g, self.rows, self.runs = g, g.shape[0] // (nc * nf), runs
        self.place = lambda k, step: lax.rem(f + k, nf) * nc + lax.rem(c - step + nc, nc)
        self.come = []
        for run in runs:
            self.send(g, run)

    def more(self, run, order):
        waits = list(order.waits)
        self.send(order.enter(self.g), run)
        order.waits = waits

    def send(self, g, run):
        nc, nf, f = lax.axis_size("ctx"), lax.axis_size("fsdp"), lax.axis_index("fsdp")
        take = lambda at, count: lax.dynamic_slice_in_dim(g, at * self.rows, count * self.rows, 0)
        for k in range(1, nf):
            if len(run) == nc:
                sent = take(lax.rem(f + k, nf) * nc, nc)
            else:
                sent = jnp.concatenate([take(self.place(k, step), 1) for step in run])
            self.sent = sent
            self.come.append((run, rotate(sent, "fsdp", k)))

    def landed(self, step):
        return [v for run, v in self.come if step in run]

    def terms(self, step):
        nc, c = lax.axis_size("ctx"), lax.axis_index("ctx")
        out = [(self.g, self.place(0, step))]
        for run, v in self.come:
            if step in run:
                out.append((v, lax.rem(c - step + nc, nc) if len(run) == nc else run.index(step)))
        return out


def block_sum(groups, last, rows, dtype, order, apart=False):
    arrays = [a for group in groups for a, _ in group]
    places = jnp.stack([jnp.asarray(at, jnp.int32) for group in groups for _, at in group])
    widths = [group[0][0].shape[1] for group in groups]
    specs = [pl.BlockSpec((rows, a.shape[1]), lambda i, p, j=j: (p[j], 0)) for j, a in enumerate(arrays)]
    if last is not None:
        arrays.append(last)
        specs.append(pl.BlockSpec(last.shape, lambda i, p: (0, 0)))
        order.land(last)
    deps = order.deps()
    outs = widths if apart else [sum(widths)]

    def kernel(places_ref, *refs):
        at, lo = 0, 0
        for i, (group, width) in enumerate(zip(groups, widths)):
            total = sum(r[...].astype(f32) for r in refs[at : at + len(group)])
            if last is not None:
                total = total + refs[len(arrays) - 1][:, lo : lo + width].astype(f32)
            if apart:
                refs[i - len(groups)][...] = total.astype(dtype)
            else:
                refs[-1][:, lo : lo + width] = total.astype(dtype)
            at, lo = at + len(group), lo + width

    out = pl.pallas_call(
        kernel,
        grid_spec=pltpu.PrefetchScalarGridSpec(
            num_scalar_prefetch=1,
            grid=(1,),
            in_specs=specs + [pl.BlockSpec(memory_space=pl.ANY)] * len(deps),
            out_specs=[pl.BlockSpec((rows, w), lambda i, p: (0, 0)) for w in outs],
        ),
        out_shape=[jax.ShapeDtypeStruct((rows, w), dtype) for w in outs],
        compiler_params=pltpu.CompilerParams(vmem_limit_bytes=16 * 2**20),
        cost_estimate=COST,
    )(places, *arrays, *deps)
    order.leave(out[0])
    return out if apart else out[0]


def finish(ring, rest, shapes, order):
    ring.at += 1
    terms = [t for one in ring.spreads for t in one.terms(ring.at)]
    rows = ring.spreads[0].rows
    order.land(ring.come)
    deps = order.deps()
    places = jnp.stack([jnp.asarray(at, jnp.int32) for _, at in terms])
    specs = [pl.BlockSpec((rows, a.shape[1]), lambda i, p, j=j: (p[j], 0)) for j, (a, _) in enumerate(terms)]
    whole = lambda shape: pl.BlockSpec(shape, lambda i, p, n=len(shape): (0,) * n)

    def kernel(*refs):
        n = 3 + len(terms)
        finish_kernel(*refs[:n], *refs[n + len(deps) :], terms=len(terms))

    return pl.pallas_call(
        kernel,
        grid_spec=pltpu.PrefetchScalarGridSpec(
            num_scalar_prefetch=1,
            grid=(1,),
            in_specs=specs
            + [whole(ring.come.shape), whole(rest.shape)]
            + [pl.BlockSpec(memory_space=pl.ANY)] * len(deps),
            out_specs=[whole(s) for s in shapes],
        ),
        out_shape=[jax.ShapeDtypeStruct(s, f32) for s in shapes],
        compiler_params=pltpu.CompilerParams(vmem_limit_bytes=16 * 2**20),
        cost_estimate=COST,
    )(places, *[a for a, _ in terms], ring.come, rest, *deps)


class Ring:
    def __init__(self, spreads, order):
        self.spreads, self.at = spreads, 0
        self.total, self.come = None, None
        self.step(order)

    def done(self):
        return self.at == lax.axis_size("ctx")

    def step(self, order):
        if self.done():
            return
        self.at += 1
        groups = [one.terms(self.at) for one in self.spreads]
        last = lax.axis_size("ctx") == self.at
        self.total = block_sum(groups, self.come, self.spreads[0].rows, f32 if last else bf16, order, last)
        if not last:
            self.come = rotate(self.total, "ctx", 1)


def halve_kernel(near, come, near_ref, away_ref):
    total = near[...].astype(f32) + come[...].astype(f32)
    near_ref[...] = total[:, : near_ref.shape[1]]
    away_ref[...] = total[:, near_ref.shape[1] :].astype(bf16)


def add_kernel(a, b, out_ref):
    out_ref[...] = a[...] + b[...]


def add_both_kernel(a, b, come, a_ref, b_ref):
    wide = a_ref.shape[1]
    a_ref[...] = a[...] + come[:, :wide]
    b_ref[...] = b[...] + come[:, wide:]


class Cube:
    def __init__(self, near, away):
        self.near, self.away, self.mask = near, away, 1
        self.come = flip(away, "tp", 1)

    def halve(self, order):
        seqs, rows, wide = self.near.shape
        while self.mask * 2 < lax.axis_size("tp"):
            wide //= 2
            order.land(self.come)
            out = (seqs, rows, wide)
            self.near, self.away = call(
                halve_kernel,
                0,
                seqs,
                [(self.near, 0), (self.come, 0)],
                [(out, f32, True), (out, bf16, True)],
                deps=order.deps(),
            vmem=16,
            )
            order.leave(self.away)
            self.mask *= 2
            self.come = flip(self.away, "tp", self.mask)

    def total(self):
        return self.near + self.come.astype(f32)


class Hops:
    def __init__(self, v, own, axes=("tp", "fsdp", "ctx")):
        self.v, self.own = v, own
        hops = {axis: [(axis, 1 << i) for i in range(lax.axis_size(axis).bit_length() - 1)] for axis in axes}
        self.todo = [hop for axis in axes for hop in hops[axis]]
        self.come, self.both = None, False

    def go(self, order):
        if self.come is not None:
            order.land(self.come)
            if self.both:
                self.v, self.own = small_call(
                    add_both_kernel, [self.v, self.own, self.come], [(self.v.shape, f32), (self.own.shape, f32)], order
                )
            else:
                self.v = small_call(add_kernel, [self.v, self.come], [(self.v.shape, f32)], order)[0]
            order.leave(self.v)
            self.come = None
        if self.todo:
            axis, mask = self.todo.pop(0)
            self.both = axis != "tp" and self.own is not None
            self.come = flip(jnp.concatenate([self.v, self.own], 1) if self.both else self.v, axis, mask)

    def end(self, order):
        while self.come is not None:
            self.go(order)
        return self.v


def small_call(kernel, operands, outs, order, scalar=None, scratch=()):
    deps = order.deps()
    n_in = len(operands) + (scalar is not None)

    def run(*refs):
        kernel(*refs[:n_in], *refs[n_in + len(deps) :])

    vmem = pl.BlockSpec(memory_space=pltpu.VMEM)
    return pl.pallas_call(
        run,
        in_specs=([] if scalar is None else [pl.BlockSpec(memory_space=pltpu.SMEM)])
        + [vmem] * len(operands)
        + [pl.BlockSpec(memory_space=pl.ANY)] * len(deps),
        out_specs=[vmem] * len(outs),
        out_shape=[jax.ShapeDtypeStruct(*o) for o in outs],
        scratch_shapes=list(scratch),
        compiler_params=pltpu.CompilerParams(vmem_limit_bytes=16 * 2**20),
        cost_estimate=COST,
    )(*([] if scalar is None else [scalar]), *operands, *deps)


class Chain:
    def __init__(self, parts, decay, reverse):
        self.parts, self.decay, self.reverse = parts, decay, reverse
        self.hop, self.last, self.entering = 0, None, []

    def send(self, order):
        n = lax.axis_size("ctx")
        self.hop += 1
        if self.hop >= n:
            return
        out = self.parts
        if self.last is not None:
            order.land(self.last)
            out = small_call(
                combine_kernel, [self.parts, self.decay, self.last], [(out.shape, bf16)], order
            )[0]
            order.leave(out)
        hop = self.hop
        pair = (n - hop, n - hop - 1) if self.reverse else (hop - 1, hop)
        self.last = lax.ppermute(out, "ctx", [pair])
        self.entering.append(self.last)

    def land(self, order):
        order.land(self.last)


class Order:
    def __init__(self):
        self.waits = []

    def land(self, *arrays):
        self.waits += arrays

    def enter(self, v):
        v = after(v, *self.waits)
        self.waits = []
        return v

    def deps(self):
        waits, self.waits = self.waits, []
        return waits

    def leave(self, v):
        self.waits = self.waits + [v]
        return v


def dot(a, b, dims=NN):
    return lax.dot_general(a, b, dims, preferred_element_type=f32)


def split(v, terms):
    out = []
    for i in range(terms):
        t = v.astype(bf16)
        out.append(t)
        if i + 1 < terms:
            v = v - t.astype(f32)
    return out


def constants(inner, q):
    heads = jnp.arange(LANES, dtype=jnp.int32)[:, None] == jnp.arange(inner, dtype=jnp.int32)[None] // HEADDIM
    spread = heads.astype(bf16)
    tri = jnp.arange(q, dtype=jnp.int32)[None] <= jnp.arange(q, dtype=jnp.int32)[:, None]
    return jnp.concatenate([spread, spread]), spread.T, tri.astype(bf16)


def widen(v, spread):
    return dot(jnp.concatenate(split(v, 2), 1), spread[...])


def narrow(v, gather, terms):
    out = None
    for t in split(v, terms):
        s = dot(t, gather[...])
        out = s if out is None else out + s
    return out


def tri_sum(tri, v, dims=NN):
    out = None
    for t in split(v, 3):
        s = dot(tri[...], t, dims)
        out = s if out is None else out + s
    return out


def one_of(refs):
    total = refs[0][...]
    for r in refs[1:]:
        total = total + r[...]
    return total


def halves(v):
    lane = lax.broadcasted_iota(jnp.int32, v.shape, 1)
    zero = jnp.zeros_like(v)
    return jnp.where(lane < HEADDIM, v, zero), jnp.where(lane >= HEADDIM, v, zero)


def sigmoid(v):
    return lax.logistic(v)


def gather_rows(places, pieces, whole):
    rows = pieces[0].shape[0]
    for i, piece in enumerate(pieces):
        whole[pl.ds(pl.multiple_of(places[i] * rows, 16), rows), :] = piece[...]


def project_kernel(nx, start, w, taps, bias, head_par, spread, tri, *refs, inner, conv):
    u_ref, slope_ref, act_ref, xdt_ref, dtl_ref, state_ref, dec_ref = refs[-7:]
    q = start.shape[0]
    u = dot(nx[...], w[...])
    u_ref[...] = u[:, :conv].astype(bf16)
    at = lax.broadcasted_iota(jnp.int32, (q, 1), 0)
    begin = start[...]
    since = jnp.broadcast_to(at - begin, (q, LANES))
    keep = [jnp.where(since >= j, 1.0, 0.0) for j in range(CONV)]
    for lo in range(0, conv, LANES):
        cols = slice(lo, lo + LANES)
        ut = u[:, cols]
        acc = bias[0:1, cols] + taps[CONV - 1 : CONV, cols] * ut[HALO:]
        for j in range(1, CONV):
            window = ut[HALO - j : HALO - j + q]
            acc = acc + taps[CONV - 1 - j : CONV - j, cols] * (window * keep[j])
        sig = sigmoid(acc)
        silu = acc * sig
        act_ref[:, cols] = silu.astype(bf16)
        slope_ref[:, cols] = (sig + silu * (1.0 - sig)).astype(bf16)
    v = u[HALO:, conv:] + head_par[0:1, :]
    dt = jnp.maximum(v, 0.0) + jnp.log1p(jnp.exp(-jnp.abs(v)))
    cum = tri_sum(tri, -dt * jnp.exp(head_par[1:2, :]))
    dtl_ref[:, :LANES] = dt
    dtl_ref[:, LANES:] = cum
    end = cum[q - 1 : q, :]
    begin_last = begin[q - 1 : q, :]
    tail = jnp.where(begin == begin_last, jnp.exp(end - cum), 0.0)
    xh = act_ref[:, :inner].astype(f32)
    xdt = (xh * widen(dt, spread)).astype(bf16)
    xdt_ref[...] = xdt
    weighted = (xdt.astype(f32) * widen(tail, spread)).astype(bf16)
    b = act_ref[:, inner : inner + STATE]
    state_ref[...] = dot(b, weighted, TN).astype(bf16)
    total = jnp.where(begin_last < 0, jnp.exp(end), 0.0)
    dec_ref[...] = widen(jnp.broadcast_to(total, (8, LANES)), spread)[0:1]


def project_first_kernel(places, nx, start, taps, bias, head_par, spread, tri, *refs, pieces, inner, conv):
    w = refs[-1]

    @pl.when(pl.program_id(0) == 0)
    def _():
        gather_rows(places, refs[:pieces], w)

    project_kernel(nx, start, w, taps, bias, head_par, spread, tri, *refs[pieces:-1], inner=inner, conv=conv)


def combine_kernel(parts, decay, last, out_ref):
    out_ref[...] = (parts[...].astype(f32) + decay[...] * last[...].astype(f32)).astype(bf16)


def score_mask(begin_col, q):
    r = lax.broadcasted_iota(jnp.int32, (q, q), 0)
    c = lax.broadcasted_iota(jnp.int32, (q, q), 1)
    return (c <= r) & (c >= begin_col)


def score_mask_t(begin_row, q):
    r = lax.broadcasted_iota(jnp.int32, (q, q), 0)
    c = lax.broadcasted_iota(jnp.int32, (q, q), 1)
    return (r <= c) & (r >= begin_row)


def local_kernel(act, xdt, dtl, start, y_ref, *, inner):
    q = start.shape[0]
    b = act[:, inner : inner + STATE]
    c = act[:, inner + STATE : inner + 2 * STATE]
    scores = jnp.where(score_mask(start[...], q), dot(c, b, NT), 0.0)
    cum = dtl[:, LANES:]
    cum_t = cum.T
    for pair in range(inner // LANES):
        cols = slice(pair * LANES, (pair + 1) * LANES)
        weights = []
        for h in (2 * pair, 2 * pair + 1):
            gap = jnp.minimum(cum[:, h : h + 1] - cum_t[h : h + 1, :], 0.0)
            weights.append((jnp.exp(gap) * scores).astype(bf16))
        even, odd = halves(xdt[:, cols])
        y_ref[:, cols] = dot(weights[0], even) + dot(weights[1], odd)


def gate_sums_kernel(nx, cot, y_in, act, dtl, start, state, w, rows, spread, y_ref, z_ref, dh_ref, sums_ref, *, inner):
    q = start.shape[0]
    c = act[:, inner + STATE : inner + 2 * STATE]
    zz = dot(nx[HALO:], w[:, :inner])
    z_ref[...] = zz
    d_hidden = dot(cot[...], w[:, inner:])
    dh_ref[...] = d_hidden
    into = widen(jnp.where(start[...] < 0, jnp.exp(dtl[:, LANES:]), 0.0), spread)
    y = y_in[...] + into * dot(c, one_of(state))
    y_ref[...] = y
    gated = (y + rows[0:1, :] * act[:, :inner].astype(f32)) * (zz * sigmoid(zz))
    e = d_hidden * rows[1:2, :]
    ones = jnp.ones((8, inner), bf16)
    sq = dot(ones, (gated * gated).astype(bf16), NT)
    eg = dot(ones, (e * gated).astype(bf16), NT)
    row = lax.broadcasted_iota(jnp.int32, (8, q), 0)
    sums_ref[...] = jnp.where(row == 0, sq, eg)


def gate_sums_first_kernel(places, nx, cot, y_in, act, dtl, start, *refs, pieces, hops, inner):
    state, (rows, spread), refs = refs[:hops], refs[hops : hops + 2], refs[hops + 2 :]
    y_ref, z_ref, dh_ref, sums_ref, w = refs[pieces], refs[pieces + 1], refs[pieces + 2], refs[pieces + 3], refs[-1]

    @pl.when(pl.program_id(0) == 0)
    def _():
        gather_rows(places, refs[:pieces], w)

    gate_sums_kernel(
        nx, cot, y_in, act, dtl, start, state, w, rows, spread, y_ref, z_ref, dh_ref, sums_ref, inner=inner
    )


def gate_sums_next_kernel(nx, cot, y_in, act, dtl, start, *refs, hops, inner):
    gate_sums_kernel(nx, cot, y_in, act, dtl, start, refs[:hops], *refs[hops:], inner=inner)


def mix_kernel(rank, hidden, w, near_ref, away_ref):
    seqs, q, cols = near_ref.shape
    k = pl.program_id(0)
    out = dot(hidden[...].reshape(seqs * q, hidden.shape[2]), w[...], NT).astype(bf16).reshape(seqs, q, cols)

    @pl.when(lax.rem(k, 2) == 0)
    def _():
        near_ref[...] = out

    @pl.when(lax.rem(k, 2) == 1)
    def _():
        away_ref[...] = out


def out_back_kernel(rank, du, rim, tap, nx, z_part, w_in, near_ref, away_ref, own, part):
    seqs, q = du.shape[0], du.shape[1] - HALO
    cols = w_in.shape[0]
    tp = near_ref.shape[2] * 2 // cols
    k = pl.program_id(0)

    @pl.when(k == 0)
    def _():
        for s in range(seqs):
            own[s * q : (s + 1) * q - 16, :] = du[s, HALO:q, :]
            edge = du[s, q : q + HALO, :].astype(f32)
            own[(s + 1) * q - 16 : (s + 1) * q, :] = (edge + rim[s].astype(f32)).astype(bf16)
        part[...] = jnp.zeros_like(part)

    out = dot(own[...], w_in[...], NT)
    row16 = lax.broadcasted_iota(jnp.int32, (16, cols), 0)
    inner = tap.shape[2] - 2 * STATE
    for s in range(seqs):
        mine = out[s * q : (s + 1) * q] + z_part[s, HALO:, :].astype(f32)
        prod = mine * nx[s, HALO:, :].astype(f32)
        folded = prod[:, :LANES]
        for lo in range(LANES, cols, LANES):
            folded = folded + prod[:, lo : lo + LANES]
        part[s * q : (s + 1) * q, :] += folded
        gains = jnp.broadcast_to(jnp.sum(prod, axis=0, keepdims=True), (8, cols))
        bc_taps = jnp.concatenate([tap[s][:, inner:], jnp.zeros((8, cols - 2 * STATE), f32)], 1)
        extra = jnp.concatenate([gains, bc_taps], 0).astype(bf16)
        for j in range(tp):
            to = slice(j // 2 * cols, (j // 2 + 1) * cols)

            @pl.when(k == j)
            def _():
                (away_ref if j % 2 else near_ref)[s, :q, to] = mine.astype(bf16)
                (away_ref if j % 2 else near_ref)[s, q:, to] = extra

    @pl.when(k == tp - 1)
    def _():
        ones = jnp.ones((16, LANES), bf16)
        for s in range(seqs):
            total = None
            for t in split(part[s * q : (s + 1) * q, :], 2):
                one = dot(ones, t, NT)
                total = one if total is None else total + one
            total = jnp.concatenate([total, jnp.zeros((16, cols - q), f32)], 1)
            for j in range(tp):
                to = slice(j // 2 * cols, (j // 2 + 1) * cols)
                ref = away_ref if j % 2 else near_ref
                ref[s, q:, to] = jnp.where(row16 == 0, total, ref[s, q:, to].astype(f32)).astype(bf16)


def pack_kernel(extra, *refs, chunks, inner):
    taps, heads, gates = refs[:chunks], refs[chunks : 2 * chunks], refs[2 * chunks : 3 * chunks]
    out = refs[-1]
    total = lambda refs: sum(jnp.sum(r[...], axis=0) for r in refs)
    more = jnp.sum(extra[...], axis=0)
    cols = more.shape[1]
    out[:, :inner] = total(taps)[:, :inner]
    out[:, inner : inner + LANES] = total(heads)
    out[:, inner + LANES : 2 * inner + LANES] = total(gates)
    out[:, 2 * inner + LANES : 2 * inner + LANES + cols] = more[:8]
    out[:, 2 * inner + LANES + cols :] = more[8:, : 2 * STATE]


def unpack_kernel(
    v, come, gain, gather, conv_ref, convb_ref, bc_ref, bcb_ref, dtb_ref, alog_ref, skip_ref, gate_ref, gain_ref
):
    inner, cols = gate_ref.shape[1], gain_ref.shape[1]
    heads = skip_ref.shape[1]
    own = v[...] + come[...]
    taps = own[:, :inner]
    conv_ref[...] = taps[:CONV]
    convb_ref[...] = taps[CONV : CONV + 1]
    head = own[:, inner : inner + LANES]
    dtb_ref[...] = head[0:1, :heads]
    alog_ref[...] = head[1:2, :heads]
    lo = 2 * inner + LANES
    gate = own[:, inner + LANES : lo]
    gate_ref[...] = gate[0:1]
    skip_ref[...] = narrow(gate, gather, 3)[1:2, :heads]
    gain_ref[...] = own[1:2, lo : lo + cols] / gain[0:1, :]
    bc = own[:, lo + cols :]
    bc_ref[...] = bc[:CONV]
    bcb_ref[...] = bc[CONV : CONV + 1]


def tokens_kernel(near, come, own, cot, inv, gain, out_ref, extra_ref):
    q, cols = out_ref.shape
    total = near[...] + come[...].astype(f32)
    extra_ref[...] = total[q:]
    both = jnp.broadcast_to(total[q : q + 8, :q][0:1], (8, q)).T[:, 0:1]
    hat = own[...].astype(f32) * inv[...]
    out_ref[...] = cot[...].astype(f32) + inv[...] * (total[:q] * gain[0:1, :] - hat * (both / D))


def finish_kernel(places, *refs, terms):
    come, rest = refs[terms], refs[terms + 1]
    zx_ref, bc_ref, dt_ref = refs[-3:]
    inner, wide, heads = zx_ref.shape[2], bc_ref.shape[1], dt_ref.shape[1]
    total = sum(r[...].astype(f32) for r in refs[:terms]) + come[...].astype(f32)
    zx_ref[:, 0, :] = rest[...]
    zx_ref[:, 1, :] = total[:, :inner]
    bc_ref[...] = total[:, inner : inner + wide]
    dt_ref[...] = total[:, inner + wide : inner + wide + heads]


def norm_kernel(x, halo, gain, nx_ref, inv_ref):
    wide = x[...].astype(f32)
    width = wide.shape[1]
    inv = lax.rsqrt(jnp.mean(wide * wide, axis=-1, keepdims=True) + NORM_EPS)
    inv_ref[...] = inv
    nx_ref[HALO:, :] = (wide * inv * gain[0:1, :]).astype(bf16)
    edge = halo[...].astype(f32)
    inv = lax.rsqrt(jnp.mean(edge * edge, axis=-1, keepdims=True) + NORM_EPS)
    nx_ref[:HALO, :] = (edge * inv * gain[0:1, :]).astype(bf16)


def gate_kernel(y_in, act, dtl, start, z, dh, sums, rows, spread, *refs, inner):
    hidden_ref, dz_ref, dy_ref, dstate_ref, grads_ref = refs[-5:]
    xh = act[:, :inner].astype(f32)
    y = y_in[...] + rows[0:1, :] * xh
    zz = z[...].astype(f32)
    sig = sigmoid(zz)
    silu = zz * sig
    gated = y * silu
    gain = rows[1:2, :]
    d_hidden = dh[...].astype(f32)
    sums_t = sums[...].T
    inv = lax.rsqrt(sums_t[:, 0:1] / INNER + NORM_EPS)
    back = sums_t[:, 1:2] * (inv * inv * inv) / INNER
    scaled = gated * inv
    hidden_ref[...] = (scaled * gain).astype(bf16)
    dg = inv * (d_hidden * gain) - gated * back
    dy = (dg * silu).astype(bf16)
    dy_ref[...] = dy
    dz_ref[:HALO, :] = jnp.zeros((HALO, inner), bf16)
    dz_ref[HALO:, :] = (dg * y * sig * (1.0 + zz * (1.0 - sig))).astype(bf16)
    gate_row = jnp.sum(d_hidden * scaled, axis=0, keepdims=True)
    dy_wide = dy.astype(f32)
    skip_row = jnp.sum(dy_wide * xh, axis=0, keepdims=True)
    row = lax.broadcasted_iota(jnp.int32, (8, inner), 0)
    grads_ref[...] = jnp.where(row == 0, gate_row, jnp.where(row == 1, skip_row, 0.0))
    into = widen(jnp.where(start[...] < 0, jnp.exp(dtl[:, LANES:]), 0.0), spread)
    c = act[:, inner + STATE : inner + 2 * STATE]
    dstate_ref[...] = dot(c, (into * dy_wide).astype(bf16), TN).astype(bf16)


def local_back_kernel(act, xdt, dtl, start, start_row, dy, *refs, hops, inner):
    state, (spread, dx_ref, dbc_ref) = refs[:hops], refs[hops:]
    q = start.shape[0]
    b = act[:, inner : inner + STATE]
    c = act[:, inner + STATE : inner + 2 * STATE]
    mask = score_mask_t(start_row[...], q)
    scores = jnp.where(mask, dot(b, c, NT), 0.0)
    cum = dtl[:, LANES:]
    cum_t = cum.T
    total = jnp.zeros((q, q), f32)
    for pair in range(inner // LANES):
        cols = slice(pair * LANES, (pair + 1) * LANES)
        dy_pair = dy[:, cols]
        x_even, x_odd = halves(xdt[:, cols])
        dy_even, dy_odd = halves(dy_pair)
        out = None
        for h, x_one, dy_one in ((2 * pair, x_even, dy_even), (2 * pair + 1, x_odd, dy_odd)):
            decay = jnp.exp(jnp.minimum(cum_t[h : h + 1, :] - cum[:, h : h + 1], 0.0))
            total = total + dot(x_one, dy_pair, NT) * decay
            term = dot((decay * scores).astype(bf16), dy_one)
            out = term if out is None else out + term
        dx_ref[:, cols] = out
    d_scores = jnp.where(mask, total, 0.0).astype(bf16)
    into = widen(jnp.where(start[...] < 0, jnp.exp(cum), 0.0), spread)
    weighted = (into * dy[...].astype(f32)).astype(bf16)
    dbc_ref[:, :STATE] = dot(d_scores, c)
    dbc_ref[:, STATE:] = dot(d_scores, b, TN) + dot(weighted, one_of(state), NT)


def conv_back_kernel(act, xdt, dtl, start, dy, y_in, dx, dbc, slope, u, dec, *refs, hops, inner, conv):
    state, later, refs = refs[:hops], refs[hops : 2 * hops], refs[2 * hops :]
    taps, rows, head_par, spread, gather, tri = refs[:6]
    du_ref, rim_ref, tap_ref, head_ref, dact = refs[-5:]
    q = start.shape[0]
    begin = start[...]
    b = act[:, inner : inner + STATE]
    dt, cum = dtl[:, :LANES], dtl[:, LANES:]
    end = cum[q - 1 : q, :]
    begin_last = begin[q - 1 : q, :]
    tail = widen(jnp.where(begin == begin_last, jnp.exp(end - cum), 0.0), spread)
    x_dt = xdt[...].astype(f32)
    d_y = dy[...].astype(f32)
    g = one_of(later)
    dx_tail = tail * dot(b, g)
    dact[:, inner : inner + STATE] = dbc[:, :STATE] + dot((x_dt * tail).astype(bf16), g, NT)
    dact[:, inner + STATE :] = dbc[:, STATE:]
    dx_local = dx[...]
    dx_all = dx_local + dx_tail
    dact[:, :inner] = dx_all * widen(dt, spread) + rows[0:1, :] * d_y
    flux_near = narrow(d_y * y_in[...] - x_dt * dx_local, gather, 3)
    flux_tail = narrow(x_dt * dx_tail, gather, 2)
    d_dt = narrow(dx_all * act[:, :inner].astype(f32), gather, 2)
    through = jnp.sum(dec[...] * (g.astype(f32) * one_of(state).astype(f32)), axis=0, keepdims=True)
    through = narrow(jnp.broadcast_to(through, (8, inner)), gather, 2)[0:1]
    d_log = tri_sum(tri, flux_near, TN) + (tri_sum(tri, flux_tail) - flux_tail) + through
    rate = jnp.exp(head_par[1:2, :])
    d_raw = (d_dt - rate * d_log) * (1.0 - jnp.exp(-dt))
    du_ref[:HALO, conv:] = jnp.zeros((HALO, LANES), bf16)
    rim_ref[:, conv:] = jnp.zeros((HALO, LANES), bf16)
    du_ref[HALO:, conv:] = d_raw.astype(bf16)
    bias_row = jnp.sum(d_raw, axis=0, keepdims=True)
    log_row = -jnp.sum(d_log * dt * rate, axis=0, keepdims=True)
    row = lax.broadcasted_iota(jnp.int32, (8, LANES), 0)
    head_ref[...] = jnp.where(row == 0, bias_row, jnp.where(row == 1, log_row, 0.0))
    since = lax.broadcasted_iota(jnp.int32, (q, LANES), 0) - begin
    keep = [jnp.where(since >= j, 1.0, 0.0) for j in range(CONV)]
    zeros = jnp.zeros((HALO, LANES), f32)
    for lo in range(0, conv, LANES):
        cols = slice(lo, lo + LANES)
        dp = dact[:, cols] * slope[:, cols].astype(f32)
        ut = u[:, cols].astype(f32)
        moved = jnp.concatenate([zeros, dp], 0)
        total = taps[CONV - 1 : CONV, cols] * moved
        tap_rows = [jnp.sum(dp * ut[HALO:], axis=0, keepdims=True)]
        for j in range(1, CONV):
            moved = jnp.concatenate([zeros, dp * keep[j], zeros], 0)[j : j + q + HALO]
            tap_rows.append(jnp.sum(moved * ut, axis=0, keepdims=True))
            total = total + taps[CONV - 1 - j : CONV - j, cols] * moved
        du_ref[:, cols] = total.astype(bf16)
        rim_ref[:, cols] = total[:HALO].astype(bf16)
        out = jnp.sum(dp, axis=0, keepdims=True)
        for j in range(CONV):
            out = jnp.where(row == CONV - 1 - j, tap_rows[j], jnp.where(row == CONV, out, 0.0) if j == 0 else out)
        tap_ref[:, cols] = out


def call(kernel, first, count, ins, outs, shared=(), scalar=None, scratch=(), into=None, deps=(), vmem=34):
    def spec(shape, base):
        block = (None,) + tuple(shape[1:])
        rest = (0,) * (len(shape) - 1)
        return pl.BlockSpec(block, lambda s: (s + base,) + rest)

    in_specs = [spec(a.shape, o) for a, o in ins]
    in_specs += [
        pl.BlockSpec(a.shape, lambda s, n=a.ndim: (0,) * n, pipeline_mode=pl.Buffered(1)) for a in shared
    ]
    operands = [a for a, _ in ins] + list(shared)
    if scalar is not None:
        in_specs.insert(0, pl.BlockSpec(memory_space=pltpu.SMEM))
        operands.insert(0, scalar)
    n_args = len(operands)
    operands += list(deps)
    in_specs += [pl.BlockSpec(memory_space=pl.ANY)] * len(deps)
    aliases = {}
    if into is not None:
        for i, buf in enumerate(into):
            if buf is not None:
                aliases[len(operands)] = i
                operands.append(buf)
                in_specs.append(pl.BlockSpec(memory_space=pl.ANY))
    n_in = len(operands)

    def run(*refs):
        kernel(*refs[:n_args], *refs[n_in:])

    return pl.pallas_call(
        run,
        grid=(count,),
        in_specs=in_specs,
        out_specs=[spec(s, first if whole else 0) if whole is not None else pl.BlockSpec(s, lambda i, n=len(s): (0,) * n) for s, _, whole in outs],
        out_shape=[jax.ShapeDtypeStruct(s, d) for s, d, _ in outs],
        scratch_shapes=list(scratch),
        input_output_aliases=aliases,
        compiler_params=pltpu.CompilerParams(vmem_limit_bytes=vmem * 2**20),
        cost_estimate=COST,
    )(*operands)


def call_slices(kernel, rank, tp, wholes, weights, outs, scratch=(), deps=()):
    specs, operands = [], []
    for a, cut in wholes:
        if cut:
            block = a.shape[:-1] + (a.shape[-1] // tp,)
            specs.append(pl.BlockSpec(block, lambda k, r, n=a.ndim: (0,) * (n - 1) + (r[0] ^ k,)))
        else:
            specs.append(pl.BlockSpec(a.shape, lambda k, r, n=a.ndim: (0,) * n))
        operands.append(a)
    for a, at, cols in weights:
        specs.append(pl.BlockSpec((a.shape[0] // tp, cols), lambda k, r, j=at // cols: (r[0] ^ k, j)))
        operands.append(a)
    n_args = len(operands) + 1
    operands += list(deps)
    specs += [pl.BlockSpec(memory_space=pl.ANY)] * len(deps)
    n_in = len(operands) + 1

    def run(*refs):
        kernel(*refs[:n_args], *refs[n_in:])

    out_specs = []
    for shape, _, cut in outs:
        n = len(shape)
        if cut is None:
            out_specs.append(pl.BlockSpec((shape[0], shape[1] // tp), lambda k, r: (0, r[0] ^ k)))
        elif cut:
            out_specs.append(
                pl.BlockSpec(shape[:-1] + (shape[-1] * 2 // tp,), lambda k, r, n=n: (0,) * (n - 1) + (k // 2,))
            )
        else:
            out_specs.append(pl.BlockSpec(shape, lambda k, r, n=n: (0,) * n))
    return pl.pallas_call(
        run,
        grid_spec=pltpu.PrefetchScalarGridSpec(
            num_scalar_prefetch=1,
            grid=(tp,),
            in_specs=specs,
            out_specs=out_specs,
            scratch_shapes=list(scratch),
        ),
        out_shape=[jax.ShapeDtypeStruct(s, d) for s, d, _ in outs],
        compiler_params=pltpu.CompilerParams(vmem_limit_bytes=28 * 2**20),
        cost_estimate=COST,
    )(rank, *operands)


def pack(taps, heads, gates, extra, order, inner):
    width = 2 * inner + LANES + extra.shape[2] + 2 * STATE
    (out,) = small_call(
        functools.partial(pack_kernel, chunks=len(taps), inner=inner),
        [extra, *taps, *heads, *gates],
        [((8, width), f32)],
        order,
    )
    return order.leave(out)


def per_device(
    tokens,
    segment_ids,
    in_gain,
    w_zx,
    w_bc,
    w_dt,
    dt_bias,
    a_log,
    skip_gain,
    conv_x,
    conv_x_bias,
    conv_bc,
    conv_bc_bias,
    gate_gain,
    w_out,
    cotangent,
):
    tp_count, tp_rank = lax.axis_size("tp"), lax.axis_index("tp")
    ctx_rank = lax.axis_index("ctx")
    seqs, q, width = tokens.shape
    inner = w_zx.shape[2]
    heads = w_dt.shape[1]
    conv = inner + 2 * STATE
    cols = width // tp_count
    n_tok = seqs * q
    chunks = 2 if seqs % 2 == 0 else 1
    per = seqs // chunks

    n_ctx = lax.axis_size("ctx")
    rank = tp_rank.astype(jnp.int32)[None]
    shape = lambda *s: (seqs,) + s
    part = lambda *s: (per,) + s
    order = Order()

    first_w = jnp.concatenate(
        [w_zx[:, 1, :], w_bc, jnp.pad(w_dt, ((0, 0), (0, LANES - heads)))], axis=1
    )
    ring_in = ring_pieces(first_w)
    halo = shift(jnp.pad(tokens[:, q - 8 :, :], ((0, 0), (8, 0), (0, 0))), "ctx", 1)
    pieces_in, places = all_pieces(ring_in)
    in_kernel = first_w.shape[0] % 16 == 0
    second_w = jnp.concatenate([after(w_zx, ring_in[1])[:, 0, :], w_out.T], axis=1)
    ring_rest = ring_pieces(after(second_w, ring_in[-1]))
    pieces_rest, _ = all_pieces(ring_rest, pieces_in[-1])
    spread, gather, tri = constants(inner, q)
    if not in_kernel:
        w_in, w_rest = assemble(pieces_in, places), assemble(pieces_rest, places)

    gain = jnp.broadcast_to(in_gain.astype(f32)[None], (8, width))
    bulk = None
    order.land(halo)
    for g in range(chunks):
        order.land(*ring_in[g + 1 : g + 2], *pieces_in[2 * g + 1 : 2 * g + 2])
        bulk = call(
            norm_kernel,
            g * per,
            per,
            [(tokens, g * per), (halo, g * per)],
            deps=order.deps(),
            vmem=16,
            outs=[(shape(q + HALO, width), bf16, True), (shape(q, 1), f32, True)],
            shared=(gain,),
            into=bulk,
        )
        order.leave(bulk[1])
    nx, inv_rms = bulk

    begin = segment_ids - ctx_rank * q
    start = begin[:, :, None]
    start_row = begin[:, None, :]
    taps = jnp.concatenate([conv_x, conv_bc], axis=1).astype(f32)
    bias = jnp.concatenate([conv_x_bias, conv_bc_bias]).astype(f32)[None]
    head_par = jnp.pad(jnp.stack([dt_bias, a_log]), ((0, 6), (0, LANES - heads)))
    rows = jnp.pad(jnp.stack([jnp.repeat(skip_gain, HEADDIM), gate_gain.astype(f32)]), ((0, 6), (0, 0)))

    states, decs, kept, y_local = [], [], [], []
    landing = lambda i: pieces_rest[min(i, len(pieces_rest) - 1)]
    for g in range(chunks):
        o = g * per
        order.land(ring_rest[min(g + 1, n_ctx - 1)])
        if g:
            order.land(landing(2 * g - 1))
        first = g == 0 and in_kernel
        given = [taps, bias, head_par, spread, tri]
        outs = [
            (part(q + HALO, conv), bf16, False),
            (part(q, conv), bf16, False),
            (part(q, conv), bf16, False),
            (part(q, inner), bf16, False),
            (part(q, 2 * LANES), f32, False),
            (part(STATE, inner), bf16, False),
            (part(1, inner), f32, False),
        ]
        if first:
            kernel = functools.partial(project_first_kernel, pieces=len(pieces_in), inner=inner, conv=conv)
        else:
            kernel = functools.partial(project_kernel, inner=inner, conv=conv)
        out = call(
            kernel,
            o,
            per,
            [(nx, o), (start, o)],
            outs + [((width, conv + LANES), bf16, None)] if first else outs,
            shared=given + pieces_in if first else [w_in] + given,
            scalar=places if first else None,
            deps=order.deps(),
            vmem=34,
        )
        if first:
            w_in = out[7]
        kept.append(out[:5])
        decs.append(order.leave(out[6]))
        states.append(Chain(out[5], out[6], False))
        states[-1].send(order)

    if n_ctx > 2:
        states[0].send(order)
    for g in range(chunks):
        u, slope, act, xdt, dtl = kept[g]
        if g == 0:
            order.land(ring_rest[min(chunks + 1, n_ctx - 1)], landing(2 * chunks - 1))
        y_local.append(
            order.leave(
                call(
                    functools.partial(local_kernel, inner=inner),
                    0,
                    per,
                    [(act, 0), (xdt, 0), (dtl, 0), (start, g * per)],
                    deps=order.deps(),
            vmem=16,
                    outs=[(part(q, inner), f32, False)],
                )[0]
            )
        )
    if n_ctx > 2:
        for one in states[1:]:
            one.send(order)
    for hop in range(3, n_ctx):
        for i, one in enumerate(states):
            if hop == 3:
                order.land(landing(2 * chunks + 1 + 2 * i))
            one.send(order)

    scans = []
    for g in range(chunks):
        o = g * per
        u, slope, act, xdt, dtl = kept[g]
        first = g == 0 and in_kernel
        hops = len(states[g].entering)
        outs = [
            (part(q, inner), f32, False),
            (part(q, inner), f32, False),
            (part(q, inner), f32, False),
            (part(8, q), f32, False),
        ]
        if first:
            kernel = functools.partial(gate_sums_first_kernel, pieces=len(pieces_rest), hops=hops, inner=inner)
            given = [rows, spread] + pieces_rest
            outs = outs + [((width, width), bf16, None)]
        else:
            kernel = functools.partial(gate_sums_next_kernel, hops=hops, inner=inner)
            given = [w_rest, rows, spread]
        out = call(
            kernel,
            o,
            per,
            [(nx, o), (cotangent, o), (y_local[g], 0), (act, 0), (dtl, 0), (start, o)]
            + [(v, 0) for v in states[g].entering],
            outs,
            shared=given,
            scalar=places if first else None,
            deps=order.deps(),
            vmem=56,
        )
        if first:
            w_rest = out[4]
        scans.append(out[:4])
        order.leave(out[3])
    sums = cube_sum(jnp.concatenate([one[3] for one in scans]), "tp")

    bulk = [None] * 2
    d_ys = []
    chains, gate_rows = [], []
    for g in range(chunks):
        o = g * per
        u, slope, act, xdt, dtl = kept[g]
        y_scan, z, d_hidden, _ = scans[g]
        out = call(
            functools.partial(gate_kernel, inner=inner),
            o,
            per,
            [(y_scan, 0), (act, 0), (dtl, 0), (start, o), (z, 0), (d_hidden, 0), (sums, o)],
            deps=order.deps(),
            vmem=34,
            outs=[
                (shape(q, inner), bf16, True),
                (shape(q + HALO, inner), bf16, True),
                (part(q, inner), bf16, False),
                (part(STATE, inner), bf16, False),
                (part(8, inner), f32, False),
            ],
            shared=(rows, spread),
            into=None if g == 0 else bulk,
        )
        bulk = list(out[:2])
        d_ys.append(out[2])
        order.leave(out[3])
        chains.append(Chain(out[3], decs[g], True))
        chains[-1].send(order)
        gate_rows.append(out[4])
    hidden, d_z = bulk

    def hop(i):
        if i < len(chains):
            chains[i].send(order)

    def back_local(g):
        o = g * per
        u, slope, act, xdt, dtl = kept[g]
        out = call(
            functools.partial(local_back_kernel, hops=n_ctx - 1, inner=inner),
            0,
            per,
            [(act, 0), (xdt, 0), (dtl, 0), (start, o), (start_row, o), (d_ys[g], 0)]
            + [(v, 0) for v in states[g].entering],
            deps=order.deps(),
            vmem=16,
            outs=[(part(q, inner), f32, False), (part(q, 2 * STATE), f32, False)],
            shared=(spread,),
        )
        order.leave(out[1])
        return out

    nx2 = nx.reshape(seqs * (q + HALO), width)
    steps = tuple(range(1, n_ctx + 1))
    grad = order.leave(dot(nx2, order.enter(d_z).reshape(seqs * (q + HALO), inner), TN).astype(bf16))
    rest_z = Spread(grad, [steps])
    hop(0)
    hop(1)
    grad = order.leave(
        dot(cotangent.reshape(n_tok, width), order.enter(hidden).reshape(n_tok, inner), TN).astype(bf16)
    )
    rest_o = Spread(grad, [steps])
    back = [back_local(0)]
    hop(0)
    hop(1)
    back += [back_local(g) for g in range(1, chunks)]
    for _ in range(3, n_ctx):
        hop(0)
        hop(1)
    z_part = order.leave(dot(order.enter(d_z).reshape(seqs * (q + HALO), inner), w_rest[:, :inner], NT).astype(bf16))
    z_part = z_part.reshape(seqs, q + HALO, width)
    own = lax.dynamic_slice_in_dim(after(tokens, halo), tp_rank * cols, cols, 2)

    bulk = [None] * 2
    tap_rows, head_rows = [], []
    for g in range(chunks):
        have = 0 if g == 0 else 1
        o = g * per
        u, slope, act, xdt, dtl = kept[g]
        chains[g].land(order)
        out = call(
            functools.partial(conv_back_kernel, hops=n_ctx - 1, inner=inner, conv=conv),
            o,
            per,
            [(act, 0), (xdt, 0), (dtl, 0), (start, o), (d_ys[g], 0), (scans[g][0], 0), (back[g][0], 0), (back[g][1], 0), (slope, 0), (u, 0), (decs[g], 0)]
            + [(v, 0) for v in states[g].entering + chains[g].entering],
            deps=order.deps(),
            outs=[
                (shape(q + HALO, conv + LANES), bf16, True),
                (shape(HALO, conv + LANES), bf16, True),
                (part(8, conv), f32, False),
                (part(8, LANES), f32, False),
            ],
            shared=(taps, rows, head_par, spread, gather, tri),
            scratch=[pltpu.VMEM((q, conv), f32)],
            into=None if g == 0 else bulk,
        )
        bulk = list(out[:2])
        tap_rows.append(out[2])
        head_rows.append(out[3])
        order.leave(out[3])
        if g == 0:
            ring = Ring([rest_z, rest_o], order)
    du = bulk[0]
    rim = rotate(bulk[1], "ctx", -1)

    grad = order.leave(dot(nx2, du.reshape(seqs * (q + HALO), conv + LANES), TN).astype(bf16))
    spread_in = Spread(grad, [steps[:1]])
    ring.step(order)
    spread_in.more(steps[1:], order)
    order.land(spread_in.sent)

    near, away = call_slices(
        mix_kernel,
        rank,
        tp_count,
        [(hidden, False)],
        deps=order.deps(),
        weights=[(w_rest, inner, inner)],
        outs=[(shape(q, width // 2), bf16, True), (shape(q, width // 2), bf16, True)],
    )
    order.leave(near)
    cube_mix = Cube(near, away)
    ring_in = Ring([spread_in], order)

    in_gain_own = lax.dynamic_slice_in_dim(in_gain, tp_rank * cols, cols, 0).astype(f32)
    order.land(rim)
    near, away = call_slices(
        out_back_kernel,
        rank,
        tp_count,
        [(du, False), (rim, False), (jnp.concatenate(tap_rows), False), (nx, True), (z_part, True)],
        [(w_in, 0, conv + LANES)],
        deps=order.deps(),
        outs=[
            (shape(q + HALO, width // 2), bf16, False),
            (shape(q + HALO, width // 2), bf16, False),
        ],
        scratch=[pltpu.VMEM((n_tok, conv + LANES), bf16), pltpu.VMEM((n_tok, LANES), f32)],
    )
    order.leave(near)
    cube = Cube(near, away)

    ring.step(order)
    cube.halve(order)
    ring_in.step(order)
    cube_mix.halve(order)
    while not ring.done():
        ring.step(order)
    grad_wz, grad_wo = ring.total
    while ring_in.at < n_ctx - 1:
        ring_in.step(order)
    gain_row = jnp.broadcast_to(in_gain_own[None], (8, cols))
    own_cot = lax.dynamic_slice_in_dim(cotangent, tp_rank * cols, cols, 2)
    order.land(cube.come)
    grad_tokens, extra = call(
        tokens_kernel,
        0,
        seqs,
        [(cube.near, 0), (cube.come, 0), (own, 0), (own_cot, 0), (inv_rms, 0)],
        [(shape(q, cols), f32, True), (shape(HALO, cols), f32, True)],
        shared=(gain_row,),
        deps=order.deps(),
        vmem=16,
    )
    order.leave(extra)
    small = Hops(pack(tap_rows, head_rows, gate_rows, extra, order, inner), None, ["fsdp", "ctx"])
    small.go(order)
    rows_own = grad_wz.shape[0]
    grad_zx, grad_bc, grad_dt = finish(
        ring_in, grad_wz, [(rows_own, 2, inner), (rows_own, 2 * STATE), (rows_own, heads)], order
    )
    bc_hops = Hops(grad_bc, None, ["tp"])
    bc_hops.go(order)
    small.go(order)
    order.land(cube_mix.come)
    mixed = order.leave((order.enter(own).astype(f32) + cube_mix.total()).astype(bf16))
    bc_hops.go(order)
    while small.todo:
        small.go(order)
    order.land(small.come)
    one = lambda n: ((1, n), f32)
    conv_own, convb_own, conv_all, convb_all, dtb, alog, skip, gate, gain_row = small_call(
        unpack_kernel,
        [small.v, small.come, gain_row, gather],
        [((CONV, inner), f32), one(inner), ((CONV, 2 * STATE), f32), one(2 * STATE), one(heads), one(heads), one(heads), one(inner), one(cols)],
        order,
    )
    grad_bc = bc_hops.end(order)

    return (
        mixed,
        grad_tokens,
        gain_row[0],
        grad_zx,
        grad_bc,
        grad_dt,
        dtb[0],
        alog[0],
        skip[0],
        conv_own,
        convb_own[0],
        conv_all,
        convb_all[0],
        gate[0],
        grad_wo.T,
    )


def solution(mesh):
    return jax.shard_map(
        per_device,
        mesh=mesh,
        in_specs=(
            P("fsdp", "ctx", None),
            P("fsdp", "ctx"),
            P(),
            P(("fsdp", "ctx"), None, "tp"),
            P(("fsdp", "ctx"), None),
            P(("fsdp", "ctx"), "tp"),
            P("tp"),
            P("tp"),
            P("tp"),
            P(None, "tp"),
            P("tp"),
            P(),
            P(),
            P("tp"),
            P("tp", ("fsdp", "ctx")),
            P("fsdp", "ctx", None),
        ),
        out_specs=(
            P("fsdp", "ctx", "tp"),
            P("fsdp", "ctx", "tp"),
            P("tp"),
            P(("fsdp", "ctx"), None, "tp"),
            P(("fsdp", "ctx"), None),
            P(("fsdp", "ctx"), "tp"),
            P("tp"),
            P("tp"),
            P("tp"),
            P(None, "tp"),
            P("tp"),
            P(),
            P(),
            P("tp"),
            P("tp", ("fsdp", "ctx")),
        ),
        check_vma=False,
    )
```
